32 devices in a mesh: rows: 8 (over z, y), seq: 4 (over x, core).
Axes of the slice: x: 2, y: 2, z: 4, core: 2. Of those that a mesh axis runs over, the one named last changes fastest.
Arguments:
- tokens: bfloat16 [32, 512, 768], P('rows', 'seq'), may hold values from -6 to 6
- segment_ids: int32 [32, 512], P('rows', 'seq'), may hold values from 0 to 8, as said below
- w_query: bfloat16 [768, 768], replicated, may hold values from -0.21875 to 0.21875
- w_key: bfloat16 [768, 768], replicated, may hold values from -0.21875 to 0.21875
- w_value: bfloat16 [768, 768], replicated, may hold values from -0.21875 to 0.21875
- b_query: float32 [768], replicated, may hold values from -3 to 3
- b_value: float32 [768], replicated, may hold values from -3 to 3
- w_out: bfloat16 [768, 768], replicated, may hold values from -1.25 to 1.25
- b_out: float32 [768], replicated, may hold values from -3 to 3
- gain_attn: float32 [768], replicated, may hold values from 0.5 to 1.5
- shift_attn: float32 [768], replicated, may hold values from -3 to 3
- w_up: bfloat16 [768, 3072], replicated, may hold values from -0.21875 to 0.21875
- b_up: float32 [3072], replicated, may hold values from -3 to 3
- w_down: bfloat16 [3072, 768], replicated, may hold values from -0.109375 to 0.109375
- b_down: float32 [768], replicated, may hold values from -3 to 3
- gain_out: float32 [768], replicated, may hold values from 0.5 to 1.5
- shift_out: float32 [768], replicated, may hold values from -3 to 3
- token_cot: bfloat16 [32, 512, 768], P('rows', 'seq'), may hold values from -6 to 6
- pool_cot: float32 [32, 8, 1728], P('rows'), may hold values from -48 to 48
Outputs:
- layer_out: bfloat16 [32, 512, 768], P('rows', 'seq')
- pooled: float32 [32, 8, 1728], P('rows')
- grad_tokens: bfloat16 [32, 512, 768], P('rows', 'seq')
- grad_w_query: float32 [768, 768], P('rows')
- grad_w_key: float32 [768, 768], P('rows')
- grad_w_value: float32 [768, 768], P('rows')
- grad_b_query: float32 [768], P('rows')
- grad_b_value: float32 [768], P('rows')
- grad_w_out: float32 [768, 768], P('rows')
- grad_b_out: float32 [768], P('rows')
- grad_gain_attn: float32 [768], P('rows')
- grad_shift_attn: float32 [768], P('rows')
- grad_w_up: float32 [768, 3072], P('rows')
- grad_b_up: float32 [3072], P('rows')
- grad_w_down: float32 [3072, 768], P('rows')
- grad_b_down: float32 [768], P('rows')
- grad_gain_out: float32 [768], P('rows')
- grad_shift_out: float32 [768], P('rows')
The draws below stay inside these ranges and needn't reach their ends.
Inputs may be any that keep to these rules, and one draw needn't show every extreme that they name: `segment_ids`: along each row the ids never fall; the id 8 marks padding, which only ends a row and takes at most 128 tokens; in each aligned block of 4 rows one row, drawn from the seed, is the single segment 0 without padding, and every other row ends in padding.
All inputs are finite; a program needn't handle non-finite values.
Results may differ from the reference program's by a relative error of at most 0.017.
Values may be sent and summed in bfloat16 or wider, within the bound.
No kernel may reach another device: no remote copies, remote signals or barrier semaphores. Data moves between devices by JAX's collectives and lax.ppermute only.
A program may use at most 128 MiB of HBM per device.

```python
import math
import jax
import jax.numpy as jnp
from jax import lax

D = 768
FF = 3072
HEADS = 12
LEN = 512
SEGS = 8
SEQ_DEV = 4
SEQS = 32
POOLW = 1728


def draw_segment_ids(key, part):
    key = jax.random.fold_in(key, 11)
    cut_key, pad_key, pick_key = jax.random.split(key, 3)
    cuts = jax.random.randint(cut_key, (SEQS, SEGS - 1), 1, LEN)
    pads = jax.random.randint(pad_key, (SEQS, 1), 1, LEN // 4 + 1)
    picked = jax.random.randint(pick_key, (SEQS // SEQ_DEV, 1), 0, SEQ_DEV)
    chosen = (jnp.arange(SEQ_DEV, dtype=jnp.int32)[None, :] == picked).reshape(SEQS, 1)
    cuts = jnp.where(chosen, LEN, cuts)
    pads = jnp.where(chosen, 0, pads)
    places = jnp.arange(LEN, dtype=jnp.int32)[None, :]
    seg_ids = jnp.sum((cuts[:, None, :] <= places[:, :, None]).astype(jnp.int32), axis=-1)
    return jnp.where(places >= LEN - pads, SEGS, seg_ids).astype(jnp.int32)


def level_of(key, dims, cuts, smallest, largest):
    level, own = 1.0, jax.random.fold_in(key, 6)
    for axis_at, shards_of in cuts:
        heights = jnp.exp(jax.random.uniform(jax.random.fold_in(own, axis_at), (shards_of,), jnp.float32, smallest / len(cuts), largest / len(cuts)))
        level = level * jnp.repeat(heights, dims[axis_at] // shards_of).reshape([-1 if axis == axis_at else 1 for axis in range(len(dims))])
    return level


def scatter_about(own_key, shape, scale, most, cuts=(), held_as=jnp.bfloat16):
    values = scale * jax.random.normal(own_key, shape, jnp.float32)
    if cuts:
        values = values * level_of(own_key, shape, cuts, -0.22, 0.18)
    return jnp.clip(values, -most, most).astype(held_as)


def setup_inputs(seed: int = 0) -> dict:
    splits = jax.random.split(jax.random.key(seed), 20)
    return {
        "tokens": scatter_about(splits[0], (SEQS, LEN, D), 1.0, 6.0, ((0, 8), (1, 4))),
        "segment_ids": draw_segment_ids(jax.random.fold_in(splits[19], 71), 0),
        "w_query": scatter_about(splits[2], (D, D), D ** -0.5, 0.21875),
        "w_key": scatter_about(splits[3], (D, D), D ** -0.5, 0.21875),
        "w_value": scatter_about(splits[4], (D, D), D ** -0.5, 0.21875),
        "b_query": scatter_about(splits[5], (D,), 0.5, 3.0, (), jnp.float32),
        "b_value": scatter_about(splits[6], (D,), 0.5, 3.0, (), jnp.float32),
        "w_out": scatter_about(splits[7], (D, D), (D // 32) ** -0.5, 1.25),
        "b_out": scatter_about(splits[8], (D,), 0.5, 3.0, (), jnp.float32),
        "gain_attn": jnp.clip(1.0 + 0.1 * jax.random.normal(splits[9], (D,), jnp.float32), 0.5, 1.5),
        "shift_attn": scatter_about(splits[10], (D,), 0.5, 3.0, (), jnp.float32),
        "w_up": scatter_about(splits[11], (D, FF), D ** -0.5, 0.21875),
        "b_up": scatter_about(splits[12], (FF,), 0.5, 3.0, (), jnp.float32),
        "w_down": scatter_about(splits[13], (FF, D), FF ** -0.5, 0.109375),
        "b_down": scatter_about(splits[14], (D,), 0.5, 3.0, (), jnp.float32),
        "gain_out": jnp.clip(1.0 + 0.1 * jax.random.normal(splits[15], (D,), jnp.float32), 0.5, 1.5),
        "shift_out": scatter_about(splits[16], (D,), 0.5, 3.0, (), jnp.float32),
        "token_cot": scatter_about(splits[17], (SEQS, LEN, D), 1.0, 6.0, ((0, 8), (1, 4))),
        "pool_cot": scatter_about(splits[18], (SEQS, SEGS, POOLW), 8.0, 48.0, ((0, 8),), jnp.float32),
    }


@jax.custom_vjp
def low(v):
    return lax.optimization_barrier(v.astype(jnp.bfloat16)).astype(jnp.float32)

@jax.custom_vjp
def low_back(v):
    return v

def low_keep(v):
    return (low(v), None)

def low_pass(kept, grad):
    return (grad,)

def back_keep(v):
    return (v, None)

def back_low(kept, grad):
    return (low(grad),)
low.defvjp(low_keep, low_pass)
low_back.defvjp(back_keep, back_low)
norm_eps = 1e-12
pool_eps = 1e-06
highest = lax.Precision.HIGHEST

def matmul(left, right):
    return jnp.dot(left, right, precision=highest, preferred_element_type=jnp.float32)

def layer_norm(hidden, gain_vec, shift_vec):
    centered = hidden - lax.optimization_barrier(jnp.mean(hidden, axis=-1, keepdims=True))
    spread = lax.optimization_barrier(jnp.mean(centered * centered, axis=-1, keepdims=True))
    return centered * lax.rsqrt(spread + norm_eps) * gain_vec + shift_vec

def pool_finish(seg_sums):
    width = seg_sums.shape[-1]
    pieces = []
    for keep_width in (width, width * 2 // 3, width // 3, width // 6, width // 12):
        window = seg_sums[..., :keep_width]
        factor = lax.rsqrt(lax.optimization_barrier(jnp.mean(window * window, axis=-1, keepdims=True)) + pool_eps)
        pieces.append(window * factor)
    return jnp.concatenate(pieces, axis=-1)

def forward(tokens, segment_ids, params):
    w_query, w_key, w_value, b_query, b_value, w_out, b_out, gain_attn, shift_attn, w_up, b_up, w_down, b_down, gain_out, shift_out = params
    group_size = math.gcd(SEQS, max(1, 4096 // LEN))
    head_size = D // HEADS
    score_scale = head_size ** (-0.5)

    def block_fn(block_in):
        rows_in, block_ids = block_in
        row_total = rows_in.shape[0]
        flat_rows = rows_in.reshape(row_total * LEN, D)
        query_heads = low(low_back(matmul(flat_rows, w_query) + b_query)).reshape(row_total, LEN, HEADS, head_size)
        key_heads = low(low_back(matmul(flat_rows, w_key))).reshape(row_total, LEN, HEADS, head_size)
        value_heads = low(low_back(matmul(flat_rows, w_value) + b_value)).reshape(row_total, LEN, HEADS, head_size)
        scores = low_back(jnp.einsum('gqhe,gkhe->ghqk', query_heads, key_heads, precision=highest) * score_scale)
        same_doc = block_ids[:, None, :, None] == block_ids[:, None, None, :]
        scores = jnp.where(same_doc, scores, -1e+30)
        attn_probs = low(jax.nn.softmax(scores, axis=-1))
        attn_mixed = jnp.einsum('ghqk,gkhe->gqhe', attn_probs, value_heads, precision=highest)
        attn_mixed = low(low_back(attn_mixed.reshape(row_total * LEN, D)))
        branch = low_back(matmul(attn_mixed, w_out) + b_out)
        normed = layer_norm(flat_rows + branch, gain_attn, shift_attn)
        up_pre = low_back(matmul(low(normed), w_up) + b_up)
        active = low(jax.nn.gelu(up_pre, approximate=False))
        down_out = low_back(matmul(active, w_down) + b_down)
        result = layer_norm(normed + down_out, gain_out, shift_out).reshape(row_total, LEN, D)
        member = (block_ids[:, :, None] == jnp.arange(SEGS, dtype=jnp.int32)[None, None, :]).astype(jnp.float32)
        seg_sums = jnp.einsum('gts,gtd->gsd', member, result, precision=highest)
        return (result, pool_finish(seg_sums))
    batches = SEQS // group_size
    outputs, pooled = lax.map(jax.checkpoint(block_fn), (tokens.reshape(batches, group_size, LEN, D), segment_ids.reshape(batches, group_size, LEN)))
    return (outputs.reshape(SEQS, LEN, D), pooled.reshape(SEQS, SEGS, POOLW))

def reference(tokens, segment_ids, w_query, w_key, w_value, b_query, b_value, w_out, b_out, gain_attn, shift_attn, w_up, b_up, w_down, b_down, gain_out, shift_out, token_cot, pool_cot):
    params = tuple((weight.astype(jnp.float32) for weight in (w_query, w_key, w_value, b_query, b_value, w_out, b_out, gain_attn, shift_attn, w_up, b_up, w_down, b_down, gain_out, shift_out)))

    def run_layer(inputs, weights):
        return forward(inputs, segment_ids, weights)
    (layer_out, pooled), pull_back = jax.vjp(run_layer, tokens.astype(jnp.float32), params)
    grad_tokens, grads = pull_back((token_cot.astype(jnp.float32), pool_cot))
    return (layer_out.astype(jnp.bfloat16), pooled, grad_tokens.astype(jnp.bfloat16), grads[0], grads[1], grads[2], grads[3], grads[4], grads[5], grads[6], grads[7], grads[8], grads[9], grads[10], grads[11], grads[12], grads[13], grads[14])
```

```python
import functools

import jax
import jax.numpy as jnp
from jax import lax
from jax.experimental import pallas as pl
from jax.experimental.pallas import tpu as pltpu
from jax.sharding import PartitionSpec as P

HEADS = 12
SEGS = 8
norm_eps = 1e-12
pool_eps = 1e-06
bf16 = jnp.bfloat16
f32 = jnp.float32
MIB = 2**20


def shape(dims, dtype=bf16):
    return jax.ShapeDtypeStruct(dims, dtype)


def dot(left, right, left_dim=1, right_dim=0):
    return lax.dot_general(
        left, right, (((left_dim,), (right_dim,)), ((), ())), preferred_element_type=f32
    )


def whole(dims):
    zeros = (0,) * len(dims)
    return pl.BlockSpec(dims, lambda *_: zeros, pipeline_mode=pl.Buffered(1))


def whole_out(dims):
    zeros = (0,) * len(dims)
    return pl.BlockSpec(dims, lambda *_: zeros)


def params(mib):
    return pltpu.CompilerParams(vmem_limit_bytes=mib * MIB)


def split_two(value):
    high = value.astype(bf16)
    return high, (value - high.astype(f32)).astype(bf16)


def split_three(value):
    high = value.astype(bf16)
    rest = value - high.astype(f32)
    mid, low = split_two(rest)
    return high, mid, low


def attend_kernel(
    t0, t1, t2, t3, wq, wk, wv, wo, bq, bv, bo, gain, shift,
    exp_out, total_out, row_out, q_out, k_out, v_out, mix_t, mixed_out, norm_out, rstd_out, low_out, ids_out,
    mask,
):
    step = pl.program_id(0)
    blocks = (t0, t1, t2, t3)
    part = t0.shape[0] - 16
    length = part * 4

    @pl.when(step == 0)
    def _():
        for at, block in enumerate(blocks):
            row_out[at * part : (at + 1) * part, :] = block[:part, :]
        rows = row_out[...]
        q_out[...] = (dot(rows, wq[...]) + bq[...]).astype(bf16) * bf16(0.125)
        k_out[...] = dot(rows, wk[...]).astype(bf16)
        v_out[...] = (dot(rows, wv[...]) + bv[...]).astype(bf16)
        ids = jnp.concatenate([block[part : part + 16, :part].astype(f32)[0:1] for block in blocks], axis=1)
        ids_out[...] = jnp.broadcast_to(ids, ids_out.shape)
        column = jnp.broadcast_to(ids, (128, length)).T[:, 0:1]
        mask[...] = jnp.where(column == ids, 0.0, -1e30)

    lanes = pl.ds(pl.multiple_of(step * 128, 128), 128)
    keys = k_out[:, lanes]
    query_t = q_out[:, lanes].T
    value_t = v_out[:, lanes].T
    for half in range(2):
        at = slice(half * 64, half * 64 + 64)
        scores = dot(keys[:, at], query_t[at, :]) + mask[...]
        expo = jnp.exp(scores - jnp.max(scores, axis=0, keepdims=True))
        inverse = 1.0 / jnp.sum(expo, axis=0, keepdims=True)
        low = expo.astype(bf16)
        exp_out[half] = low
        total_out[0, half : half + 1, :] = inverse
        mix_t[pl.ds(pl.multiple_of(step * 128 + half * 64, 64), 64), :] = dot(value_t[at, :], low) * inverse

    @pl.when(step == pl.num_programs(0) - 1)
    def _():
        mixed = mix_t[...].astype(bf16).T
        mixed_out[...] = mixed
        hidden = row_out[...].astype(f32) + (dot(mixed, wo[...]) + bo[...])
        centered = hidden - jnp.mean(hidden, axis=-1, keepdims=True)
        rstd = lax.rsqrt(jnp.mean(centered * centered, axis=-1, keepdims=True) + norm_eps)
        normal = centered * rstd
        norm_out[...] = normal
        rstd_out[...] = jnp.broadcast_to(rstd, rstd_out.shape)
        low_out[...] = (normal * gain[...] + shift[...]).astype(bf16)


def attend(blocks, wq, wk, wv, wo, bq, bv, bo, gain, shift):
    part, width = blocks[0].shape
    length = (part - 16) * 4
    pairs = width // 128
    square = whole((width, width))
    vec = whole((1, width))
    flat = whole_out((length, width))
    return pl.pallas_call(
        attend_kernel,
        grid=(pairs,),
        in_specs=[whole((part, width))] * 4 + [square] * 4 + [vec] * 5,
        out_specs=[
            pl.BlockSpec((2, length, length), lambda i: (i, 0, 0)),
            pl.BlockSpec((1, 8, length), lambda i: (i, 0, 0)),
            flat, flat, flat, flat,
            whole_out((width, length)),
            flat, flat,
            whole_out((length, 128)),
            flat,
            whole_out((8, length)),
        ],
        out_shape=[
            shape((2 * pairs, length, length)),
            shape((pairs, 8, length), f32),
            shape((length, width)),
            shape((length, width)),
            shape((length, width)),
            shape((length, width)),
            shape((width, length), f32),
            shape((length, width)),
            shape((length, width), f32),
            shape((length, 128), f32),
            shape((length, width)),
            shape((8, length), f32),
        ],
        scratch_shapes=[pltpu.VMEM((length, length), f32)],
        compiler_params=params(56),
        name="attend_forward",
    )(*blocks, wq, wk, wv, wo, bq, bv, bo, gain, shift)


def gelu_both(v):
    bell = jnp.exp(v * v * -0.5)
    t = 1.0 / (1.0 + (0.3275911 * 0.7071067811865476) * jnp.abs(v))
    poly = ((((1.061405429 * t - 1.453152027) * t + 1.421413741) * t - 0.284496736) * t + 0.254829592) * t
    tail = 0.5 * poly * bell
    phi = jnp.where(v < 0, tail, 1.0 - tail)
    return v * phi, phi + v * bell * 0.3989422804014327


def pool_windows(width):
    return (width, width * 2 // 3, width // 3, width // 6, width // 12)


def feed_kernel(
    core, low, w_up, b_up, w_down, normal, gain_a, shift_a, b_down, gain, shift, c0, c1, c2, c3, ids, pool_cot,
    act_out, slope_out, l0, l1, l2, l3, pooled_out, hidden_out, keep_out, send_out, low_out, sums_out,
    acc,
):
    step = pl.program_id(0)
    length, width = low.shape
    up = dot(low[...], w_up[...]) + b_up[...]
    active, slope = gelu_both(up)
    active_low = active.astype(bf16)
    act_out[...] = active_low
    slope_out[...] = slope.astype(bf16)
    down = dot(active_low, w_down[...])

    @pl.when(step == 0)
    def _():
        acc[...] = down

    @pl.when(step > 0)
    def _():
        acc[...] += down

    @pl.when(step == pl.num_programs(0) - 1)
    def _():
        part = length // 4
        hidden = normal[...] * gain_a[...] + shift_a[...] + (acc[...] + b_down[...])
        centered = hidden - jnp.mean(hidden, axis=-1, keepdims=True)
        rstd = lax.rsqrt(jnp.mean(centered * centered, axis=-1, keepdims=True) + norm_eps)
        unit = centered * rstd
        result = unit * gain[...] + shift[...]
        for at, out in enumerate((l0, l1, l2, l3)):
            out[...] = result[at * part : (at + 1) * part].astype(bf16)
        groups = lax.broadcasted_iota(jnp.int32, (16, length), 0).astype(f32)
        member = jnp.where((groups == ids[0:1, :]) & (groups < SEGS), 1.0, 0.0).astype(bf16)
        seg_sums = sum(dot(member, piece) for piece in split_three(result))[:SEGS]
        at = 0
        grad_sums = []
        for window in pool_windows(width):
            sums = seg_sums[:, :window]
            cot = pool_cot[:, at : at + window]
            factor = lax.rsqrt(jnp.mean(sums * sums, axis=-1, keepdims=True) + pool_eps)
            pooled_out[:, at : at + window] = sums * factor
            inner = jnp.sum(cot * sums, axis=-1, keepdims=True) * (factor * factor * factor / window)
            piece = cot * factor - sums * inner
            if window < width:
                piece = jnp.concatenate([piece, jnp.zeros((SEGS, width - window), f32)], axis=1)
            grad_sums.append(piece)
            at += window
        total = jnp.concatenate([sum(grad_sums), jnp.zeros((16 - SEGS, width), f32)], axis=0)
        spread = sum(dot(member, piece, 0, 0) for piece in split_two(total))
        cot = jnp.concatenate([c[...].astype(f32) for c in (c0, c1, c2, c3)], axis=0)
        grad = cot + spread
        scaled = grad * gain[...]
        hidden_grad = rstd * (
            scaled
            - jnp.mean(scaled, axis=-1, keepdims=True)
            - unit * jnp.mean(scaled * unit, axis=-1, keepdims=True)
        )
        hidden_out[...] = hidden_grad
        rounded = hidden_grad.astype(bf16)
        low_out[...] = rounded
        half = width // 2
        first = core[0] == 0
        keep_out[...] = jnp.where(first, rounded[:, :half], rounded[:, half:])
        send_out[...] = jnp.where(first, rounded[:, half:], rounded[:, :half])
        sums_out[...] = jnp.concatenate(
            [
                jnp.sum(grad * unit, axis=0, keepdims=True),
                jnp.sum(grad, axis=0, keepdims=True),
                jnp.sum(rounded.astype(f32), axis=0, keepdims=True),
                jnp.zeros((5, width), f32),
            ],
            axis=0,
        )


def feed(core, low, w_up, b_up, w_down, normal, gain_a, shift_a, b_down, gain, shift, cots, ids, pool_cot):
    length, width = low.shape
    hidden = w_up.shape[1]
    tile = 512
    part = length // 4
    vec = whole((1, width))
    flat = whole_out((length, width))
    halves = whole_out((length, width // 2))
    return pl.pallas_call(
        feed_kernel,
        grid=(hidden // tile,),
        in_specs=[
            pl.BlockSpec(memory_space=pltpu.SMEM),
            whole((length, width)),
            pl.BlockSpec((width, tile), lambda i: (0, i)),
            pl.BlockSpec((1, tile), lambda i: (0, i)),
            pl.BlockSpec((tile, width), lambda i: (i, 0)),
            whole((length, width)),
            vec, vec, vec, vec, vec,
            *[whole((part, width))] * 4,
            whole((8, length)),
            whole(pool_cot.shape),
        ],
        out_specs=[
            pl.BlockSpec((length, tile), lambda i: (0, i)),
            pl.BlockSpec((length, tile), lambda i: (0, i)),
            *[whole_out((part, width))] * 4,
            whole_out(pool_cot.shape),
            flat, halves, halves, flat,
            whole_out((8, width)),
        ],
        out_shape=[
            shape((length, hidden)),
            shape((length, hidden)),
            *[shape((part, width))] * 4,
            shape(pool_cot.shape, f32),
            shape((length, width), f32),
            shape((length, width // 2)),
            shape((length, width // 2)),
            shape((length, width)),
            shape((8, width), f32),
        ],
        scratch_shapes=[pltpu.VMEM((length, width), f32)],
        compiler_params=params(56),
        name="feed_forward",
    )(core, low, w_up, b_up, w_down, normal, gain_a, shift_a, b_down, gain, shift, *cots, ids, pool_cot)


def feed_back_kernel(
    core, grad_low, w_down, slope, w_up, hidden, normal, rstd, gain, wo,
    keep_out, send_out, b_up_out, hidden_out, mixed_out, keep_b, send_b, sums_out,
    acc,
):
    step = pl.program_id(0)
    steps = pl.num_programs(0)
    width = hidden.shape[1]
    grad_up = (dot(grad_low[...], w_down[...], 1, 1) * slope[...].astype(f32)).astype(bf16)
    kept = (step // (steps // 2)) == core[0]

    @pl.when(kept)
    def _():
        keep_out[...] = grad_up

    @pl.when(jnp.logical_not(kept))
    def _():
        send_out[...] = grad_up

    b_up_out[...] = jnp.broadcast_to(jnp.sum(grad_up.astype(f32), axis=0, keepdims=True), b_up_out.shape)
    back = dot(grad_up, w_up[...], 1, 1)

    @pl.when(step == 0)
    def _():
        acc[...] = back

    @pl.when(step > 0)
    def _():
        acc[...] += back

    @pl.when(step == steps - 1)
    def _():
        grad = hidden[...] + acc[...]
        unit = normal[...]
        scaled = grad * gain[...]
        hidden_grad = rstd[:, 0:1] * (
            scaled
            - jnp.mean(scaled, axis=-1, keepdims=True)
            - unit * jnp.mean(scaled * unit, axis=-1, keepdims=True)
        )
        hidden_out[...] = hidden_grad
        rounded = hidden_grad.astype(bf16)
        mixed_out[...] = dot(rounded, wo[...], 1, 1).astype(bf16)
        half = width // 2
        first = core[0] == 0
        keep_b[...] = jnp.where(first, rounded[:, :half], rounded[:, half:])
        send_b[...] = jnp.where(first, rounded[:, half:], rounded[:, :half])
        sums_out[...] = jnp.concatenate(
            [
                jnp.sum(grad * unit, axis=0, keepdims=True),
                jnp.sum(grad, axis=0, keepdims=True),
                jnp.sum(rounded.astype(f32), axis=0, keepdims=True),
                jnp.zeros((5, width), f32),
            ],
            axis=0,
        )


def feed_back(core, grad_low, w_down, slope, w_up, hidden, normal, rstd, gain, wo):
    length, width = grad_low.shape
    feed_width = w_up.shape[1]
    tile = 512
    steps = feed_width // tile
    per = steps // 2
    flat = whole((length, width))
    halves = whole_out((length, width // 2))
    return pl.pallas_call(
        feed_back_kernel,
        grid_spec=pltpu.PrefetchScalarGridSpec(
            num_scalar_prefetch=1,
            grid=(steps,),
            in_specs=[
                flat,
                pl.BlockSpec((tile, width), lambda i, c: (i, 0)),
                pl.BlockSpec((length, tile), lambda i, c: (0, i)),
                pl.BlockSpec((width, tile), lambda i, c: (0, i)),
                flat,
                flat,
                whole((length, 128)),
                whole((1, width)),
                whole((width, width)),
            ],
            out_specs=[
                pl.BlockSpec((length, tile), lambda i, c: (0, jnp.clip(i - per * c[0], 0, per - 1))),
                pl.BlockSpec((length, tile), lambda i, c: (0, jnp.clip(i - per * (1 - c[0]), 0, per - 1))),
                pl.BlockSpec((8, tile), lambda i, c: (0, i)),
                whole_out((length, width)),
                whole_out((length, width)),
                halves,
                halves,
                whole_out((8, width)),
            ],
            scratch_shapes=[pltpu.VMEM((length, width), f32)],
        ),
        out_shape=[
            shape((length, feed_width // 2)),
            shape((length, feed_width // 2)),
            shape((8, feed_width), f32),
            shape((length, width), f32),
            shape((length, width)),
            shape((length, width // 2)),
            shape((length, width // 2)),
            shape((8, width), f32),
        ],
        compiler_params=params(56),
        name="feed_backward",
    )(core, grad_low, w_down, slope, w_up, hidden, normal, rstd, gain, wo)


def attend_back_kernel(core, expo, total, q, k, v, mix_t, grad_mixed, keep_out, send_out, sums_out):
    step = pl.program_id(0)
    steps = pl.num_programs(0)
    length = expo.shape[1]
    lanes = pl.ds(pl.multiple_of(step * 128, 128), 128)
    query = q[:, lanes]
    key_t = k[:, lanes].T
    value = v[:, lanes]
    grad_t = grad_mixed[:, lanes].astype(f32).T
    mix = mix_t[pl.ds(pl.multiple_of(step * 128, 128), 128), :]
    inverse = total[0, 0:2, :]
    scale = jnp.concatenate(
        [jnp.broadcast_to(inverse[0:1], (64, length)), jnp.broadcast_to(inverse[1:2], (64, length))], axis=0
    )
    scaled_t = (grad_t * scale).astype(bf16)
    scaled = scaled_t.T
    product = scaled_t.astype(f32) * mix
    grads_q, grads_k, grads_v = [], [], []
    for half in range(2):
        at = slice(half * 64, half * 64 + 64)
        inner = jnp.sum(product[at], axis=0, keepdims=True)
        probs = expo[half]
        grad_probs = dot(value[:, at], scaled_t[at, :])
        grad_scores = (probs.astype(f32) * (grad_probs - inner)).astype(bf16)
        grads_v.append(dot(probs, scaled[:, at]))
        grads_k.append(dot(grad_scores, query[:, at]))
        grads_q.append(dot(key_t[at, :], grad_scores))
    grad_query = (jnp.concatenate(grads_q, axis=0).T * 0.125).astype(bf16)
    grad_key = jnp.concatenate(grads_k, axis=1).astype(bf16)
    grad_value = jnp.concatenate(grads_v, axis=1).astype(bf16)
    kept = (step // (steps // 2)) == core[0]

    @pl.when(kept)
    def _():
        keep_out[0] = grad_query
        keep_out[1] = grad_key
        keep_out[2] = grad_value

    @pl.when(jnp.logical_not(kept))
    def _():
        send_out[0] = grad_query
        send_out[1] = grad_key
        send_out[2] = grad_value

    sums_out[...] = jnp.concatenate(
        [
            jnp.sum(grad_query.astype(f32), axis=0, keepdims=True),
            jnp.sum(grad_value.astype(f32), axis=0, keepdims=True),
            jnp.zeros((6, 128), f32),
        ],
        axis=0,
    )


def attend_back(core, expo, total, q, k, v, mix_t, grad_mixed):
    heads, length, _ = expo.shape
    width = q.shape[1]
    pairs = heads // 2
    per = pairs // 2
    flat = whole((length, width))
    return pl.pallas_call(
        attend_back_kernel,
        grid_spec=pltpu.PrefetchScalarGridSpec(
            num_scalar_prefetch=1,
            grid=(pairs,),
            in_specs=[
                pl.BlockSpec((2, length, length), lambda i, c: (i, 0, 0)),
                pl.BlockSpec((1, 8, length), lambda i, c: (i, 0, 0)),
                flat,
                flat,
                flat,
                whole((width, length)),
                flat,
            ],
            out_specs=[
                pl.BlockSpec((3, length, 128), lambda i, c: (0, 0, jnp.clip(i - per * c[0], 0, per - 1))),
                pl.BlockSpec((3, length, 128), lambda i, c: (0, 0, jnp.clip(i - per * (1 - c[0]), 0, per - 1))),
                pl.BlockSpec((8, 128), lambda i, c: (0, i)),
            ],
        ),
        out_shape=[
            shape((3, length, width // 2)),
            shape((3, length, width // 2)),
            shape((8, width), f32),
        ],
        compiler_params=params(56),
        name="attend_backward",
    )(core, expo, total, q, k, v, mix_t, grad_mixed)


def input_grad_kernel(core, hidden, keep, send, wq, wk, wv, o0, o1, o2, o3):
    width = hidden.shape[1]
    half = width // 2
    part = o0.shape[0]
    mine = pl.ds(pl.multiple_of(core[0] * half, 128), half)
    other = pl.ds(pl.multiple_of((1 - core[0]) * half, 128), half)
    total = hidden[...]
    for at, weight in enumerate((wq, wk, wv)):
        total += dot(keep[at], weight[:, mine], 1, 1) + dot(send[at], weight[:, other], 1, 1)
    for at, out in enumerate((o0, o1, o2, o3)):
        out[...] = total[at * part : (at + 1) * part].astype(bf16)


def input_grad(core, hidden, keep, send, wq, wk, wv):
    length, width = hidden.shape
    part = length // 4
    vmem = pl.BlockSpec(memory_space=pltpu.VMEM)
    return pl.pallas_call(
        input_grad_kernel,
        in_specs=[pl.BlockSpec(memory_space=pltpu.SMEM)] + [vmem] * 6,
        out_specs=[vmem] * 4,
        out_shape=[shape((part, width))] * 4,
        compiler_params=params(40),
        name="input_gradient",
    )(core, hidden, keep, send, wq, wk, wv)


def down_weight_kernel(own, other, keep, got, out):
    out[...] = (dot(own[...], keep[...], 0, 0) + dot(other[...], got[...], 0, 0)).astype(bf16)


def down_weight(own, other, keep, got):
    length, feed_width = own.shape
    half = keep.shape[1]
    tile = 768
    return pl.pallas_call(
        down_weight_kernel,
        grid=(feed_width // tile,),
        in_specs=[pl.BlockSpec((length, tile), lambda i: (0, i))] * 2 + [whole((length, half))] * 2,
        out_specs=pl.BlockSpec((tile, half), lambda i: (i, 0)),
        out_shape=shape((feed_width, half)),
        compiler_params=params(40),
        name="down_weight",
    )(own, other, keep, got)


def up_weight_kernel(own, other, keep, got, mix, mix_other, keep_b, got_b, first, second, out_w):
    step = pl.program_id(0)
    steps = pl.num_programs(0)
    value = (dot(own[...], keep[...], 0, 0) + dot(other[...], got[...], 0, 0)).astype(bf16)

    @pl.when(step < steps // 2)
    def _():
        first[...] = value

    @pl.when(step >= steps // 2)
    def _():
        second[...] = value

    @pl.when(step == 0)
    def _():
        out_w[...] = (dot(mix[...], keep_b[...], 0, 0) + dot(mix_other[...], got_b[...], 0, 0)).astype(bf16)


def up_weight(own, other, keep, got, mix, mix_other, keep_b, got_b):
    length, width = own.shape
    cols = keep.shape[1]
    tile = 384
    steps = cols // tile
    flat = whole((length, width))
    moving = pl.BlockSpec((length, tile), lambda i: (0, i))
    half = whole((length, width // 2))
    return pl.pallas_call(
        up_weight_kernel,
        grid=(steps,),
        in_specs=[flat, flat, moving, moving, flat, flat, half, half],
        out_specs=[
            pl.BlockSpec((width, tile), lambda i: (0, jnp.minimum(i, steps // 2 - 1))),
            pl.BlockSpec((width, tile), lambda i: (0, jnp.maximum(i - steps // 2, 0))),
            whole_out((width, width // 2)),
        ],
        out_shape=[shape((width, cols // 2)), shape((width, cols // 2)), shape((width, width // 2))],
        compiler_params=params(40),
        name="up_weight",
    )(own, other, keep, got, mix, mix_other, keep_b, got_b)


def head_weight_kernel(own, other, keep, got, out_q, out_kv):
    half = out_q.shape[1]
    left, right = own[...], other[...]
    out_q[...] = (dot(left, keep[0], 0, 0) + dot(right, got[0], 0, 0)).astype(bf16)
    for at in (1, 2):
        value = dot(left, keep[at], 0, 0) + dot(right, got[at], 0, 0)
        out_kv[:, (at - 1) * half : at * half] = value.astype(bf16)


def head_weight(own, other, keep, got):
    width = own.shape[1]
    vmem = pl.BlockSpec(memory_space=pltpu.VMEM)
    return pl.pallas_call(
        head_weight_kernel,
        in_specs=[vmem] * 4,
        out_specs=[vmem] * 2,
        out_shape=[shape((width, width // 2)), shape((width, width))],
        compiler_params=params(40),
        name="head_weight",
    )(own, other, keep, got)


def place_kernel(seq_at, b0, b1, b2, b3, out):
    for at, block in enumerate((b0, b1, b2, b3)):
        out[seq_at[0] ^ at] = block[...]


def place(seq_at, blocks):
    vmem = pl.BlockSpec(memory_space=pltpu.VMEM)
    return pl.pallas_call(
        place_kernel,
        in_specs=[pl.BlockSpec(memory_space=pltpu.SMEM)] + [vmem] * 4,
        out_specs=vmem,
        out_shape=shape((4, *blocks[0].shape)),
        compiler_params=params(16),
        name="place_rows",
    )(seq_at, *blocks)


def swap_seq(value, mask):
    return lax.ppermute(value, "seq", [(at, at ^ mask) for at in range(4)])


def reduce_part(value, order, row_at, seq_at, row_count):
    bits = row_count.bit_length() - 1
    value = value.reshape((2,) * bits + value.shape[1:])
    names = [1 << at for at in reversed(range(bits))] + ["x"]
    for axis in order:
        dim = names.index(axis)
        names.pop(dim)
        if axis == "x":
            bit = (seq_at >> 1) & 1
        else:
            bit = (row_at // axis) & 1
        keep = lax.dynamic_index_in_dim(value, bit, dim, keepdims=False)
        send = lax.dynamic_index_in_dim(value, 1 - bit, dim, keepdims=False)
        if axis == "x":
            got = swap_seq(send, 2)
        else:
            got = lax.ppermute(send, "rows", [(at, at ^ axis) for at in range(row_count)])
        value = (keep.astype(f32) + got.astype(f32)).astype(bf16)
    return value


def order_pair(bit, own, got):
    return jnp.where(bit == 0, own, got), jnp.where(bit == 0, got, own)


def local(
    row_count,
    tokens, segment_ids, w_query, w_key, w_value, b_query, b_value, w_out, b_out, gain_attn, shift_attn,
    w_up, b_up, w_down, b_down, gain_out, shift_out, token_cot, pool_cot,
):
    part, width = tokens.shape[1:]
    feed_width = w_up.shape[1]
    seq_at = lax.axis_index("seq")
    row_at = lax.axis_index("rows")
    core = (seq_at & 1).reshape(1)
    where_at = seq_at.reshape(1)

    def vec(v):
        return v.reshape(1, -1)

    ids = jnp.pad(segment_ids.astype(bf16)[:, None, :], ((0, 0), (0, 15), (0, width - part)))

    def token_block(mask):
        at = seq_at ^ mask
        return jnp.concatenate(
            [
                lax.dynamic_index_in_dim(tokens, at, 0, keepdims=False),
                lax.dynamic_index_in_dim(ids, at, 0, keepdims=False),
            ],
            axis=0,
        )

    def cot_block(mask):
        return lax.dynamic_index_in_dim(token_cot, seq_at ^ mask, 0, keepdims=False)

    blocks = [token_block(0)] + [swap_seq(token_block(mask), mask) for mask in (1, 2, 3)]
    cots = [cot_block(0)] + [swap_seq(cot_block(mask), mask) for mask in (1, 2, 3)]
    row_pool_cot = lax.dynamic_index_in_dim(pool_cot, seq_at, 0, keepdims=False)

    expo, total, row, q, k, v, mix_t, mixed, normal, rstd, low, ids_row = attend(
        blocks, w_query, w_key, w_value, w_out, vec(b_query), vec(b_value), vec(b_out), vec(gain_attn), vec(shift_attn)
    )
    row_other, mixed_other, low_other = swap_seq(row, 1), swap_seq(mixed, 1), swap_seq(low, 1)
    active, slope, l0, l1, l2, l3, pooled, hidden_two, keep_d, send_d, grad_down, sums_two = feed(
        core, low, w_up, vec(b_up), w_down, normal, vec(gain_attn), vec(shift_attn), vec(b_down),
        vec(gain_out), vec(shift_out), cots, ids_row, row_pool_cot,
    )
    active_other, got_d = swap_seq(active, 1), swap_seq(send_d, 1)
    layer_out = place(where_at, [l0] + [swap_seq(out, mask) for mask, out in ((1, l1), (2, l2), (3, l3))])
    pooled_all = lax.all_gather(pooled.astype(bf16), "seq", axis=0).astype(f32)

    keep_u, send_u, b_up_sum, hidden_one, grad_mixed, keep_b, send_b, sums_one = feed_back(
        core, grad_down, w_down, slope, w_up, hidden_two, normal, rstd, vec(gain_attn), w_out
    )
    got_u, got_b = swap_seq(send_u, 1), swap_seq(send_b, 1)
    grad_w_down = down_weight(active, active_other, keep_d, got_d)
    up_first, up_second, out_part = up_weight(low, low_other, keep_u, got_u, mixed, mixed_other, keep_b, got_b)
    keep_h, send_h, sums_head = attend_back(core, expo, total, q, k, v, mix_t, grad_mixed)
    got_h = swap_seq(send_h, 1)
    g0, g1, g2, g3 = input_grad(core, hidden_one, keep_h, send_h, w_query, w_key, w_value)
    query_part, key_value_part = head_weight(row, row_other, keep_h, got_h)
    grad_tokens = place(where_at, [g0] + [swap_seq(out, mask) for mask, out in ((1, g1), (2, g2), (3, g3))])

    shards = row_count
    bits = [1 << at for at in range(shards.bit_length() - 1)]
    order_a = ["x"] + bits
    order_b = [bits[0], "x"] + bits[1:]
    order_c = bits[1:] + [bits[0], "x"]
    half = width // 2
    rows = width // shards // 2
    vectors = jnp.concatenate(
        [
            b_up_sum[0].reshape(shards, -1),
            jnp.stack([sums_head[0], sums_head[1], sums_one[2], sums_one[0], sums_one[1], sums_two[2], sums_two[0], sums_two[1]])
            .reshape(8, shards, width // shards)
            .transpose(1, 0, 2)
            .reshape(shards, -1),
        ],
        axis=1,
    )
    count = vectors.shape[1]
    vec_rows = -(-count // (2 * half))
    vectors = jnp.pad(vectors, ((0, 0), (0, 2 * half * vec_rows - count))).reshape(shards, 2, vec_rows, half)
    vectors = jnp.pad(vectors, ((0, 0), (0, 0), (0, 16 - vec_rows), (0, 0))).astype(bf16)

    def cut(value):
        return value.reshape(shards, 2, -1, value.shape[1])

    query_all = jnp.concatenate([cut(query_part), vectors], axis=2)
    reduce = functools.partial(reduce_part, row_at=row_at, seq_at=seq_at, row_count=row_count)
    piece_d = reduce(cut(grad_w_down), order_b)
    piece_u1 = reduce(cut(up_first), order_a)
    piece_u2 = reduce(cut(up_second), order_c)
    piece_o = reduce(cut(out_part), order_c)
    piece_q = reduce(query_all, order_a)
    piece_kv = reduce(cut(key_value_part), order_b)
    feed_piece = jnp.concatenate(
        [piece_d, piece_u1[:, :half], piece_u1[:, half:], piece_u2[:, :half], piece_u2[:, half:]], axis=0
    )
    head_piece = jnp.concatenate([piece_o, piece_kv[:, :half], piece_kv[:, half:], piece_q], axis=0)

    def gather(piece):
        x_bit = (seq_at >> 1) & 1
        both = jnp.stack(order_pair(x_bit, piece, swap_seq(piece, 2)))
        other = swap_seq(both, 1)
        return both, other

    feed_own, feed_other = gather(feed_piece)
    head_own, head_other = gather(head_piece)
    core_bit = seq_at & 1

    def columns(own, other, at, count):
        left, right = order_pair(core_bit, own[:, at : at + count], other[:, at : at + count])
        left = left.reshape(2 * count, half)
        right = right.reshape(2 * count, half)
        return jnp.concatenate([left, right], axis=1).astype(f32)

    down_rows = piece_d.shape[0]
    out_w_down = columns(feed_own, feed_other, 0, down_rows)

    def up_columns(own, other):
        pieces = [own[:, down_rows + at * rows : down_rows + (at + 1) * rows].reshape(2 * rows, half) for at in range(4)]
        return jnp.concatenate(pieces, axis=1)

    left, right = order_pair(core_bit, up_columns(feed_own, None), up_columns(feed_other, None))
    out_w_up = jnp.concatenate([left, right], axis=1).astype(f32)
    out_w_out = columns(head_own, head_other, 0, rows)
    out_w_key = columns(head_own, head_other, rows, rows)
    out_w_value = columns(head_own, head_other, 2 * rows, rows)
    out_w_query = columns(head_own, head_other, 3 * rows, rows)
    at = 4 * rows
    vec_own = head_own[:, at : at + vec_rows].astype(f32) + head_other[:, at : at + vec_rows].astype(f32)
    vec_all = vec_own.reshape(-1)[:count]
    out_b_up = vec_all[: feed_width // shards]
    rest = vec_all[feed_width // shards :].reshape(8, width // shards)
    return (
        layer_out, pooled_all, grad_tokens,
        out_w_query, out_w_key, out_w_value, rest[0], rest[1], out_w_out, rest[2], rest[3], rest[4],
        out_w_up, out_b_up, out_w_down, rest[5], rest[6], rest[7],
    )


def solution(mesh):
    split = P("rows", "seq", None)
    in_specs = (split, P("rows", "seq"), *[P()] * 15, split, P("rows", None, None))
    mat, line = P("rows", None), P("rows")
    out_specs = (
        split, P("rows", None, None), split,
        mat, mat, mat, line, line, mat, line, line, line, mat, line, mat, line, line, line,
    )
    body = functools.partial(local, mesh.shape["rows"])
    return jax.shard_map(body, mesh=mesh, in_specs=in_specs, out_specs=out_specs, check_vma=False)
```

```python
import functools

import jax
import jax.numpy as jnp
from jax import lax
from jax.experimental import pallas as pl
from jax.experimental.pallas import tpu as pltpu
from jax.sharding import PartitionSpec as P

HEADS = 12
SEGS = 8
FEED_TILE = 1024
PIECES = 4
COST = 0.001
LATE = 4000.0
D_SPLIT = (4, 4, 4)
BYTES = 1.0
norm_eps = 1e-12
pool_eps = 1e-06
bf16 = jnp.bfloat16
f32 = jnp.float32
MIB = 2**20


def shape(dims, dtype=bf16):
    return jax.ShapeDtypeStruct(dims, dtype)


def dot(left, right, left_dim=1, right_dim=0):
    return lax.dot_general(
        left, right, (((left_dim,), (right_dim,)), ((), ())), preferred_element_type=f32
    )


def in_vmem(kernel, name, mib, outs, args, work, scratch=(), scalars=0, fetch=(), far_in=(), near=(), free=(), far_own=()):
    args, outs, fetch = list(args), list(outs), dict(fetch)
    in_specs = [pl.BlockSpec(memory_space=pltpu.VMEM)] * len(args)
    for at in range(scalars):
        in_specs[at] = pl.BlockSpec(memory_space=pltpu.SMEM)
    for at in [*fetch, *far_in]:
        in_specs[at] = pl.BlockSpec(memory_space=pltpu.HBM)
        args[at] = pltpu.with_memory_space_constraint(args[at], pltpu.HBM)
    out_specs = [pl.BlockSpec(memory_space=pltpu.VMEM)] * len(outs)
    far_out = [at for at in range(len(outs)) if at not in near and at not in free and at not in far_own]
    held_in = [pltpu.VMEM(args[at].shape, args[at].dtype) for at in fetch]
    held_out = [pltpu.VMEM(outs[at].shape, outs[at].dtype) for at in far_out]
    size = sum(v.size * v.dtype.itemsize for v in (*args, *outs))
    for at in [*far_out, *far_own]:
        out_specs[at] = pl.BlockSpec(memory_space=pltpu.HBM)
        outs[at] = pltpu.HBM(outs[at].shape, outs[at].dtype)
    pieces = [(at, dim, count, piece) for at, (dim, count) in fetch.items() for piece in range(count)]
    pieces.sort(key=lambda piece: piece[3])
    count_in, count_out = len(args), len(outs)

    def body(*refs):
        ins, results = list(refs[:count_in]), list(refs[count_in : count_in + count_out])
        rest = list(refs[count_in + count_out :])
        own = [rest.pop(0) for _ in scratch]
        buffers = dict(zip(fetch, [rest.pop(0) for _ in held_in]))
        staged = dict(zip(far_out, [rest.pop(0) for _ in held_out]))
        sems_in, sems_out = rest
        copies = {at: [] for at in fetch}
        for number, (at, dim, count, piece) in enumerate(pieces):
            length = args[at].shape[dim] // count
            where = [slice(None)] * args[at].ndim
            where[dim] = pl.ds(piece * length, length)
            where = tuple(where)
            copy = pltpu.make_async_copy(ins[at].at[where], buffers[at].at[where], sems_in.at[number])
            copy.start()
            copies[at].append(copy)
        for at in fetch:
            ins[at] = Fetched(buffers[at], copies[at])
        sent = {}

        def flush(*numbers):
            for at in numbers:
                sent[at] = pltpu.make_async_copy(staged[at], results[at], sems_out.at[at])
                sent[at].start()

        kernel(*ins, *[staged.get(at, results[at]) for at in range(count_out)], *own, flush=flush)
        flush(*[at for at in far_out if at not in sent])
        for copy in sent.values():
            copy.wait()
        for one in ins:
            if isinstance(one, Fetched):
                one.finish()

    sems = [pltpu.SemaphoreType.DMA((max(1, len(pieces)),)), pltpu.SemaphoreType.DMA((len(outs),))]
    return pl.pallas_call(
        body,
        in_specs=in_specs,
        out_specs=out_specs,
        out_shape=outs,
        scratch_shapes=[*scratch, *held_in, *held_out, *sems],
        compiler_params=pltpu.CompilerParams(vmem_limit_bytes=mib * MIB),
        cost_estimate=pl.CostEstimate(flops=int(work * COST), bytes_accessed=int(size * BYTES), transcendentals=0),
        name=name,
    )(*args)


class Fetched:
    def __init__(self, ref, copies):
        self.ref, self.copies, self.waited = ref, copies, set()

    def piece(self, at=0):
        if at not in self.waited:
            self.waited.add(at)
            self.copies[at].wait()
        return self.ref

    def finish(self):
        for at in range(len(self.copies)):
            self.piece(at)

    def __getitem__(self, where):
        self.finish()
        return self.ref[where]

    @property
    def shape(self):
        return self.ref.shape


def load_kernel(*refs, flush):
    count = (len(refs) - 1) // 2
    copies = [pltpu.make_async_copy(refs[at], refs[count + at], refs[-1].at[at]) for at in range(count)]
    for copy in copies:
        copy.start()
    for copy in copies:
        copy.wait()


def load(*arrays):
    outs = [shape(v.shape, v.dtype) for v in arrays]
    every = range(len(arrays))
    scratch = [pltpu.SemaphoreType.DMA((len(arrays),))]
    return in_vmem(load_kernel, "load_weights", 4, outs, arrays, 1e9, scratch, far_in=every, near=every)


def split_two(value):
    high = value.astype(bf16)
    return high, (value - high.astype(f32)).astype(bf16)


def attend_kernel(
    t0, t1, t2, t3, wq, wk, wv, wo, bq, bv, bo, gain, shift,
    exp_out, total_out, row_out, q_out, k_out, v_out, mix_t, mixed_out, norm_out, rstd_out, low_out, low_far, ids_out,
    mask, stage, sems,
    *, flush,
):
    blocks = (t0, t1, t2, t3)
    part = t0.shape[0] - 16
    length, width = row_out.shape
    for at, block in enumerate(blocks):
        row_out[at * part : (at + 1) * part, :] = block[:part, :]
    rows = row_out[...]
    q_out[...] = (dot(rows, wq[...]) + bq[...]).astype(bf16) * bf16(0.125)
    k_out[...] = dot(rows, wk[...]).astype(bf16)
    v_out[...] = (dot(rows, wv[...]) + bv[...]).astype(bf16)
    flush(2, 3, 4, 5)
    ids = jnp.concatenate([block[part : part + 16, :part].astype(f32)[0:1] for block in blocks], axis=1)
    ids_out[...] = jnp.broadcast_to(ids, ids_out.shape)
    column = jnp.broadcast_to(ids, (128, length)).T[:, 0:1]
    mask[...] = jnp.where(column == ids, 0.0, -1e30)

    sent = []
    for pair in range(width // 128):
        lanes = slice(pair * 128, pair * 128 + 128)
        keys = k_out[:, lanes]
        query_t = q_out[:, lanes].T
        value_t = v_out[:, lanes].T
        for half in range(2):
            at = slice(half * 64, half * 64 + 64)
            head = 2 * pair + half
            scores = dot(keys[:, at], query_t[at, :]) + mask[...]
            expo = jnp.exp(scores - jnp.max(scores, axis=0, keepdims=True))
            inverse = 1.0 / jnp.sum(expo, axis=0, keepdims=True)
            low = expo.astype(bf16)
            stage[head] = low
            sent.append(pltpu.make_async_copy(stage.at[head], exp_out.at[head], sems.at[head]))
            sent[-1].start()
            total_out[head : head + 1, :] = inverse
            mix_t[head * 64 : head * 64 + 64, :] = dot(value_t[at, :], low) * inverse

    mixed = mix_t[...].astype(bf16).T
    mixed_out[...] = mixed
    flush(1, 6, 7)
    hidden = row_out[...].astype(f32) + (dot(mixed, wo[...]) + bo[...])
    centered = hidden - jnp.mean(hidden, axis=-1, keepdims=True)
    rstd = lax.rsqrt(jnp.mean(centered * centered, axis=-1, keepdims=True) + norm_eps)
    normal = centered * rstd
    norm_out[...] = normal
    rstd_out[...] = jnp.broadcast_to(rstd, rstd_out.shape)
    low = (normal * gain[...] + shift[...]).astype(bf16)
    low_out[...] = low
    low_far[...] = low
    for copy in sent:
        copy.wait()


def attend(blocks, wq, wk, wv, wo, bq, bv, bo, gain, shift):
    part, width = blocks[0].shape
    length = (part - 16) * 4
    heads = width // 64
    flat = shape((length, width))
    wide = shape((length, width), f32)
    outs = [
        shape((heads, length, length)), shape((16, length), f32), flat, flat, flat, flat, shape((width, length), f32),
        flat, wide, shape((length, 128), f32), flat, flat, shape((8, length), f32),
    ]
    args = (*blocks, wq, wk, wv, wo, bq, bv, bo, gain, shift)
    scratch = [
        pltpu.VMEM((length, length), f32),
        pltpu.VMEM((heads, length, length), bf16),
        pltpu.SemaphoreType.DMA((heads,)),
    ]
    fetch = {at: (0, 1) for at in range(4)}
    return in_vmem(
        attend_kernel, "attend_forward", 20, outs, args, 10e9 * LATE, scratch, fetch=fetch, near=(8, 9, 10, 12), far_own=(0,)
    )


def gelu_both(v):
    phi = 0.5 + 0.5 * lax.erf(v * 0.7071067811865476)
    bell = jnp.exp2(v * (v * (-0.5 * 1.4426950408889634)))
    return v * phi, phi + (v * 0.3989422804014327) * bell


def pool_windows(width):
    return (width, width * 2 // 3, width // 3, width // 6, width // 12)


def pool_places(width):
    w = pool_windows(width)
    return ((0, 0), (8, 0), (8, w[1]), (16, 0), (16, w[3]))


def feed_kernel(
    core, low, w_up, b_up, w_down, normal, gain_a, shift_a, b_down, gain, shift, c0, c1, c2, c3, ids, pool_cot, rstd_a, wo,
    act_out, l0, l1, l2, keep_out, sums_out,
    keep_u, send_u, b_up_out, hidden_one, mixed_out, sums_one,
    acc, unit_s, rstd_s, slope_out, hidden_out, low_out, up_s, down_s, cot_s, out_s, sems,
    *, flush,
):
    length, width = low.shape
    part = length // 4
    hidden_width = w_up.shape[1]
    tile = FEED_TILE
    copies = []
    for at in range(0, hidden_width, tile):
        ups, downs = [], []
        for piece in range(PIECES):
            rows = slice(piece * (width // PIECES), (piece + 1) * (width // PIECES))
            cols = slice(at, at + tile)
            number = len(copies) * PIECES + piece
            ups.append(pltpu.make_async_copy(w_up.at[rows, cols], up_s.at[rows, cols], sems.at[number]))
            rows = slice(at + piece * (tile // PIECES), at + (piece + 1) * (tile // PIECES))
            downs.append(pltpu.make_async_copy(w_down.at[rows, :], down_s.at[rows, :], sems.at[number + PIECES]))
        copies += [ups, downs]
    late = []
    sources = (c0, c1, c2, c3)
    first_sem = len(copies) * PIECES
    for number, source in enumerate(sources):
        late.append(pltpu.make_async_copy(source, cot_s.at[number], sems.at[first_sem + number]))
    late.append(pltpu.make_async_copy(wo, out_s, sems.at[first_sem + 4]))
    for copy in copies[0]:
        copy.start()
    for at in range(0, hidden_width, tile):
        cols = slice(at, at + tile)
        turn = at // tile
        for copy in copies[2 * turn]:
            copy.wait()
        for copy in sum(copies[2 * turn + 1 : 2 * turn + 3], []):
            copy.start()
        up = dot(low[...], up_s[:, cols]) + b_up[:, cols]
        active, slope = gelu_both(up)
        active_low = active.astype(bf16)
        act_out[:, cols] = active_low
        slope_out[:, cols] = slope.astype(bf16)
        for copy in copies[2 * turn + 1]:
            copy.wait()
        if 2 * turn + 2 == len(copies):
            for copy in late:
                copy.start()
        down = dot(active_low, down_s[cols, :])
        if at == 0:
            acc[...] = down
        else:
            acc[...] += down

    groups = lax.broadcasted_iota(jnp.int32, (16, length), 0).astype(f32)
    member = jnp.where((groups == ids[0:1, :]) & (groups < SEGS), 1.0, 0.0).astype(bf16)
    outs = (l0, l1, l2.at[0], l2.at[1])
    seg_sums = jnp.zeros((16, width), f32)
    for at in range(4):
        rows = slice(at * part, (at + 1) * part)
        hidden = normal[rows, :] * gain_a[...] + shift_a[...] + (acc[rows, :] + b_down[...])
        centered = hidden - jnp.mean(hidden, axis=-1, keepdims=True)
        rstd = lax.rsqrt(jnp.mean(centered * centered, axis=-1, keepdims=True) + norm_eps)
        unit = centered * rstd
        unit_s[rows, :] = unit
        rstd_s[rows, :] = jnp.broadcast_to(rstd, (part, 128))
        result = unit * gain[...] + shift[...]
        outs[at][0:part, :] = result.astype(bf16)
        for piece in split_two(result):
            seg_sums += dot(member[:, rows], piece)
    seg_sums = seg_sums[:SEGS]
    first_lane = 0
    total = jnp.zeros((SEGS, width), f32)
    pooled = []
    for window in pool_windows(width):
        sums = seg_sums[:, :window]
        cot = pool_cot[:, first_lane : first_lane + window]
        factor = lax.rsqrt(jnp.mean(sums * sums, axis=-1, keepdims=True) + pool_eps)
        pooled.append(sums * factor)
        inner = jnp.sum(cot * sums, axis=-1, keepdims=True) * (factor * factor * factor / window)
        piece = cot * factor - sums * inner
        if window < width:
            piece = jnp.concatenate([piece, jnp.zeros((SEGS, width - window), f32)], axis=1)
        total += piece
        first_lane += window
    zeros = jnp.zeros((8, width), f32)
    rest = jnp.zeros((8, width - pooled[3].shape[1] - pooled[4].shape[1]), f32)
    upper = jnp.concatenate([pooled[0], jnp.concatenate(pooled[1:3], axis=1)], axis=0).astype(bf16)
    lower = jnp.concatenate([jnp.concatenate([pooled[3], pooled[4], rest], axis=1), zeros], axis=0).astype(bf16)
    for out in outs:
        out[part : part + 16, :] = upper
        out[part + 16 : part + 32, :] = lower
    flush(1, 2, 3)
    total = split_two(jnp.concatenate([total, zeros], axis=0))
    half = width // 2
    first = core[0] == 0
    sums = [jnp.zeros((1, width), f32)] * 3
    for copy in late[:4]:
        copy.wait()
    for at in range(4):
        rows = slice(at * part, (at + 1) * part)
        grad = cot_s[at].astype(f32) + sum(dot(member[:, rows], piece, 0, 0) for piece in total)
        unit = unit_s[rows, :]
        scaled = grad * gain[...]
        hidden_grad = rstd_s[rows, 0:1] * (
            scaled
            - jnp.mean(scaled, axis=-1, keepdims=True)
            - unit * jnp.mean(scaled * unit, axis=-1, keepdims=True)
        )
        hidden_out[rows, :] = hidden_grad
        rounded = hidden_grad.astype(bf16)
        low_out[rows, :] = rounded
        keep_out[rows, :] = jnp.where(first, rounded[:, :half], rounded[:, half:])
        act_out[rows, hidden_width:] = jnp.where(first, rounded[:, half:], rounded[:, :half])
        for to, value in enumerate((grad * unit, grad, rounded.astype(f32))):
            sums[to] += jnp.sum(value, axis=0, keepdims=True)
    sums_out[...] = jnp.concatenate([*sums, jnp.zeros((5, width), f32)], axis=0)

    half_feed = hidden_width // 2
    for at, out in enumerate((send_u, keep_u)):
        which = core[0] if at == 1 else 1 - core[0]
        cols = pl.ds(pl.multiple_of(which * half_feed, 128), half_feed)
        grad_up = (dot(low_out[...], down_s[cols, :], 1, 1) * slope_out[:, cols].astype(f32)).astype(bf16)
        out[:, :half_feed] = grad_up
        b_up_out[:, cols] = jnp.broadcast_to(jnp.sum(grad_up.astype(f32), axis=0, keepdims=True), (8, half_feed))
        if at == 0:
            flush(0, 4, 5)
        back = dot(grad_up, up_s[:, cols], 1, 1)
        if at == 0:
            acc[...] = hidden_out[...] + back
        else:
            acc[...] += back

    sums = [jnp.zeros((1, width), f32)] * 3
    for at in range(0, length, 64):
        rows = slice(at, at + 64)
        grad = acc[rows, :]
        unit = normal[rows, :]
        scaled = grad * gain_a[...]
        hidden_grad = rstd_a[rows, 0:1] * (
            scaled
            - jnp.mean(scaled, axis=-1, keepdims=True)
            - unit * jnp.mean(scaled * unit, axis=-1, keepdims=True)
        )
        hidden_one[rows, :] = hidden_grad
        rounded = hidden_grad.astype(bf16)
        low_out[rows, :] = rounded
        keep_u[rows, half_feed:] = jnp.where(first, rounded[:, :half], rounded[:, half:])
        send_u[rows, half_feed:] = jnp.where(first, rounded[:, half:], rounded[:, :half])
        for to, value in enumerate((grad * unit, grad, rounded.astype(f32))):
            sums[to] += jnp.sum(value, axis=0, keepdims=True)
    flush(7, 6, 8, 9)
    late[4].wait()
    mixed_out[...] = dot(low_out[...], out_s[...], 1, 1).astype(bf16)
    sums_one[...] = jnp.concatenate([*sums, jnp.zeros((5, width), f32)], axis=0)


def feed(core, low, w_up, b_up, w_down, normal, gain_a, shift_a, b_down, gain, shift, cots, ids, pool_cot, rstd, wo):
    length, width = low.shape
    hidden = w_up.shape[1]
    half = shape((length, width // 2))
    wide = shape((length, width), f32)
    part = length // 4 + 32
    outs = [
        shape((length, hidden + width // 2)), shape((part, width)), shape((part, width)), shape((2, part, width)),
        half, shape((8, width), f32), shape((length, hidden // 2 + width // 2)), shape((length, hidden // 2 + width // 2)),
        shape((8, hidden), f32), wide, shape((length, width)), shape((8, width), f32),
    ]
    scratch = [
        pltpu.VMEM((length, width), f32),
        pltpu.VMEM((length, width), f32),
        pltpu.VMEM((length, 128), f32),
        pltpu.VMEM((length, hidden), bf16),
        pltpu.VMEM((length, width), f32),
        pltpu.VMEM((length, width), bf16),
        pltpu.VMEM(w_up.shape, bf16),
        pltpu.VMEM(w_down.shape, bf16),
        pltpu.VMEM((4, length // 4, width), bf16),
        pltpu.VMEM((width, width), bf16),
        pltpu.SemaphoreType.DMA((2 * hidden // FEED_TILE * PIECES + 5,)),
    ]
    args = (core, low, w_up, b_up, w_down, normal, gain_a, shift_a, b_down, gain, shift, *cots, ids, pool_cot, rstd, wo)
    return in_vmem(
        feed_kernel, "feed_both", 38, outs, args, 18e9 * LATE, scratch, 1, far_in=(2, 4, 11, 12, 13, 14, 18)
    )


def attend_back_kernel(
    core, expo, total, q, k, v, mix_t, grad_mixed, keep_out, send_out, sums_out,
    held, q_s, k_s, v_s, mix_s, grad_s, sems,
    *, flush,
):
    length = expo.shape[1]
    pairs = q.shape[1] // 128
    per = pairs // 2
    slots = held.shape[0]

    def copies(at):
        which = core[0] if at >= per else 1 - core[0]
        pair = which * per + at % per
        lanes = pl.ds(pl.multiple_of(pair * 128, 128), 128)
        slot = at % slots
        sources = [
            (q.at[:, lanes], q_s), (k.at[:, lanes], k_s), (v.at[:, lanes], v_s),
            (mix_t.at[lanes, :], mix_s), (grad_mixed.at[:, lanes], grad_s),
            (expo.at[pl.ds(2 * pair, 2)], held),
        ]
        return [
            pltpu.make_async_copy(source, to.at[slot], sems.at[slot, number])
            for number, (source, to) in enumerate(sources)
        ]

    for at in range(slots - 1):
        for copy in copies(at):
            copy.start()
    for at in range(pairs):
        if at + slots - 1 < pairs:
            for copy in copies(at + slots - 1):
                copy.start()
        which = core[0] if at >= per else 1 - core[0]
        out = keep_out if at >= per else send_out
        pair, slot = at % per, at % slots
        lanes = pl.ds(pl.multiple_of(which * (per * 128) + pair * 128, 128), 128)
        for copy in copies(at):
            copy.wait()
        grad_t = grad_s[slot].T.astype(f32)
        query, value, mix = q_s[slot], v_s[slot], mix_s[slot]
        key_t = k_s[slot].T
        halves = []
        inner = []
        for half in range(2):
            rows = slice(half * 64, half * 64 + 64)
            inverse = total[pl.ds(which * pairs + 2 * pair + half, 1), :]
            scaled = (grad_t[rows] * inverse).astype(bf16)
            halves.append(scaled)
            inner.append(jnp.sum(scaled.astype(f32) * mix[rows], axis=0, keepdims=True))
        scaled_rows = jnp.concatenate(halves, axis=0).T
        grads_q, grads_k, grads_v = [], [], []
        for half in range(2):
            rows = slice(half * 64, half * 64 + 64)
            probs = held[slot, half]
            grad_probs = dot(value[:, rows], halves[half])
            grad_scores = (probs.astype(f32) * (grad_probs - inner[half])).astype(bf16)
            grads_v.append(dot(probs, scaled_rows[:, rows]))
            grads_k.append(dot(grad_scores, query[:, rows]))
            grads_q.append(dot(key_t[rows, :], grad_scores))
        here = slice(pair * 128, pair * 128 + 128)
        grad_query = (jnp.concatenate(grads_q, axis=0).T * 0.125).astype(bf16)
        grad_value = jnp.concatenate(grads_v, axis=1).astype(bf16)
        out[0, :, here] = grad_query
        out[1, :, here] = jnp.concatenate(grads_k, axis=1).astype(bf16)
        out[2, :, here] = grad_value
        sums_out[:, lanes] = jnp.concatenate(
            [
                jnp.sum(grad_query.astype(f32), axis=0, keepdims=True),
                jnp.sum(grad_value.astype(f32), axis=0, keepdims=True),
                jnp.zeros((6, 128), f32),
            ],
            axis=0,
        )


def attend_back(core, expo, total, q, k, v, mix_t, grad_mixed):
    length, width = q.shape
    outs = [shape((3, length, width // 2)), shape((3, length, width // 2)), shape((8, width), f32)]
    args = (core, expo, total, q, k, v, mix_t, grad_mixed)
    slots = 3
    scratch = [
        pltpu.VMEM((slots, 2, length, length), bf16),
        *[pltpu.VMEM((slots, length, 128), bf16)] * 3,
        pltpu.VMEM((slots, 128, length), f32),
        pltpu.VMEM((slots, length, 128), bf16),
        pltpu.SemaphoreType.DMA((slots, 6)),
    ]
    return in_vmem(
        attend_back_kernel, "attend_backward", 14, outs, args, 9e9 * LATE, scratch, 1,
        fetch={2: (0, 1)}, far_in=(1, 3, 4, 5, 6, 7), free=(0, 1, 2),
    )


def add_input_grad(core, hidden, keep, send, wq, wk, wv, o0, o1, o2):
    width = hidden.shape[1]
    half = width // 2
    part = o0.shape[0]
    mine = pl.ds(pl.multiple_of(core[0] * half, 128), half)
    other = pl.ds(pl.multiple_of((1 - core[0]) * half, 128), half)
    total = hidden[...]
    for at, weight in enumerate((wq, wk, wv)):
        total += dot(keep[at], weight[:, mine], 1, 1) + dot(send[at], weight[:, other], 1, 1)
    total = total.astype(bf16)
    for at, out in enumerate((o0, o1, o2.at[0], o2.at[1])):
        out[...] = total[at * part : (at + 1) * part]


def down_weight_kernel(own, other, keep, out, *, flush):
    size = out.shape[0] // 4
    for at in range(4):
        rows = slice(at * size, (at + 1) * size)
        left, right = own[:, rows], other[:, rows]
        out[rows, :] = (dot(left, keep[...], 0, 0) + dot(right, other[:, 4 * size :], 0, 0)).astype(bf16)


def down_weight(own, other, keep):
    half = keep.shape[1]
    outs = [shape((own.shape[1] - half, half))]
    return in_vmem(down_weight_kernel, "down_weight", 14, outs, (own, other, keep), 4e9 * LATE, free=(0,))[0]


def weights_kernel(
    core, low, low_other, mixed, mixed_other, row, row_other, keep_u, got_u, keep_h, send_h, got_h, hidden, wq, wk, wv,
    b_up, sums_head, sums_one, sums_two,
    out_u, out_o, out_h, vec, g0, g1, g2,
    *, flush,
):
    half = out_o.shape[1]
    tiles = out_u.shape[0]
    for at in range(tiles):
        cols = slice(at * half, (at + 1) * half)
        out_u[at] = (dot(low[...], keep_u[:, cols], 0, 0) + dot(low_other[...], got_u[:, cols], 0, 0)).astype(bf16)
    cols = slice(tiles * half, (tiles + 1) * half)
    out_o[...] = (dot(mixed[...], keep_u[:, cols], 0, 0) + dot(mixed_other[...], got_u[:, cols], 0, 0)).astype(bf16)
    for at in range(3):
        out_h[at] = (dot(row[...], keep_h[at], 0, 0) + dot(row_other[...], got_h[at], 0, 0)).astype(bf16)
    add_input_grad(core, hidden, keep_h, send_h, wq, wk, wv, g0, g1, g2)
    shards = vec.shape[0]
    lines = jnp.concatenate([sums_head[0:2], sums_one[0:3], sums_two[0:3]], axis=0)
    line = lines.shape[1] // shards
    up = b_up.shape[1] // shards
    first = lax.broadcasted_iota(jnp.int32, (8, up), 0) == 0
    for at in range(shards):
        piece = lines[:, at * line : (at + 1) * line]
        if line < half:
            piece = jnp.concatenate([piece, jnp.zeros((8, half - line), f32)], axis=1)
        vec[at, 0] = jnp.concatenate([piece, jnp.zeros((8, half), f32)], axis=0).astype(bf16)
        piece = jnp.where(first, b_up[:, at * up : (at + 1) * up], 0.0)
        if up < half:
            piece = jnp.concatenate([piece, jnp.zeros((8, half - up), f32)], axis=1)
        vec[at, 1] = jnp.concatenate([piece, jnp.zeros((8, half), f32)], axis=0).astype(bf16)


def weights(shards, *args):
    low, keep_u = args[1], args[7]
    length, width = low.shape
    half = width // 2
    part = length // 4
    outs = [
        shape((keep_u.shape[1] // half - 1, width, half)), shape((width, half)), shape((3, width, half)),
        shape((shards, 2, 16, half)), shape((part, width)), shape((part, width)), shape((2, part, width)),
    ]
    every = range(len(outs))
    return in_vmem(weights_kernel, "other_weights", 14, outs, args, 11e9 * LATE, scalars=1, free=every)


def pack_kernel(seq_at, tokens, *rest, flush):
    ids, outs = (rest[0], rest[1:]) if len(rest) == 5 else (None, rest)
    part, width = tokens.shape[1:]
    for at in range(4):
        out = outs[at]
        row = seq_at[0] ^ at
        out[:part, :] = tokens.piece()[row]
        if ids is not None:
            line = ids[pl.ds(row, 1), :].astype(f32)
            line = jnp.concatenate([line, jnp.zeros((1, width - part), f32)], axis=1)
            out[part : part + 16, :] = jnp.broadcast_to(line, (16, width)).astype(bf16)


def pack(seq_at, tokens, ids=None):
    _, part, width = tokens.shape
    extra = 0 if ids is None else 16
    args = (seq_at, tokens) if ids is None else (seq_at, tokens, ids)
    outs = [shape((part + extra, width))] * 4
    return in_vmem(pack_kernel, "pack_rows", 6, outs, args, 1e8, scalars=1, fetch={1: (0, 1)})


def place_kernel(seq_at, b0, b1, b2, b3, out, *pooled, flush):
    part, width = out.shape[1:]
    for at, block in enumerate((b0, b1, b2, b3)):
        to = seq_at[0] ^ at
        rows = block.piece()[0] if at == 2 else block[...]
        out[to] = rows[:part, :]
        if pooled:
            first = 0
            rows = rows[part : part + 32, :].astype(f32)
            for window, (row, lane) in zip(pool_windows(width), pool_places(width)):
                pooled[0][to, :, first : first + window] = rows[row : row + 8, lane : lane + window]
                first += window


def place(seq_at, blocks, part, pooled):
    width = blocks[0].shape[1]
    outs = [shape((4, part, width))]
    if pooled:
        outs.append(shape((4, SEGS, sum(pool_windows(width))), f32))
    fetch = {at: (0, 1) for at in range(1, 5)}
    return in_vmem(place_kernel, "place_rows", 6, outs, (seq_at, *blocks), 1e8, scalars=1, fetch=fetch)


def swap_seq(value, mask):
    return lax.ppermute(value, "seq", [(at, at ^ mask) for at in range(4)])


def exchange(own, core_block, chip_blocks):
    got_core = swap_seq(core_block, 1)
    got_chip = swap_seq(chip_blocks, 2)
    return [own, got_core, got_chip]


def forward(blocks):
    return [*blocks, swap_seq(blocks[2][1], 1)]


class Part:
    def __init__(self, blocks, names, first, rows):
        self.blocks, self.names, self.first, self.rows, self.got = blocks, names, first, rows, None


class Exchanges:
    def __init__(self, row_at, seq_at, row_count):
        self.row_count = row_count
        self.axes = ["x"] + [1 << at for at in range(row_count.bit_length() - 1)]
        self.bits = jnp.stack([(seq_at >> 1) & 1] + [(row_at // axis) & 1 for axis in self.axes[1:]])

    def part(self, blocks, first=0, rows=None):
        names = [("tile", blocks.shape[0])] + [(axis, 2) for axis in reversed(self.axes[1:])] + [("x", 2)]
        rows = blocks.shape[3] if rows is None else rows
        return Part(blocks.reshape(-1, *blocks.shape[3:]), names, first, rows)

    def swap(self, value, axis):
        if axis == "x":
            return swap_seq(value, 2)
        return lax.ppermute(value, "rows", [(at, at ^ axis) for at in range(self.row_count)])

    def tick(self, moves, settle=()):
        parts = [part for part, _ in moves] + list(settle)
        ins = []
        for part in parts:
            for value in (part.blocks, part.got and part.got[0]):
                if value is not None and not any(value is other for other in ins):
                    ins.append(value)
        find = lambda value: [value is other for other in ins].index(True)
        lanes = parts[0].blocks.shape[2]
        used = list(dict.fromkeys(axis for _, axis in moves))
        outs, plan, rows_of, kept = [], [], dict.fromkeys([*used, None], 0), []
        for part, axis in [*moves, *[(part, None) for part in settle]]:
            count = part.blocks.shape[0]
            source = (find(part.blocks), part.first, part.rows, part.got and (find(part.got[0]), part.got[1]))
            if axis is None:
                plan.append((source, axis, [(at, None) for at in range(count)], rows_of[axis], None))
                rows_of[axis] += count * part.rows
                continue
            names = [name for name, _ in part.names]
            low = 1
            for _, size in part.names[names.index(axis) + 1 :]:
                low *= size
            pairs = [(at, at + low) for at in range(count) if (at // low) % 2 == 0]
            plan.append((source, axis, pairs, rows_of[axis], len(kept)))
            kept.append(shape((count // 2, part.rows, lanes)))
            part.got = (axis, rows_of[axis])
            rows_of[axis] += len(pairs) * part.rows
            part.names = [entry for entry in part.names if entry[0] != axis]
        flat = [*used, *([None] if settle else [])]
        outs = [shape((rows_of[axis], lanes)) for axis in flat] + kept

        def kernel(bits, *refs, flush):
            given, sends, keeps = refs[: len(ins)], refs[len(ins) : len(ins) + len(flat)], refs[len(ins) + len(flat) :]
            for (blocks, first, rows, got), axis, pairs, row, keep in plan:
                send = sends[flat.index(axis)]

                def value(at):
                    block = given[blocks][at, first : first + rows, :]
                    if got is None:
                        return block
                    other = given[got[0]][got[1] + at * rows : got[1] + (at + 1) * rows, :]
                    return (block.astype(f32) + other.astype(f32)).astype(bf16)

                for number, (zero, one) in enumerate(pairs):
                    where = slice(row + number * rows, row + (number + 1) * rows)
                    if axis is None:
                        send[where, :] = value(zero)
                        continue
                    bit = bits[self.axes.index(axis)] == 0
                    left, right = value(zero), value(one)
                    send[where, :] = jnp.where(bit, right, left)
                    keeps[keep][number] = jnp.where(bit, left, right)

        every = range(len(outs))
        results = in_vmem(kernel, "halves", 10, outs, (self.bits, *ins), 1e8, scalars=1, free=every)
        arrived = {axis: self.swap(results[flat.index(axis)], axis) for axis in used}
        for (part, axis), blocks in zip(moves, results[len(flat) :]):
            part.blocks, part.first = blocks, 0
            part.got = (arrived[axis], part.got[1])
        return results[len(used)] if settle else None

    def before(self, parts, value):
        blocks = [part.blocks for part in parts]
        value, blocks = lax.optimization_barrier((value, blocks))
        for part, new in zip(parts, blocks):
            part.blocks = new
        return value

    def after(self, parts, value):
        found = []
        for part in parts:
            if not any(part.got[0] is other for other in found):
                found.append(part.got[0])
        value, new = lax.optimization_barrier((value, found))
        for part in parts:
            at = [part.got[0] is other for other in found].index(True)
            part.got = (new[at], part.got[1])
        return value


def sides(bits, piece, got_x, got_c, got_xc):
    mine = [jnp.where(bits[0] == 0, piece, got_x), jnp.where(bits[0] == 0, got_x, piece)]
    other = [jnp.where(bits[0] == 0, got_c, got_xc), jnp.where(bits[0] == 0, got_xc, got_c)]
    left = [jnp.where(bits[1] == 0, a, b) for a, b in zip(mine, other)]
    right = [jnp.where(bits[1] == 0, b, a) for a, b in zip(mine, other)]
    return left, right


def final_kernel(kinds, bits, *refs, flush):
    own, outs = refs[:4], refs[4:]
    half = own[0].shape[1]
    for pieces, out in zip(kinds, outs):
        for at, rows, to_row, to_lane in pieces:
            left, right = sides(bits, *[ref[at : at + rows, :].astype(f32) for ref in own])
            if to_lane is None:
                line = (left[to_row // 16] + right[to_row // 16])[to_row % 16 : to_row % 16 + 1, : out.shape[1]]
                out[...] = line
                continue
            for x in range(2):
                first = x * (out.shape[0] // 2) + to_row
                out[first : first + rows, to_lane : to_lane + half] = left[x]
                right_lane = out.shape[1] // 2 + to_lane
                out[first : first + rows, right_lane : right_lane + half] = right[x]


def gather(piece):
    got_x = swap_seq(piece, 2)
    return piece, got_x, swap_seq(piece, 1), swap_seq(got_x, 1)


def final(bits, pieces, kinds, outs):
    kernel = functools.partial(final_kernel, kinds)
    return in_vmem(kernel, "final_rows", 12, outs, (bits, *pieces), 1e8, scalars=1)


def together(*values):
    return lax.optimization_barrier(values)


def local(
    row_count,
    tokens, segment_ids, w_query, w_key, w_value, b_query, b_value, w_out, b_out, gain_attn, shift_attn,
    w_up, b_up, w_down, b_down, gain_out, shift_out, token_cot, pool_cot,
):
    part, width = tokens.shape[1:]
    feed_width = w_up.shape[1]
    half = width // 2
    seq_at = lax.axis_index("seq")
    row_at = lax.axis_index("rows")
    core = (seq_at & 1).reshape(1)
    where_at = seq_at.reshape(1)
    ex = Exchanges(row_at, seq_at, row_count)
    last_bits = jnp.stack([(seq_at >> 1) & 1, seq_at & 1])
    y, zs = ex.axes[1], ex.axes[2:]
    z1, z2 = zs[0], zs[1]

    def vec(v):
        return v.reshape(1, -1)

    own = pack(where_at, tokens, segment_ids)
    token_cot, own, near = together(token_cot, own, (w_query, w_key, w_value, w_out))
    swapped = {mask: swap_seq(own[mask], mask) for mask in (2, 3, 1)}
    blocks = [own[0]] + [swapped[mask] for mask in (1, 2, 3)]
    near_query, near_key, near_value, near_out = load(*near)
    own = pack(where_at, token_cot)
    own, blocks, near_query, near_key, near_value, near_out = together(
        own, blocks, near_query, near_key, near_value, near_out
    )
    swapped = {mask: swap_seq(own[mask], mask) for mask in (2, 3, 1)}
    cots = [own[0]] + [swapped[mask] for mask in (1, 2, 3)]
    row_pool_cot = lax.dynamic_index_in_dim(pool_cot, seq_at, 0, keepdims=False)

    expo, total, row, q, k, v, mix_t, mixed, normal, rstd, low, low_far, ids_row = attend(
        blocks, near_query, near_key, near_value, near_out,
        vec(b_query), vec(b_value), vec(b_out), vec(gain_attn), vec(shift_attn),
    )
    row_other, mixed_other, low_other = swap_seq(row, 1), swap_seq(mixed, 1), swap_seq(low_far, 1)
    act, l0, l1, l2, keep_d, sums_two, keep_u, send_u, b_up_sum, hidden_one, grad_mixed, sums_one = feed(
        core, low, w_up, vec(b_up), w_down, normal, vec(gain_attn), vec(shift_attn), vec(b_down),
        vec(gain_out), vec(shift_out), cots, ids_row, row_pool_cot, rstd, w_out,
    )
    act_other, got_u = swap_seq(act, 1), swap_seq(send_u, 1)
    layer_blocks = exchange(l0, l1, l2)

    def cut(value):
        return value.reshape(-1, row_count, 2, value.shape[-2] // row_count // 2, half)

    row_other, mixed_other, low_other, grad_mixed = together(row_other, mixed_other, low_other, grad_mixed)
    keep_h, send_h, sums_head = attend_back(core, expo, total, q, k, v, mix_t, grad_mixed)
    act_other, got_u, layer_blocks, keep_d, send_h = together(act_other, got_u, layer_blocks, keep_d, send_h)
    got_h = swap_seq(send_h, 1)
    grad_w_down = cut(down_weight(act, act_other, keep_d))
    layer_blocks, got_h, grad_w_down = together(forward(layer_blocks), got_h, grad_w_down)
    down = grad_w_down.shape[3]
    sizes = [down * at // 12 for at in D_SPLIT]
    d_a, d_b, d_c = (ex.part(grad_w_down, sum(sizes[:at]), sizes[at]) for at in range(3))
    d_parts = [d_a, d_b, d_c]
    ex.tick([(d_c, z1), (d_b, y), (d_a, "x")])
    keep_u = ex.before(d_parts, keep_u)
    grad_w_up, grad_w_out, head, lines, *grads = weights(
        row_count, core, low_far, low_other, mixed, mixed_other, row, row_other, keep_u, got_u, keep_h, send_h, got_h,
        hidden_one, w_query, w_key, w_value, b_up_sum, sums_head, sums_one, sums_two,
    )
    grad_w_up, grad_w_out, head = cut(grad_w_up), cut(grad_w_out), cut(head)
    rows = grad_w_up.shape[3]
    u_a, u_b, u_c, o = ex.part(grad_w_up[:1]), ex.part(grad_w_up[1:2]), ex.part(grad_w_up[2:]), ex.part(grad_w_out)
    u_parts = [u_a, u_b, u_c, o]
    third = rows // 3
    q_part, k_first, k_rest = ex.part(head[0:1]), ex.part(head[1:2], 0, third), ex.part(head[1:2], third, rows - third)
    v_part, line_part = ex.part(head[2:3]), ex.part(lines[None])
    a_parts, b_parts = [q_part, k_first, line_part], [k_rest, v_part]
    head_parts = a_parts + b_parts

    def moves(parts, axis):
        return [(part, axis) for part in parts]

    ex.tick(
        moves([d_b, u_a, *a_parts], "x") + moves([d_a, u_b, *b_parts], y) + moves([u_c, o], z1) + moves([d_c], z2)
    )
    layer_blocks = ex.before(head_parts, layer_blocks)
    layer_out, pooled = place(where_at, layer_blocks, part, True)
    layer_out, grads = ex.after(d_parts + u_parts + head_parts, (layer_out, grads))
    ex.tick(
        moves([u_c], z2) + moves([d_c, u_a, *a_parts], y) + moves([u_b, o, *b_parts], "x") + moves([d_a, d_b], z1)
    )
    ex.tick(moves([u_a, u_b, *head_parts], z1) + moves([u_c, o], y) + moves([d_a, d_b], z2) + moves([d_c], "x"))
    grads = ex.before(head_parts, grads)
    grad_blocks = exchange(*grads)
    late = u_parts + head_parts
    if zs[2:]:
        ex.tick(moves([u_a, u_b, o, *head_parts], z2) + moves([u_c], "x"))
        for z in zs[2:]:
            ex.tick(moves(d_parts + late, z))
        down_piece = ex.tick([], d_parts)
    else:
        down_piece = ex.tick(moves([u_a, u_b, o, *head_parts], z2) + moves([u_c], "x"), d_parts)
    d_kinds = (tuple((sum(sizes[:at]), sizes[at], sum(sizes[:at]), 0) for at in range(3) if sizes[at]),)
    grad_tokens = place(where_at, forward(grad_blocks), part, False)[0]
    grad_tokens, down_pieces = ex.after(late, (grad_tokens, gather(down_piece)))
    late_piece = ex.tick([], late)
    late_pieces = gather(late_piece)
    down_pieces, late_piece = together(down_pieces, late_piece)
    out_w_down = final(last_bits, down_pieces, d_kinds, [shape((2 * down, width), f32)])[0]
    out_w_down, late_pieces = together(out_w_down, late_pieces)
    wide = [shape((2 * rows, feed_width), f32)] + [shape((2 * rows, width), f32)] * 4 + [shape((1, width // row_count), f32)] * 8
    wide += [shape((1, feed_width // row_count), f32)]
    at_q = 5 * rows
    at_k = at_q + rows
    at_lines = at_k + third
    at_rest = at_lines + 16
    kinds = (
        tuple((at * rows, rows, 0, at * half) for at in range(4)),
        ((4 * rows, rows, 0, 0),),
        ((at_q, rows, 0, 0),),
        ((at_k, third, 0, 0), (at_rest, rows - third, third, 0)),
        ((at_rest + rows - third, rows, 0, 0),),
        *[((at_lines, 16, at, None),) for at in (*range(8), 16)],
    )
    out_w_up, out_w_out, out_w_query, out_w_key, out_w_value, *rest = final(last_bits, late_pieces, kinds, wide)
    rest = [line.reshape(-1) for line in rest]
    return (
        layer_out, pooled, grad_tokens,
        out_w_query, out_w_key, out_w_value, rest[0], rest[1], out_w_out, rest[4], rest[2], rest[3],
        out_w_up, rest[8], out_w_down, rest[7], rest[5], rest[6],
    )


def solution(mesh):
    split = P("rows", "seq", None)
    in_specs = (split, P("rows", "seq"), *[P()] * 15, split, P("rows", None, None))
    mat, line = P("rows", None), P("rows")
    out_specs = (
        split, P("rows", None, None), split,
        mat, mat, mat, line, line, mat, line, line, line, mat, line, mat, line, line, line,
    )
    body = functools.partial(local, mesh.shape["rows"])
    return jax.shard_map(body, mesh=mesh, in_specs=in_specs, out_specs=out_specs, check_vma=False)
```

```python
import functools

import jax
import jax.numpy as jnp
from jax import lax
from jax.experimental import pallas as pl
from jax.experimental.pallas import tpu as pltpu
from jax.sharding import PartitionSpec as P

HEADS = 12
SEGS = 8
FEED_TILE = 1024
PIECES = 4
COST = 0.001
LATE = 4000.0
D_SPLIT = (4, 4, 4)
BYTES = 1.0
norm_eps = 1e-12
pool_eps = 1e-06
bf16 = jnp.bfloat16
f32 = jnp.float32
MIB = 2**20


def shape(dims, dtype=bf16):
    return jax.ShapeDtypeStruct(dims, dtype)


def dot(left, right, left_dim=1, right_dim=0):
    return lax.dot_general(
        left, right, (((left_dim,), (right_dim,)), ((), ())), preferred_element_type=f32
    )


def in_vmem(kernel, name, mib, outs, args, work, scratch=(), scalars=0, fetch=(), far_in=(), near=(), free=(), far_own=()):
    args, outs, fetch = list(args), list(outs), dict(fetch)
    in_specs = [pl.BlockSpec(memory_space=pltpu.VMEM)] * len(args)
    for at in range(scalars):
        in_specs[at] = pl.BlockSpec(memory_space=pltpu.SMEM)
    for at in [*fetch, *far_in]:
        in_specs[at] = pl.BlockSpec(memory_space=pltpu.HBM)
        args[at] = pltpu.with_memory_space_constraint(args[at], pltpu.HBM)
    out_specs = [pl.BlockSpec(memory_space=pltpu.VMEM)] * len(outs)
    far_out = [at for at in range(len(outs)) if at not in near and at not in free and at not in far_own]
    held_in = [pltpu.VMEM(args[at].shape, args[at].dtype) for at in fetch]
    held_out = [pltpu.VMEM(outs[at].shape, outs[at].dtype) for at in far_out]
    size = sum(v.size * v.dtype.itemsize for v in (*args, *outs))
    for at in [*far_out, *far_own]:
        out_specs[at] = pl.BlockSpec(memory_space=pltpu.HBM)
        outs[at] = pltpu.HBM(outs[at].shape, outs[at].dtype)
    pieces = [(at, dim, count, piece) for at, (dim, count) in fetch.items() for piece in range(count)]
    pieces.sort(key=lambda piece: piece[3])
    count_in, count_out = len(args), len(outs)

    def body(*refs):
        ins, results = list(refs[:count_in]), list(refs[count_in : count_in + count_out])
        rest = list(refs[count_in + count_out :])
        own = [rest.pop(0) for _ in scratch]
        buffers = dict(zip(fetch, [rest.pop(0) for _ in held_in]))
        staged = dict(zip(far_out, [rest.pop(0) for _ in held_out]))
        sems_in, sems_out = rest
        copies = {at: [] for at in fetch}
        for number, (at, dim, count, piece) in enumerate(pieces):
            length = args[at].shape[dim] // count
            where = [slice(None)] * args[at].ndim
            where[dim] = pl.ds(piece * length, length)
            where = tuple(where)
            copy = pltpu.make_async_copy(ins[at].at[where], buffers[at].at[where], sems_in.at[number])
            copy.start()
            copies[at].append(copy)
        for at in fetch:
            ins[at] = Fetched(buffers[at], copies[at])
        sent = {}

        def flush(*numbers):
            for at in numbers:
                sent[at] = pltpu.make_async_copy(staged[at], results[at], sems_out.at[at])
                sent[at].start()

        kernel(*ins, *[staged.get(at, results[at]) for at in range(count_out)], *own, flush=flush)
        flush(*[at for at in far_out if at not in sent])
        for copy in sent.values():
            copy.wait()
        for one in ins:
            if isinstance(one, Fetched):
                one.finish()

    sems = [pltpu.SemaphoreType.DMA((max(1, len(pieces)),)), pltpu.SemaphoreType.DMA((len(outs),))]
    return pl.pallas_call(
        body,
        in_specs=in_specs,
        out_specs=out_specs,
        out_shape=outs,
        scratch_shapes=[*scratch, *held_in, *held_out, *sems],
        compiler_params=pltpu.CompilerParams(vmem_limit_bytes=mib * MIB),
        cost_estimate=pl.CostEstimate(flops=int(work * COST), bytes_accessed=int(size * BYTES), transcendentals=0),
        name=name,
    )(*args)


class Fetched:
    def __init__(self, ref, copies):
        self.ref, self.copies, self.waited = ref, copies, set()

    def piece(self, at=0):
        if at not in self.waited:
            self.waited.add(at)
            self.copies[at].wait()
        return self.ref

    def finish(self):
        for at in range(len(self.copies)):
            self.piece(at)

    def __getitem__(self, where):
        self.finish()
        return self.ref[where]

    @property
    def shape(self):
        return self.ref.shape


def load_kernel(*refs, flush):
    count = (len(refs) - 1) // 2
    copies = [pltpu.make_async_copy(refs[at], refs[count + at], refs[-1].at[at]) for at in range(count)]
    for copy in copies:
        copy.start()
    for copy in copies:
        copy.wait()


def load(*arrays):
    outs = [shape(v.shape, v.dtype) for v in arrays]
    every = range(len(arrays))
    scratch = [pltpu.SemaphoreType.DMA((len(arrays),))]
    return in_vmem(load_kernel, "load_weights", 4, outs, arrays, 1e9, scratch, far_in=every, near=every)


def split_two(value):
    high = value.astype(bf16)
    return high, (value - high.astype(f32)).astype(bf16)


def attend_kernel(
    t0, t1, t2, t3, wq, wk, wv, bq, bv,
    exp_out, total_out, row_out, q_out, k_out, v_out, mix_t, mixed_out, mixed_far, row_near, ids_out,
    mask, stage, sems,
    *, flush,
):
    blocks = (t0, t1, t2, t3)
    part = t0.shape[0] - 16
    length, width = row_out.shape
    for at, block in enumerate(blocks):
        row_out[at * part : (at + 1) * part, :] = block[:part, :]
    rows = row_out[...]
    row_near[...] = rows
    q_out[...] = (dot(rows, wq[...]) + bq[...]).astype(bf16) * bf16(0.125)
    k_out[...] = dot(rows, wk[...]).astype(bf16)
    v_out[...] = (dot(rows, wv[...]) + bv[...]).astype(bf16)
    flush(2, 3, 4, 5)
    ids = jnp.concatenate([block[part : part + 16, :part].astype(f32)[0:1] for block in blocks], axis=1)
    ids_out[...] = jnp.broadcast_to(ids, ids_out.shape)
    column = jnp.broadcast_to(ids, (128, length)).T[:, 0:1]
    mask[...] = jnp.where(column == ids, 0.0, -1e30)

    sent = []
    for pair in range(width // 128):
        lanes = slice(pair * 128, pair * 128 + 128)
        keys = k_out[:, lanes]
        query_t = q_out[:, lanes].T
        value_t = v_out[:, lanes].T
        for half in range(2):
            at = slice(half * 64, half * 64 + 64)
            head = 2 * pair + half
            scores = dot(keys[:, at], query_t[at, :]) + mask[...]
            expo = jnp.exp(scores - jnp.max(scores, axis=0, keepdims=True))
            inverse = 1.0 / jnp.sum(expo, axis=0, keepdims=True)
            low = expo.astype(bf16)
            stage[head] = low
            sent.append(pltpu.make_async_copy(stage.at[head], exp_out.at[head], sems.at[head]))
            sent[-1].start()
            total_out[head : head + 1, :] = inverse
            mix_t[head * 64 : head * 64 + 64, :] = dot(value_t[at, :], low) * inverse

    mixed = mix_t[...].astype(bf16).T
    mixed_out[...] = mixed
    mixed_far[...] = mixed
    flush(1, 6)
    for copy in sent:
        copy.wait()


def attend(blocks, wq, wk, wv, bq, bv):
    part, width = blocks[0].shape
    length = (part - 16) * 4
    heads = width // 64
    flat = shape((length, width))
    outs = [
        shape((heads, length, length)), shape((16, length), f32), flat, flat, flat, flat, shape((width, length), f32),
        flat, flat, flat, shape((8, length), f32),
    ]
    args = (*blocks, wq, wk, wv, bq, bv)
    scratch = [
        pltpu.VMEM((length, length), f32),
        pltpu.VMEM((heads, length, length), bf16),
        pltpu.SemaphoreType.DMA((heads,)),
    ]
    fetch = {at: (0, 1) for at in range(1, 4)}
    return in_vmem(
        attend_kernel, "attend_forward", 20, outs, args, 10e9 * LATE, scratch, fetch=fetch, near=(7, 9, 10), far_own=(0,)
    )


def gelu_both(v):
    phi = 0.5 + 0.5 * lax.erf(v * 0.7071067811865476)
    bell = jnp.exp2(v * (v * (-0.5 * 1.4426950408889634)))
    return v * phi, phi + (v * 0.3989422804014327) * bell


def pool_windows(width):
    return (width, width * 2 // 3, width // 3, width // 6, width // 12)


def pool_places(width):
    w = pool_windows(width)
    return ((0, 0), (8, 0), (8, w[1]), (16, 0), (16, w[3]))


def feed_kernel(
    core, mixed, w_up, b_up, w_down, row, gain_a, shift_a, b_down, gain, shift, c0, c1, c2, c3, ids, pool_cot, bo, wo,
    low_far, act_out, l0, l1, l2, keep_out, sums_out,
    keep_u, send_u, b_up_out, hidden_one, mixed_out, sums_one,
    acc, unit_s, rstd_s, slope_out, low_out, up_s, down_s, cot_s, out_s, normal, rstd_a, sems,
    *, flush,
):
    length, width = mixed.shape
    part = length // 4
    hidden_width = w_up.shape[1]
    tile = FEED_TILE
    early, ups, downs = [], [], []
    numbers = iter(range(3 * PIECES + 4))
    for piece in range(PIECES):
        rows = slice(piece * (width // PIECES), (piece + 1) * (width // PIECES))
        early.append(pltpu.make_async_copy(wo.at[rows, :], out_s.at[rows, :], sems.at[next(numbers)]))
        ups.append(pltpu.make_async_copy(w_up.at[rows, :], up_s.at[rows, :], sems.at[next(numbers)]))
        rows = slice(piece * (hidden_width // PIECES), (piece + 1) * (hidden_width // PIECES))
        downs.append(pltpu.make_async_copy(w_down.at[rows, :], down_s.at[rows, :], sems.at[next(numbers)]))
    late = [
        pltpu.make_async_copy(source, cot_s.at[number], sems.at[next(numbers)])
        for number, source in enumerate((c0, c1, c2, c3))
    ]
    for copy in early + ups:
        copy.start()
    for copy in early:
        copy.wait()
    for copy in downs + late:
        copy.start()
    acc[...] = dot(mixed[...], out_s[...])
    for at in range(0, length, 32):
        rows = slice(at, at + 32)
        hidden = row[rows, :].astype(f32) + (acc[rows, :] + bo[...])
        centered = hidden - jnp.mean(hidden, axis=-1, keepdims=True)
        rstd = lax.rsqrt(jnp.mean(centered * centered, axis=-1, keepdims=True) + norm_eps)
        unit = centered * rstd
        normal[rows, :] = unit
        rstd_a[rows, :] = jnp.broadcast_to(rstd, (32, 128))
        low_far[rows, :] = (unit * gain_a[...] + shift_a[...]).astype(bf16)
    flush(0)
    for copy in ups:
        copy.wait()
    for at in range(0, hidden_width, tile):
        cols = slice(at, at + tile)
        up = dot(low_far[...], up_s[:, cols]) + b_up[:, cols]
        active, slope = gelu_both(up)
        active_low = active.astype(bf16)
        act_out[:, cols] = active_low
        slope_out[:, cols] = slope.astype(bf16)
        if at == 0:
            for copy in downs:
                copy.wait()
        down = dot(active_low, down_s[cols, :])
        if at == 0:
            acc[...] = down
        else:
            acc[...] += down

    groups = lax.broadcasted_iota(jnp.int32, (16, length), 0).astype(f32)
    member = jnp.where((groups == ids[0:1, :]) & (groups < SEGS), 1.0, 0.0).astype(bf16)
    outs = (l0, l1, l2.at[0], l2.at[1])
    seg_sums = jnp.zeros((16, width), f32)
    for at in range(4):
        rows = slice(at * part, (at + 1) * part)
        hidden = normal[rows, :] * gain_a[...] + shift_a[...] + (acc[rows, :] + b_down[...])
        centered = hidden - jnp.mean(hidden, axis=-1, keepdims=True)
        rstd = lax.rsqrt(jnp.mean(centered * centered, axis=-1, keepdims=True) + norm_eps)
        unit = centered * rstd
        unit_s[rows, :] = unit
        rstd_s[rows, :] = jnp.broadcast_to(rstd, (part, 128))
        result = unit * gain[...] + shift[...]
        outs[at][0:part, :] = result.astype(bf16)
        for piece in split_two(result):
            seg_sums += dot(member[:, rows], piece)
    seg_sums = seg_sums[:SEGS]
    first_lane = 0
    total = jnp.zeros((SEGS, width), f32)
    pooled = []
    for window in pool_windows(width):
        sums = seg_sums[:, :window]
        cot = pool_cot[:, first_lane : first_lane + window]
        factor = lax.rsqrt(jnp.mean(sums * sums, axis=-1, keepdims=True) + pool_eps)
        pooled.append(sums * factor)
        inner = jnp.sum(cot * sums, axis=-1, keepdims=True) * (factor * factor * factor / window)
        piece = cot * factor - sums * inner
        if window < width:
            piece = jnp.concatenate([piece, jnp.zeros((SEGS, width - window), f32)], axis=1)
        total += piece
        first_lane += window
    zeros = jnp.zeros((8, width), f32)
    rest = jnp.zeros((8, width - pooled[3].shape[1] - pooled[4].shape[1]), f32)
    upper = jnp.concatenate([pooled[0], jnp.concatenate(pooled[1:3], axis=1)], axis=0).astype(bf16)
    lower = jnp.concatenate([jnp.concatenate([pooled[3], pooled[4], rest], axis=1), zeros], axis=0).astype(bf16)
    for out in outs:
        out[part : part + 16, :] = upper
        out[part + 16 : part + 32, :] = lower
    flush(2, 3, 4)
    total = split_two(jnp.concatenate([total, zeros], axis=0))
    half = width // 2
    first = core[0] == 0
    sums = [jnp.zeros((1, width), f32)] * 3
    for copy in late:
        copy.wait()
    for at in range(4):
        rows = slice(at * part, (at + 1) * part)
        grad = cot_s[at].astype(f32) + sum(dot(member[:, rows], piece, 0, 0) for piece in total)
        unit = unit_s[rows, :]
        scaled = grad * gain[...]
        hidden_grad = rstd_s[rows, 0:1] * (
            scaled
            - jnp.mean(scaled, axis=-1, keepdims=True)
            - unit * jnp.mean(scaled * unit, axis=-1, keepdims=True)
        )
        acc[rows, :] = hidden_grad
        rounded = hidden_grad.astype(bf16)
        low_out[rows, :] = rounded
        keep_out[rows, :] = jnp.where(first, rounded[:, :half], rounded[:, half:])
        act_out[rows, hidden_width:] = jnp.where(first, rounded[:, half:], rounded[:, :half])
        for to, value in enumerate((grad * unit, grad, rounded.astype(f32))):
            sums[to] += jnp.sum(value, axis=0, keepdims=True)
    sums_out[...] = jnp.concatenate([*sums, jnp.zeros((5, width), f32)], axis=0)

    half_feed = hidden_width // 2
    for at, out in enumerate((send_u, keep_u)):
        which = core[0] if at == 1 else 1 - core[0]
        cols = pl.ds(pl.multiple_of(which * half_feed, 128), half_feed)
        grad_up = (dot(low_out[...], down_s[cols, :], 1, 1) * slope_out[:, cols].astype(f32)).astype(bf16)
        out[:, :half_feed] = grad_up
        b_up_out[:, cols] = jnp.broadcast_to(jnp.sum(grad_up.astype(f32), axis=0, keepdims=True), (8, half_feed))
        if at == 0:
            flush(1, 5, 6)
        back = dot(grad_up, up_s[:, cols], 1, 1)
        acc[...] += back

    sums = [jnp.zeros((1, width), f32)] * 3
    for at in range(0, length, 64):
        rows = slice(at, at + 64)
        grad = acc[rows, :]
        unit = normal[rows, :]
        scaled = grad * gain_a[...]
        hidden_grad = rstd_a[rows, 0:1] * (
            scaled
            - jnp.mean(scaled, axis=-1, keepdims=True)
            - unit * jnp.mean(scaled * unit, axis=-1, keepdims=True)
        )
        hidden_one[rows, :] = hidden_grad
        rounded = hidden_grad.astype(bf16)
        low_out[rows, :] = rounded
        keep_u[rows, half_feed:] = jnp.where(first, rounded[:, :half], rounded[:, half:])
        send_u[rows, half_feed:] = jnp.where(first, rounded[:, half:], rounded[:, :half])
        for to, value in enumerate((grad * unit, grad, rounded.astype(f32))):
            sums[to] += jnp.sum(value, axis=0, keepdims=True)
    flush(8, 7, 9, 10)
    mixed_out[...] = dot(low_out[...], out_s[...], 1, 1).astype(bf16)
    sums_one[...] = jnp.concatenate([*sums, jnp.zeros((5, width), f32)], axis=0)


def feed(core, mixed, w_up, b_up, w_down, row, gain_a, shift_a, b_down, gain, shift, cots, ids, pool_cot, bo, wo):
    length, width = mixed.shape
    hidden = w_up.shape[1]
    half = shape((length, width // 2))
    wide = shape((length, width), f32)
    part = length // 4 + 32
    outs = [
        shape((length, width)), shape((length, hidden + width // 2)), shape((part, width)), shape((part, width)), shape((2, part, width)),
        half, shape((8, width), f32), shape((length, hidden // 2 + width // 2)), shape((length, hidden // 2 + width // 2)),
        shape((8, hidden), f32), wide, shape((length, width)), shape((8, width), f32),
    ]
    scratch = [
        pltpu.VMEM((length, width), f32),
        pltpu.VMEM((length, width), f32),
        pltpu.VMEM((length, 128), f32),
        pltpu.VMEM((length, hidden), bf16),
        pltpu.VMEM((length, width), bf16),
        pltpu.VMEM(w_up.shape, bf16),
        pltpu.VMEM(w_down.shape, bf16),
        pltpu.VMEM((4, length // 4, width), bf16),
        pltpu.VMEM((width, width), bf16),
        pltpu.VMEM((length, width), f32),
        pltpu.VMEM((length, 128), f32),
        pltpu.SemaphoreType.DMA((3 * PIECES + 4,)),
    ]
    args = (core, mixed, w_up, b_up, w_down, row, gain_a, shift_a, b_down, gain, shift, *cots, ids, pool_cot, bo, wo)
    return in_vmem(
        feed_kernel, "feed_both", 37, outs, args, 18e9 * LATE, scratch, 1, far_in=(2, 4, 11, 12, 13, 14, 18)
    )


def attend_back_kernel(
    core, expo, total, q, k, v, mix_t, grad_mixed, keep_out, send_out, sums_out,
    held, q_s, k_s, v_s, mix_s, grad_s, sems,
    *, flush,
):
    length = expo.shape[1]
    pairs = q.shape[1] // 128
    per = pairs // 2
    slots = held.shape[0]

    def copies(at):
        which = core[0] if at >= per else 1 - core[0]
        pair = which * per + at % per
        lanes = pl.ds(pl.multiple_of(pair * 128, 128), 128)
        slot = at % slots
        sources = [
            (q.at[:, lanes], q_s), (k.at[:, lanes], k_s), (v.at[:, lanes], v_s),
            (mix_t.at[lanes, :], mix_s), (grad_mixed.at[:, lanes], grad_s),
            (expo.at[pl.ds(2 * pair, 2)], held),
        ]
        return [
            pltpu.make_async_copy(source, to.at[slot], sems.at[slot, number])
            for number, (source, to) in enumerate(sources)
        ]

    def start(group):
        for at in group:
            for copy in copies(at):
                copy.start()

    groups = [range(0, 1), range(1, per), range(per, pairs)]
    start(groups[0])
    start(groups[1])
    for at in range(pairs):
        for number, group in enumerate(groups):
            if at == group[0]:
                for member in group:
                    for copy in copies(member):
                        copy.wait()
                if number == 0:
                    start(groups[2])
        which = core[0] if at >= per else 1 - core[0]
        out = keep_out if at >= per else send_out
        pair, slot = at % per, at % slots
        lanes = pl.ds(pl.multiple_of(which * (per * 128) + pair * 128, 128), 128)
        grad_t = grad_s[slot].T.astype(f32)
        query, value, mix = q_s[slot], v_s[slot], mix_s[slot]
        key_t = k_s[slot].T
        halves = []
        inner = []
        for half in range(2):
            rows = slice(half * 64, half * 64 + 64)
            inverse = total[pl.ds(which * pairs + 2 * pair + half, 1), :]
            scaled = (grad_t[rows] * inverse).astype(bf16)
            halves.append(scaled)
            inner.append(jnp.sum(scaled.astype(f32) * mix[rows], axis=0, keepdims=True))
        scaled_rows = jnp.concatenate(halves, axis=0).T
        grads_q, grads_k, grads_v = [], [], []
        for half in range(2):
            rows = slice(half * 64, half * 64 + 64)
            probs = held[slot, half]
            grad_probs = dot(value[:, rows], halves[half])
            grad_scores = (probs.astype(f32) * (grad_probs - inner[half])).astype(bf16)
            grads_v.append(dot(probs, scaled_rows[:, rows]))
            grads_k.append(dot(grad_scores, query[:, rows]))
            grads_q.append(dot(key_t[rows, :], grad_scores))
        here = slice(pair * 128, pair * 128 + 128)
        grad_query = (jnp.concatenate(grads_q, axis=0).T * 0.125).astype(bf16)
        grad_value = jnp.concatenate(grads_v, axis=1).astype(bf16)
        out[0, :, here] = grad_query
        out[1, :, here] = jnp.concatenate(grads_k, axis=1).astype(bf16)
        out[2, :, here] = grad_value
        sums_out[:, lanes] = jnp.concatenate(
            [
                jnp.sum(grad_query.astype(f32), axis=0, keepdims=True),
                jnp.sum(grad_value.astype(f32), axis=0, keepdims=True),
                jnp.zeros((6, 128), f32),
            ],
            axis=0,
        )


def attend_back(core, expo, total, q, k, v, mix_t, grad_mixed):
    length, width = q.shape
    outs = [shape((3, length, width // 2)), shape((3, length, width // 2)), shape((8, width), f32)]
    args = (core, expo, total, q, k, v, mix_t, grad_mixed)
    slots = width // 128
    scratch = [
        pltpu.VMEM((slots, 2, length, length), bf16),
        *[pltpu.VMEM((slots, length, 128), bf16)] * 3,
        pltpu.VMEM((slots, 128, length), f32),
        pltpu.VMEM((slots, length, 128), bf16),
        pltpu.SemaphoreType.DMA((slots, 6)),
    ]
    return in_vmem(
        attend_back_kernel, "attend_backward", 20, outs, args, 9e9 * LATE, scratch, 1,
        fetch={2: (0, 1)}, far_in=(1, 3, 4, 5, 6, 7), free=(0, 1, 2),
    )


def add_input_grad(core, hidden, keep, send, wq, wk, wv, o0, o1, o2):
    width = hidden.shape[1]
    half = width // 2
    part = o0.shape[0]
    mine = pl.ds(pl.multiple_of(core[0] * half, 128), half)
    other = pl.ds(pl.multiple_of((1 - core[0]) * half, 128), half)
    total = hidden[...]
    for at, weight in enumerate((wq, wk, wv)):
        total += dot(keep[at], weight[:, mine], 1, 1) + dot(send[at], weight[:, other], 1, 1)
    total = total.astype(bf16)
    for at, out in enumerate((o0, o1, o2.at[0], o2.at[1])):
        out[...] = total[at * part : (at + 1) * part]


def down_weight_kernel(own, other, keep, out, *, flush):
    size = out.shape[0] // 4
    for at in range(4):
        rows = slice(at * size, (at + 1) * size)
        left, right = own[:, rows], other[:, rows]
        out[rows, :] = (dot(left, keep[...], 0, 0) + dot(right, other[:, 4 * size :], 0, 0)).astype(bf16)


def down_weight(own, other, keep):
    half = keep.shape[1]
    outs = [shape((own.shape[1] - half, half))]
    return in_vmem(down_weight_kernel, "down_weight", 14, outs, (own, other, keep), 4e9 * LATE, free=(0,))[0]


def weights_kernel(
    core, low, low_other, mixed, mixed_other, row, row_other, keep_u, got_u, keep_h, send_h, got_h, hidden, wq, wk, wv,
    b_up, sums_head, sums_one, sums_two,
    out_u, out_o, out_h, vec, g0, g1, g2,
    *, flush,
):
    half = out_o.shape[1]
    tiles = out_u.shape[0]
    for at in range(tiles):
        cols = slice(at * half, (at + 1) * half)
        out_u[at] = (dot(low[...], keep_u[:, cols], 0, 0) + dot(low_other[...], got_u[:, cols], 0, 0)).astype(bf16)
    cols = slice(tiles * half, (tiles + 1) * half)
    out_o[...] = (dot(mixed[...], keep_u[:, cols], 0, 0) + dot(mixed_other[...], got_u[:, cols], 0, 0)).astype(bf16)
    for at in range(3):
        out_h[at] = (dot(row[...], keep_h[at], 0, 0) + dot(row_other[...], got_h[at], 0, 0)).astype(bf16)
    add_input_grad(core, hidden, keep_h, send_h, wq, wk, wv, g0, g1, g2)
    shards = vec.shape[0]
    lines = jnp.concatenate([sums_head[0:2], sums_one[0:3], sums_two[0:3]], axis=0)
    line = lines.shape[1] // shards
    up = b_up.shape[1] // shards
    first = lax.broadcasted_iota(jnp.int32, (8, up), 0) == 0
    for at in range(shards):
        piece = lines[:, at * line : (at + 1) * line]
        if line < half:
            piece = jnp.concatenate([piece, jnp.zeros((8, half - line), f32)], axis=1)
        vec[at, 0] = jnp.concatenate([piece, jnp.zeros((8, half), f32)], axis=0).astype(bf16)
        piece = jnp.where(first, b_up[:, at * up : (at + 1) * up], 0.0)
        if up < half:
            piece = jnp.concatenate([piece, jnp.zeros((8, half - up), f32)], axis=1)
        vec[at, 1] = jnp.concatenate([piece, jnp.zeros((8, half), f32)], axis=0).astype(bf16)


def weights(shards, *args):
    low, keep_u = args[1], args[7]
    length, width = low.shape
    half = width // 2
    part = length // 4
    outs = [
        shape((keep_u.shape[1] // half - 1, width, half)), shape((width, half)), shape((3, width, half)),
        shape((shards, 2, 16, half)), shape((part, width)), shape((part, width)), shape((2, part, width)),
    ]
    every = range(len(outs))
    return in_vmem(weights_kernel, "other_weights", 14, outs, args, 11e9 * LATE, scalars=1, free=every)


def pack_kernel(seq_at, tokens, *rest, flush):
    ids, outs, sems = (rest[0], rest[1:5], rest[5]) if len(rest) == 6 else (None, rest[:4], rest[4])
    part, width = tokens.shape[1:]
    copies = []
    for at in (2, 3, 1, 0):
        copies.append(pltpu.make_async_copy(tokens.at[seq_at[0] ^ at], outs[at].at[:part, :], sems.at[at]))
        copies[-1].start()
    if ids is not None:
        for at, out in enumerate(outs):
            line = ids[pl.ds(seq_at[0] ^ at, 1), :].astype(f32)
            line = jnp.concatenate([line, jnp.zeros((1, width - part), f32)], axis=1)
            out[part : part + 16, :] = jnp.broadcast_to(line, (16, width)).astype(bf16)
    for copy in copies:
        copy.wait()


def pack(seq_at, tokens, ids=None):
    _, part, width = tokens.shape
    extra = 0 if ids is None else 16
    args = (seq_at, tokens) if ids is None else (seq_at, tokens, ids)
    outs = [shape((part + extra, width))] * 4
    fetch = {} if ids is None else {2: (0, 1)}
    scratch = [pltpu.SemaphoreType.DMA((4,))]
    return in_vmem(
        pack_kernel, "pack_rows", 6, outs, args, 1e8, scratch, 1, fetch=fetch, far_in=(1,), near=(0, 1, 2, 3)
    )


def place_kernel(seq_at, b0, b1, b2, b3, out, *pooled, flush):
    part, width = out.shape[1:]
    for at, block in enumerate((b0, b1, b2, b3)):
        to = seq_at[0] ^ at
        rows = block.piece()[0] if at == 2 else block[...]
        out[to] = rows[:part, :]
        if pooled:
            first = 0
            rows = rows[part : part + 32, :].astype(f32)
            for window, (row, lane) in zip(pool_windows(width), pool_places(width)):
                pooled[0][to, :, first : first + window] = rows[row : row + 8, lane : lane + window]
                first += window


def place(seq_at, blocks, part, pooled):
    width = blocks[0].shape[1]
    outs = [shape((4, part, width))]
    if pooled:
        outs.append(shape((4, SEGS, sum(pool_windows(width))), f32))
    fetch = {at: (0, 1) for at in range(1, 5)}
    return in_vmem(place_kernel, "place_rows", 6, outs, (seq_at, *blocks), 1e8, scalars=1, fetch=fetch)


def swap_seq(value, mask):
    return lax.ppermute(value, "seq", [(at, at ^ mask) for at in range(4)])


def exchange(own, core_block, chip_blocks):
    got_core = swap_seq(core_block, 1)
    got_chip = swap_seq(chip_blocks, 2)
    return [own, got_core, got_chip]


def forward(blocks):
    return [*blocks, swap_seq(blocks[2][1], 1)]


class Part:
    def __init__(self, blocks, names, first, rows):
        self.blocks, self.names, self.first, self.rows, self.got = blocks, names, first, rows, None


class Exchanges:
    def __init__(self, row_at, seq_at, row_count):
        self.row_count = row_count
        self.axes = ["x"] + [1 << at for at in range(row_count.bit_length() - 1)]
        self.bits = jnp.stack([(seq_at >> 1) & 1] + [(row_at // axis) & 1 for axis in self.axes[1:]])

    def part(self, blocks, first=0, rows=None):
        names = [("tile", blocks.shape[0])] + [(axis, 2) for axis in reversed(self.axes[1:])] + [("x", 2)]
        rows = blocks.shape[3] if rows is None else rows
        return Part(blocks.reshape(-1, *blocks.shape[3:]), names, first, rows)

    def swap(self, value, axis):
        if axis == "x":
            return swap_seq(value, 2)
        return lax.ppermute(value, "rows", [(at, at ^ axis) for at in range(self.row_count)])

    def tick(self, moves, settle=(), far=False):
        parts = [part for part, _ in moves] + list(settle)
        ins = []
        for part in parts:
            for value in (part.blocks, part.got and part.got[0]):
                if value is not None and not any(value is other for other in ins):
                    ins.append(value)
        find = lambda value: [value is other for other in ins].index(True)
        lanes = parts[0].blocks.shape[2]
        used = list(dict.fromkeys(axis for _, axis in moves))
        outs, plan, rows_of, kept = [], [], dict.fromkeys([*used, None], 0), []
        for part, axis in [*moves, *[(part, None) for part in settle]]:
            count = part.blocks.shape[0]
            source = (find(part.blocks), part.first, part.rows, part.got and (find(part.got[0]), part.got[1]))
            if axis is None:
                plan.append((source, axis, [(at, None) for at in range(count)], rows_of[axis], None))
                rows_of[axis] += count * part.rows
                continue
            names = [name for name, _ in part.names]
            low = 1
            for _, size in part.names[names.index(axis) + 1 :]:
                low *= size
            pairs = [(at, at + low) for at in range(count) if (at // low) % 2 == 0]
            plan.append((source, axis, pairs, rows_of[axis], len(kept)))
            kept.append(shape((count // 2, part.rows, lanes)))
            part.got = (axis, rows_of[axis])
            rows_of[axis] += len(pairs) * part.rows
            part.names = [entry for entry in part.names if entry[0] != axis]
        flat = [*used, *([None] if settle else [])]
        outs = [shape((rows_of[axis], lanes)) for axis in flat] + kept

        def kernel(bits, *refs, flush):
            given, sends, keeps = refs[: len(ins)], refs[len(ins) : len(ins) + len(flat)], refs[len(ins) + len(flat) :]
            for (blocks, first, rows, got), axis, pairs, row, keep in plan:
                send = sends[flat.index(axis)]

                def value(at):
                    block = given[blocks][at, first : first + rows, :]
                    if got is None:
                        return block
                    other = given[got[0]][got[1] + at * rows : got[1] + (at + 1) * rows, :]
                    return (block.astype(f32) + other.astype(f32)).astype(bf16)

                for number, (zero, one) in enumerate(pairs):
                    where = slice(row + number * rows, row + (number + 1) * rows)
                    if axis is None:
                        send[where, :] = value(zero)
                        continue
                    bit = bits[self.axes.index(axis)] == 0
                    left, right = value(zero), value(one)
                    send[where, :] = jnp.where(bit, right, left)
                    keeps[keep][number] = jnp.where(bit, left, right)

        every = range(len(flat) if far else 0, len(outs))
        results = in_vmem(kernel, "halves", 10, outs, (self.bits, *ins), 1e8, scalars=1, free=every)
        arrived = {axis: self.swap(results[flat.index(axis)], axis) for axis in used}
        for (part, axis), blocks in zip(moves, results[len(flat) :]):
            part.blocks, part.first = blocks, 0
            part.got = (arrived[axis], part.got[1])
        return results[len(used)] if settle else None

    def before(self, parts, value):
        blocks = [part.blocks for part in parts]
        value, blocks = lax.optimization_barrier((value, blocks))
        for part, new in zip(parts, blocks):
            part.blocks = new
        return value

    def after(self, parts, value):
        found = []
        for part in parts:
            if not any(part.got[0] is other for other in found):
                found.append(part.got[0])
        value, new = lax.optimization_barrier((value, found))
        for part in parts:
            at = [part.got[0] is other for other in found].index(True)
            part.got = (new[at], part.got[1])
        return value


def sides(bits, piece, got_x, got_c, got_xc):
    mine = [jnp.where(bits[0] == 0, piece, got_x), jnp.where(bits[0] == 0, got_x, piece)]
    other = [jnp.where(bits[0] == 0, got_c, got_xc), jnp.where(bits[0] == 0, got_xc, got_c)]
    left = [jnp.where(bits[1] == 0, a, b) for a, b in zip(mine, other)]
    right = [jnp.where(bits[1] == 0, b, a) for a, b in zip(mine, other)]
    return left, right


def final_kernel(kinds, bits, *refs, flush):
    own, outs = refs[:4], refs[4:]
    half = own[0].shape[1]
    for pieces, out in zip(kinds, outs):
        for at, rows, to_row, to_lane in pieces:
            left, right = sides(bits, *[ref[at : at + rows, :].astype(f32) for ref in own])
            if to_lane is None:
                line = (left[to_row // 16] + right[to_row // 16])[to_row % 16, : out.shape[0]]
                out[...] = line
                continue
            for x in range(2):
                first = x * (out.shape[0] // 2) + to_row
                out[first : first + rows, to_lane : to_lane + half] = left[x]
                right_lane = out.shape[1] // 2 + to_lane
                out[first : first + rows, right_lane : right_lane + half] = right[x]


def gather(piece, meanwhile=None):
    got_x = swap_seq(piece, 2)
    if meanwhile is not None:
        got_x, meanwhile = lax.optimization_barrier((got_x, meanwhile))
    return (piece, got_x, swap_seq(piece, 1), swap_seq(got_x, 1)), meanwhile


def final(bits, pieces, kinds, outs):
    kernel = functools.partial(final_kernel, kinds)
    return in_vmem(kernel, "final_rows", 12, outs, (bits, *pieces), 1e8, scalars=1)


def together(*values):
    return lax.optimization_barrier(values)


def local(
    row_count,
    tokens, segment_ids, w_query, w_key, w_value, b_query, b_value, w_out, b_out, gain_attn, shift_attn,
    w_up, b_up, w_down, b_down, gain_out, shift_out, token_cot, pool_cot,
):
    part, width = tokens.shape[1:]
    feed_width = w_up.shape[1]
    half = width // 2
    seq_at = lax.axis_index("seq")
    row_at = lax.axis_index("rows")
    core = (seq_at & 1).reshape(1)
    where_at = seq_at.reshape(1)
    ex = Exchanges(row_at, seq_at, row_count)
    last_bits = jnp.stack([(seq_at >> 1) & 1, seq_at & 1])
    y, zs = ex.axes[1], ex.axes[2:]
    z1, z2 = zs[0], zs[1]

    def vec(v):
        return v.reshape(1, -1)

    own = pack(where_at, tokens, segment_ids)
    token_cot, own, near = together(token_cot, own, (w_query, w_key, w_value))
    swapped = {mask: swap_seq(own[mask], mask) for mask in (2, 3, 1)}
    blocks = [own[0]] + [swapped[mask] for mask in (1, 2, 3)]
    near_query, near_key, near_value = load(*near)
    own = pack(where_at, token_cot)
    own, blocks, near_query, near_key, near_value = together(
        own, blocks, near_query, near_key, near_value
    )
    swapped = {mask: swap_seq(own[mask], mask) for mask in (2, 3, 1)}
    cots = [own[0]] + [swapped[mask] for mask in (1, 2, 3)]
    row_pool_cot = lax.dynamic_index_in_dim(pool_cot, seq_at, 0, keepdims=False)

    expo, total, row, q, k, v, mix_t, mixed_near, mixed, row_near, ids_row = attend(
        blocks, near_query, near_key, near_value, vec(b_query), vec(b_value)
    )
    low_far, act, l0, l1, l2, keep_d, sums_two, keep_u, send_u, b_up_sum, hidden_one, grad_mixed, sums_one = feed(
        core, mixed_near, w_up, vec(b_up), w_down, row_near, vec(gain_attn), vec(shift_attn), vec(b_down),
        vec(gain_out), vec(shift_out), cots, ids_row, row_pool_cot, vec(b_out), w_out,
    )
    row_other, mixed_other, low_other = swap_seq(row, 1), swap_seq(mixed, 1), swap_seq(low_far, 1)
    act_other, got_u = swap_seq(act, 1), swap_seq(send_u, 1)
    layer_blocks = exchange(l0, l1, l2)

    def cut(value):
        return value.reshape(-1, row_count, 2, value.shape[-2] // row_count // 2, half)

    row_other, mixed_other, grad_mixed = together(row_other, mixed_other, grad_mixed)
    keep_h, send_h, sums_head = attend_back(core, expo, total, q, k, v, mix_t, grad_mixed)
    act_other, got_u, layer_blocks, keep_d, send_h = together(act_other, got_u, layer_blocks, keep_d, send_h)
    got_h = swap_seq(send_h, 1)
    grad_w_down = cut(down_weight(act, act_other, keep_d))
    layer_blocks, got_h, low_other, grad_w_down = together(forward(layer_blocks), got_h, low_other, grad_w_down)
    down = grad_w_down.shape[3]
    sizes = [down * at // 12 for at in D_SPLIT]
    d_a, d_b, d_c = (ex.part(grad_w_down, sum(sizes[:at]), sizes[at]) for at in range(3))
    d_parts = [d_a, d_b, d_c]
    ex.tick([(d_c, z1), (d_b, y), (d_a, "x")])
    keep_u = ex.before(d_parts, keep_u)
    grad_w_up, grad_w_out, head, lines, *grads = weights(
        row_count, core, low_far, low_other, mixed, mixed_other, row, row_other, keep_u, got_u, keep_h, send_h, got_h,
        hidden_one, w_query, w_key, w_value, b_up_sum, sums_head, sums_one, sums_two,
    )
    grad_w_up, grad_w_out, head = cut(grad_w_up), cut(grad_w_out), cut(head)
    rows = grad_w_up.shape[3]
    u_a, u_b, u_c, o = ex.part(grad_w_up[:1]), ex.part(grad_w_up[1:2]), ex.part(grad_w_up[2:]), ex.part(grad_w_out)
    u_parts = [u_a, u_b, u_c, o]
    third = rows // 3
    q_part, k_first, k_rest = ex.part(head[0:1]), ex.part(head[1:2], 0, third), ex.part(head[1:2], third, rows - third)
    v_part, line_part = ex.part(head[2:3]), ex.part(lines[None])
    a_parts, b_parts = [q_part, k_first, line_part], [k_rest, v_part]
    head_parts = a_parts + b_parts

    def moves(parts, axis):
        return [(part, axis) for part in parts]

    ex.tick(
        moves([d_b, u_a, *a_parts], "x") + moves([d_a, u_b, *b_parts], y) + moves([u_c, o], z1) + moves([d_c], z2)
    )
    layer_blocks = ex.before(head_parts, layer_blocks)
    layer_out, pooled = place(where_at, layer_blocks, part, True)
    grad_core = swap_seq(grads[1], 1)
    layer_out, grads, grad_core = ex.after(d_parts + u_parts + head_parts, (layer_out, grads, grad_core))
    ex.tick(
        moves([u_c], z2) + moves([u_a, *a_parts], y) + moves([d_c, u_b, o, *b_parts], "x") + moves([d_a, d_b], z1)
    )
    ex.tick(moves([u_a, u_b, *head_parts], z1) + moves([d_c, u_c, o], y) + moves([d_a, d_b], z2))
    grads = ex.before(head_parts, grads)
    grad_blocks = ex.after(d_parts + u_parts + head_parts, [grads[0], grad_core, swap_seq(grads[2], 2)])
    late = u_parts + head_parts
    if zs[2:]:
        ex.tick(moves([u_a, u_b, o, *head_parts], z2) + moves([u_c], "x"))
        for z in zs[2:]:
            ex.tick(moves(d_parts + late, z))
        down_piece = ex.tick([], d_parts)
    else:
        down_piece = ex.tick(moves([u_a, u_b, o, *head_parts], z2) + moves([u_c], "x"), d_parts)
    d_kinds = (tuple((sum(sizes[:at]), sizes[at], sum(sizes[:at]), 0) for at in range(3) if sizes[at]),)
    grad_tokens = place(where_at, forward(grad_blocks), part, False)[0]
    grad_tokens, down_pieces = ex.after(late, (grad_tokens, gather(down_piece)[0]))
    late_piece = ex.tick([], late)
    down_pieces, late_piece = together(down_pieces, late_piece)
    out_w_down = final(last_bits, down_pieces, d_kinds, [shape((2 * down, width), f32)])[0]
    late_pieces, out_w_down = gather(late_piece, out_w_down)
    wide = [shape((2 * rows, feed_width), f32)] + [shape((2 * rows, width), f32)] * 4 + [shape((width // row_count,), f32)] * 8
    wide += [shape((feed_width // row_count,), f32)]
    at_q = 5 * rows
    at_k = at_q + rows
    at_lines = at_k + third
    at_rest = at_lines + 16
    kinds = (
        tuple((at * rows, rows, 0, at * half) for at in range(4)),
        ((4 * rows, rows, 0, 0),),
        ((at_q, rows, 0, 0),),
        ((at_k, third, 0, 0), (at_rest, rows - third, third, 0)),
        ((at_rest + rows - third, rows, 0, 0),),
        *[((at_lines, 16, at, None),) for at in (*range(8), 16)],
    )
    out_w_up, out_w_out, out_w_query, out_w_key, out_w_value, *rest = final(last_bits, late_pieces, kinds, wide)
    return (
        layer_out, pooled, grad_tokens,
        out_w_query, out_w_key, out_w_value, rest[0], rest[1], out_w_out, rest[4], rest[2], rest[3],
        out_w_up, rest[8], out_w_down, rest[7], rest[5], rest[6],
    )


def solution(mesh):
    split = P("rows", "seq", None)
    in_specs = (split, P("rows", "seq"), *[P()] * 15, split, P("rows", None, None))
    mat, line = P("rows", None), P("rows")
    out_specs = (
        split, P("rows", None, None), split,
        mat, mat, mat, line, line, mat, line, line, line, mat, line, mat, line, line, line,
    )
    body = functools.partial(local, mesh.shape["rows"])
    return jax.shard_map(body, mesh=mesh, in_specs=in_specs, out_specs=out_specs, check_vma=False)
```

```python
import functools

import jax
import jax.numpy as jnp
from jax import lax
from jax.experimental import pallas as pl
from jax.experimental.pallas import tpu as pltpu
from jax.sharding import PartitionSpec as P

HEADS = 12
SEGS = 8
FEED_TILE = 1024
PIECES = 4
COST = 0.001
LATE = 4000.0
D_SPLIT = (4, 4, 4)
BYTES = 1.0
norm_eps = 1e-12
pool_eps = 1e-06
bf16 = jnp.bfloat16
f32 = jnp.float32
MIB = 2**20


def shape(dims, dtype=bf16):
    return jax.ShapeDtypeStruct(dims, dtype)


def dot(left, right, left_dim=1, right_dim=0):
    return lax.dot_general(
        left, right, (((left_dim,), (right_dim,)), ((), ())), preferred_element_type=f32
    )


def in_vmem(kernel, name, mib, outs, args, work, scratch=(), scalars=0, fetch=(), far_in=(), near=(), free=(), far_own=()):
    args, outs, fetch = list(args), list(outs), dict(fetch)
    in_specs = [pl.BlockSpec(memory_space=pltpu.VMEM)] * len(args)
    for at in range(scalars):
        in_specs[at] = pl.BlockSpec(memory_space=pltpu.SMEM)
    for at in [*fetch, *far_in]:
        in_specs[at] = pl.BlockSpec(memory_space=pltpu.HBM)
        args[at] = pltpu.with_memory_space_constraint(args[at], pltpu.HBM)
    out_specs = [pl.BlockSpec(memory_space=pltpu.VMEM)] * len(outs)
    far_out = [at for at in range(len(outs)) if at not in near and at not in free and at not in far_own]
    held_in = [pltpu.VMEM(args[at].shape, args[at].dtype) for at in fetch]
    held_out = [pltpu.VMEM(outs[at].shape, outs[at].dtype) for at in far_out]
    size = sum(v.size * v.dtype.itemsize for v in (*args, *outs))
    for at in [*far_out, *far_own]:
        out_specs[at] = pl.BlockSpec(memory_space=pltpu.HBM)
        outs[at] = pltpu.HBM(outs[at].shape, outs[at].dtype)
    pieces = [(at, dim, count, piece) for at, (dim, count) in fetch.items() for piece in range(count)]
    pieces.sort(key=lambda piece: piece[3])
    count_in, count_out = len(args), len(outs)

    def body(*refs):
        ins, results = list(refs[:count_in]), list(refs[count_in : count_in + count_out])
        rest = list(refs[count_in + count_out :])
        own = [rest.pop(0) for _ in scratch]
        buffers = dict(zip(fetch, [rest.pop(0) for _ in held_in]))
        staged = dict(zip(far_out, [rest.pop(0) for _ in held_out]))
        sems_in = rest.pop(0) if pieces else None
        sems_out = rest.pop(0) if far_out else None
        copies = {at: [] for at in fetch}
        for number, (at, dim, count, piece) in enumerate(pieces):
            length = args[at].shape[dim] // count
            where = [slice(None)] * args[at].ndim
            where[dim] = pl.ds(piece * length, length)
            where = tuple(where)
            copy = pltpu.make_async_copy(ins[at].at[where], buffers[at].at[where], sems_in.at[number])
            copy.start()
            copies[at].append(copy)
        for at in fetch:
            ins[at] = Fetched(buffers[at], copies[at])
        sent = {}

        def flush(*numbers):
            for at in numbers:
                sent[at] = pltpu.make_async_copy(staged[at], results[at], sems_out.at[far_out.index(at)])
                sent[at].start()

        kernel(*ins, *[staged.get(at, results[at]) for at in range(count_out)], *own, flush=flush)
        flush(*[at for at in far_out if at not in sent])
        for copy in sent.values():
            copy.wait()
        for one in ins:
            if isinstance(one, Fetched):
                one.finish()

    sems = [pltpu.SemaphoreType.DMA((count,)) for count in (len(pieces), len(far_out)) if count]
    return pl.pallas_call(
        body,
        in_specs=in_specs,
        out_specs=out_specs,
        out_shape=outs,
        scratch_shapes=[*scratch, *held_in, *held_out, *sems],
        compiler_params=pltpu.CompilerParams(vmem_limit_bytes=mib * MIB),
        cost_estimate=pl.CostEstimate(flops=int(work * COST), bytes_accessed=int(size * BYTES), transcendentals=0),
        name=name,
    )(*args)


class Fetched:
    def __init__(self, ref, copies):
        self.ref, self.copies, self.waited = ref, copies, set()

    def piece(self, at=0):
        if at not in self.waited:
            self.waited.add(at)
            self.copies[at].wait()
        return self.ref

    def finish(self):
        for at in range(len(self.copies)):
            self.piece(at)

    def __getitem__(self, where):
        self.finish()
        return self.ref[where]

    @property
    def shape(self):
        return self.ref.shape


def load_kernel(*refs, flush):
    count = (len(refs) - 1) // 2
    copies = [pltpu.make_async_copy(refs[at], refs[count + at], refs[-1].at[at]) for at in range(count)]
    for copy in copies:
        copy.start()
    for copy in copies:
        copy.wait()


def load(*arrays):
    outs = [shape(v.shape, v.dtype) for v in arrays]
    every = range(len(arrays))
    scratch = [pltpu.SemaphoreType.DMA((len(arrays),))]
    return in_vmem(load_kernel, "load_weights", 4, outs, arrays, 1e9, scratch, far_in=every, near=every)


def split_two(value):
    high = value.astype(bf16)
    return high, (value - high.astype(f32)).astype(bf16)


def attend_kernel(
    t0, t1, t2, t3, wq, wk, wv, bq, bv,
    exp_out, total_out, row_out, q_out, k_out, v_out, mix_t, mixed_out, mixed_far, row_near, ids_out,
    mask, stage, sems,
    *, flush,
):
    blocks = (t0, t1, t2, t3)
    part = t0.shape[0] - 16
    length, width = row_out.shape
    for at, block in enumerate(blocks):
        row_out[at * part : (at + 1) * part, :] = block[:part, :]
    rows = row_out[...]
    row_near[...] = rows
    q_out[...] = (dot(rows, wq[...]) + bq[...]).astype(bf16) * bf16(0.125)
    k_out[...] = dot(rows, wk[...]).astype(bf16)
    v_out[...] = (dot(rows, wv[...]) + bv[...]).astype(bf16)
    flush(2, 3, 4, 5)
    ids = jnp.concatenate([block[part : part + 16, :part].astype(f32)[0:1] for block in blocks], axis=1)
    ids_out[...] = jnp.broadcast_to(ids, ids_out.shape)
    column = jnp.broadcast_to(ids, (128, length)).T[:, 0:1]
    mask[...] = jnp.where(column == ids, 0.0, -1e30)

    sent = []
    for pair in range(width // 128):
        lanes = slice(pair * 128, pair * 128 + 128)
        keys = k_out[:, lanes]
        query_t = q_out[:, lanes].T
        value_t = v_out[:, lanes].T
        for half in range(2):
            at = slice(half * 64, half * 64 + 64)
            head = 2 * pair + half
            scores = dot(keys[:, at], query_t[at, :]) + mask[...]
            expo = jnp.exp(scores - jnp.max(scores, axis=0, keepdims=True))
            inverse = 1.0 / jnp.sum(expo, axis=0, keepdims=True)
            low = expo.astype(bf16)
            stage[head] = low
            sent.append(pltpu.make_async_copy(stage.at[head], exp_out.at[head], sems.at[head]))
            sent[-1].start()
            total_out[head : head + 1, :] = inverse
            mix_t[head * 64 : head * 64 + 64, :] = dot(value_t[at, :], low) * inverse

    flush(1, 6)
    mixed = mix_t[...].astype(bf16).T
    mixed_out[...] = mixed
    mixed_far[...] = mixed
    for copy in sent:
        copy.wait()


def attend(blocks, wq, wk, wv, bq, bv):
    part, width = blocks[0].shape
    length = (part - 16) * 4
    heads = width // 64
    flat = shape((length, width))
    outs = [
        shape((heads, length, length)), shape((16, length), f32), flat, flat, flat, flat, shape((width, length), f32),
        flat, flat, flat, shape((8, length), f32),
    ]
    args = (*blocks, wq, wk, wv, bq, bv)
    scratch = [
        pltpu.VMEM((length, length), f32),
        pltpu.VMEM((heads, length, length), bf16),
        pltpu.SemaphoreType.DMA((heads,)),
    ]
    fetch = {at: (0, 1) for at in range(1, 4)}
    return in_vmem(
        attend_kernel, "attend_forward", 20, outs, args, 10e9 * LATE, scratch, fetch=fetch, near=(7, 9, 10), far_own=(0,)
    )


def gelu_both(v):
    phi = 0.5 + 0.5 * lax.erf(v * 0.7071067811865476)
    bell = jnp.exp2(v * (v * (-0.5 * 1.4426950408889634)))
    return v * phi, phi + (v * 0.3989422804014327) * bell


def pool_windows(width):
    return (width, width * 2 // 3, width // 3, width // 6, width // 12)


def pool_places(width):
    w = pool_windows(width)
    return ((0, 0), (8, 0), (8, w[1]), (16, 0), (16, w[3]))


def feed_kernel(
    core, mixed, w_up, b_up, w_down, row, gain_a, shift_a, b_down, gain, shift, c0, c1, c2, c3, ids, pool_cot, bo, wo,
    low_far, act_out, l0, l1, l2, keep_out, sums_out,
    keep_u, send_u, b_up_out, hidden_one, mixed_out, sums_one,
    acc, unit_s, rstd_s, slope_out, low_out, up_s, down_s, cot_s, out_s, normal, rstd_a, sems,
    *, flush,
):
    length, width = mixed.shape
    part = length // 4
    hidden_width = w_up.shape[1]
    tile = FEED_TILE
    early, ups, downs = [], [], []
    numbers = iter(range(3 * PIECES + 4))
    for piece in range(PIECES):
        rows = slice(piece * (width // PIECES), (piece + 1) * (width // PIECES))
        early.append(pltpu.make_async_copy(wo.at[rows, :], out_s.at[rows, :], sems.at[next(numbers)]))
        ups.append(pltpu.make_async_copy(w_up.at[rows, :], up_s.at[rows, :], sems.at[next(numbers)]))
        rows = slice(piece * (hidden_width // PIECES), (piece + 1) * (hidden_width // PIECES))
        downs.append(pltpu.make_async_copy(w_down.at[rows, :], down_s.at[rows, :], sems.at[next(numbers)]))
    late = [
        pltpu.make_async_copy(source, cot_s.at[number], sems.at[next(numbers)])
        for number, source in enumerate((c0, c1, c2, c3))
    ]
    for copy in early + ups:
        copy.start()
    for copy in early:
        copy.wait()
    for copy in downs + late:
        copy.start()
    acc[...] = dot(mixed[...], out_s[...])
    for at in range(0, length, 32):
        rows = slice(at, at + 32)
        hidden = row[rows, :].astype(f32) + (acc[rows, :] + bo[...])
        centered = hidden - jnp.mean(hidden, axis=-1, keepdims=True)
        rstd = lax.rsqrt(jnp.mean(centered * centered, axis=-1, keepdims=True) + norm_eps)
        unit = centered * rstd
        normal[rows, :] = unit
        rstd_a[rows, :] = jnp.broadcast_to(rstd, (32, 128))
        low_far[rows, :] = (unit * gain_a[...] + shift_a[...]).astype(bf16)
    flush(0)
    for copy in ups:
        copy.wait()
    for at in range(0, hidden_width, tile):
        cols = slice(at, at + tile)
        up = dot(low_far[...], up_s[:, cols]) + b_up[:, cols]
        active, slope = gelu_both(up)
        active_low = active.astype(bf16)
        act_out[:, cols] = active_low
        slope_out[:, cols] = slope.astype(bf16)
        if at == 0:
            for copy in downs:
                copy.wait()
        down = dot(active_low, down_s[cols, :])
        if at == 0:
            acc[...] = down
        else:
            acc[...] += down

    groups = lax.broadcasted_iota(jnp.int32, (16, length), 0).astype(f32)
    member = jnp.where((groups == ids[0:1, :]) & (groups < SEGS), 1.0, 0.0).astype(bf16)
    outs = (l0, l1, l2.at[0], l2.at[1])
    seg_sums = jnp.zeros((16, width), f32)
    for at in range(4):
        rows = slice(at * part, (at + 1) * part)
        hidden = normal[rows, :] * gain_a[...] + shift_a[...] + (acc[rows, :] + b_down[...])
        centered = hidden - jnp.mean(hidden, axis=-1, keepdims=True)
        rstd = lax.rsqrt(jnp.mean(centered * centered, axis=-1, keepdims=True) + norm_eps)
        unit = centered * rstd
        unit_s[rows, :] = unit
        rstd_s[rows, :] = jnp.broadcast_to(rstd, (part, 128))
        result = unit * gain[...] + shift[...]
        outs[at][0:part, :] = result.astype(bf16)
        for piece in split_two(result):
            seg_sums += dot(member[:, rows], piece)
    seg_sums = seg_sums[:SEGS]
    first_lane = 0
    total = jnp.zeros((SEGS, width), f32)
    pooled = []
    for window in pool_windows(width):
        sums = seg_sums[:, :window]
        cot = pool_cot[:, first_lane : first_lane + window]
        factor = lax.rsqrt(jnp.mean(sums * sums, axis=-1, keepdims=True) + pool_eps)
        pooled.append(sums * factor)
        inner = jnp.sum(cot * sums, axis=-1, keepdims=True) * (factor * factor * factor / window)
        piece = cot * factor - sums * inner
        if window < width:
            piece = jnp.concatenate([piece, jnp.zeros((SEGS, width - window), f32)], axis=1)
        total += piece
        first_lane += window
    zeros = jnp.zeros((8, width), f32)
    rest = jnp.zeros((8, width - pooled[3].shape[1] - pooled[4].shape[1]), f32)
    upper = jnp.concatenate([pooled[0], jnp.concatenate(pooled[1:3], axis=1)], axis=0).astype(bf16)
    lower = jnp.concatenate([jnp.concatenate([pooled[3], pooled[4], rest], axis=1), zeros], axis=0).astype(bf16)
    for out in outs:
        out[part : part + 16, :] = upper
        out[part + 16 : part + 32, :] = lower
    flush(2, 3, 4)
    total = split_two(jnp.concatenate([total, zeros], axis=0))
    half = width // 2
    first = core[0] == 0
    sums = [jnp.zeros((1, width), f32)] * 3
    for copy in late:
        copy.wait()
    for at in range(4):
        rows = slice(at * part, (at + 1) * part)
        grad = cot_s[at].astype(f32) + sum(dot(member[:, rows], piece, 0, 0) for piece in total)
        unit = unit_s[rows, :]
        scaled = grad * gain[...]
        hidden_grad = rstd_s[rows, 0:1] * (
            scaled
            - jnp.mean(scaled, axis=-1, keepdims=True)
            - unit * jnp.mean(scaled * unit, axis=-1, keepdims=True)
        )
        acc[rows, :] = hidden_grad
        rounded = hidden_grad.astype(bf16)
        low_out[rows, :] = rounded
        keep_out[rows, :] = jnp.where(first, rounded[:, :half], rounded[:, half:])
        act_out[rows, hidden_width:] = jnp.where(first, rounded[:, half:], rounded[:, :half])
        for to, value in enumerate((grad * unit, grad, rounded.astype(f32))):
            sums[to] += jnp.sum(value, axis=0, keepdims=True)
    sums_out[...] = jnp.concatenate([*sums, jnp.zeros((5, width), f32)], axis=0)

    half_feed = hidden_width // 2
    for at, out in enumerate((send_u, keep_u)):
        which = core[0] if at == 1 else 1 - core[0]
        cols = pl.ds(pl.multiple_of(which * half_feed, 128), half_feed)
        grad_up = (dot(low_out[...], down_s[cols, :], 1, 1) * slope_out[:, cols].astype(f32)).astype(bf16)
        out[:, :half_feed] = grad_up
        b_up_out[:, cols] = jnp.broadcast_to(jnp.sum(grad_up.astype(f32), axis=0, keepdims=True), (8, half_feed))
        if at == 0:
            flush(1, 5, 6)
        back = dot(grad_up, up_s[:, cols], 1, 1)
        acc[...] += back

    sums = [jnp.zeros((1, width), f32)] * 3
    for at in range(0, length, 64):
        rows = slice(at, at + 64)
        grad = acc[rows, :]
        unit = normal[rows, :]
        scaled = grad * gain_a[...]
        hidden_grad = rstd_a[rows, 0:1] * (
            scaled
            - jnp.mean(scaled, axis=-1, keepdims=True)
            - unit * jnp.mean(scaled * unit, axis=-1, keepdims=True)
        )
        hidden_one[rows, :] = hidden_grad
        rounded = hidden_grad.astype(bf16)
        low_out[rows, :] = rounded
        keep_u[rows, half_feed:] = jnp.where(first, rounded[:, :half], rounded[:, half:])
        send_u[rows, half_feed:] = jnp.where(first, rounded[:, half:], rounded[:, :half])
        for to, value in enumerate((grad * unit, grad, rounded.astype(f32))):
            sums[to] += jnp.sum(value, axis=0, keepdims=True)
    flush(8, 7, 9, 10)
    mixed_out[...] = dot(low_out[...], out_s[...], 1, 1).astype(bf16)
    sums_one[...] = jnp.concatenate([*sums, jnp.zeros((5, width), f32)], axis=0)


def feed(core, mixed, w_up, b_up, w_down, row, gain_a, shift_a, b_down, gain, shift, cots, ids, pool_cot, bo, wo):
    length, width = mixed.shape
    hidden = w_up.shape[1]
    half = shape((length, width // 2))
    wide = shape((length, width), f32)
    part = length // 4 + 32
    outs = [
        shape((length, width)), shape((length, hidden + width // 2)), shape((part, width)), shape((part, width)), shape((2, part, width)),
        half, shape((8, width), f32), shape((length, hidden // 2 + width // 2)), shape((length, hidden // 2 + width // 2)),
        shape((8, hidden), f32), wide, shape((length, width)), shape((8, width), f32),
    ]
    scratch = [
        pltpu.VMEM((length, width), f32),
        pltpu.VMEM((length, width), f32),
        pltpu.VMEM((length, 128), f32),
        pltpu.VMEM((length, hidden), bf16),
        pltpu.VMEM((length, width), bf16),
        pltpu.VMEM(w_up.shape, bf16),
        pltpu.VMEM(w_down.shape, bf16),
        pltpu.VMEM((4, length // 4, width), bf16),
        pltpu.VMEM((width, width), bf16),
        pltpu.VMEM((length, width), f32),
        pltpu.VMEM((length, 128), f32),
        pltpu.SemaphoreType.DMA((3 * PIECES + 4,)),
    ]
    args = (core, mixed, w_up, b_up, w_down, row, gain_a, shift_a, b_down, gain, shift, *cots, ids, pool_cot, bo, wo)
    return in_vmem(
        feed_kernel, "feed_both", 37, outs, args, 18e9 * LATE, scratch, 1, far_in=(2, 4, 11, 12, 13, 14, 18)
    )


def attend_back_kernel(
    core, expo, total, q, k, v, mix_t, grad_mixed, keep_out, send_out, sums_out,
    held, q_s, k_s, v_s, mix_s, grad_s, sems,
    *, flush,
):
    length = expo.shape[1]
    pairs = q.shape[1] // 128
    per = pairs // 2
    slots = held.shape[0]

    def copies(at):
        which = core[0] if at >= per else 1 - core[0]
        pair = which * per + at % per
        lanes = pl.ds(pl.multiple_of(pair * 128, 128), 128)
        slot = at % slots
        sources = [
            (q.at[:, lanes], q_s), (k.at[:, lanes], k_s), (v.at[:, lanes], v_s),
            (mix_t.at[lanes, :], mix_s), (grad_mixed.at[:, lanes], grad_s),
            (expo.at[pl.ds(2 * pair, 2)], held),
        ]
        return [
            pltpu.make_async_copy(source, to.at[slot], sems.at[slot, number])
            for number, (source, to) in enumerate(sources)
        ]

    def start(group):
        for at in group:
            for copy in copies(at):
                copy.start()

    groups = [range(0, 1), range(1, per), range(per, pairs)]
    start(groups[0])
    start(groups[1])
    for at in range(pairs):
        for number, group in enumerate(groups):
            if at == group[0]:
                for member in group:
                    for copy in copies(member):
                        copy.wait()
                if number == 0:
                    start(groups[2])
        which = core[0] if at >= per else 1 - core[0]
        out = keep_out if at >= per else send_out
        pair, slot = at % per, at % slots
        lanes = pl.ds(pl.multiple_of(which * (per * 128) + pair * 128, 128), 128)
        grad_t = grad_s[slot].T.astype(f32)
        query, value, mix = q_s[slot], v_s[slot], mix_s[slot]
        key_t = k_s[slot].T
        halves = []
        inner = []
        for half in range(2):
            rows = slice(half * 64, half * 64 + 64)
            inverse = total[pl.ds(which * pairs + 2 * pair + half, 1), :]
            scaled = (grad_t[rows] * inverse).astype(bf16)
            halves.append(scaled)
            inner.append(jnp.sum(scaled.astype(f32) * mix[rows], axis=0, keepdims=True))
        scaled_rows = jnp.concatenate(halves, axis=0).T
        grads_q, grads_k, grads_v = [], [], []
        for half in range(2):
            rows = slice(half * 64, half * 64 + 64)
            probs = held[slot, half]
            grad_probs = dot(value[:, rows], halves[half])
            grad_scores = (probs.astype(f32) * (grad_probs - inner[half])).astype(bf16)
            grads_v.append(dot(probs, scaled_rows[:, rows]))
            grads_k.append(dot(grad_scores, query[:, rows]))
            grads_q.append(dot(key_t[rows, :], grad_scores))
        here = slice(pair * 128, pair * 128 + 128)
        grad_query = (jnp.concatenate(grads_q, axis=0).T * 0.125).astype(bf16)
        grad_value = jnp.concatenate(grads_v, axis=1).astype(bf16)
        out[0, :, here] = grad_query
        out[1, :, here] = jnp.concatenate(grads_k, axis=1).astype(bf16)
        out[2, :, here] = grad_value
        sums_out[:, lanes] = jnp.concatenate(
            [
                jnp.sum(grad_query.astype(f32), axis=0, keepdims=True),
                jnp.sum(grad_value.astype(f32), axis=0, keepdims=True),
                jnp.zeros((6, 128), f32),
            ],
            axis=0,
        )


def attend_back(core, expo, total, q, k, v, mix_t, grad_mixed):
    length, width = q.shape
    outs = [shape((3, length, width // 2)), shape((3, length, width // 2)), shape((8, width), f32)]
    args = (core, expo, total, q, k, v, mix_t, grad_mixed)
    slots = width // 128
    scratch = [
        pltpu.VMEM((slots, 2, length, length), bf16),
        *[pltpu.VMEM((slots, length, 128), bf16)] * 3,
        pltpu.VMEM((slots, 128, length), f32),
        pltpu.VMEM((slots, length, 128), bf16),
        pltpu.SemaphoreType.DMA((slots, 6)),
    ]
    return in_vmem(
        attend_back_kernel, "attend_backward", 20, outs, args, 9e9 * LATE, scratch, 1,
        fetch={2: (0, 1)}, far_in=(1, 3, 4, 5, 6, 7), free=(0, 1, 2),
    )


def add_input_grad(core, hidden, keep, send, wq, wk, wv, o0, o1, o2):
    width = hidden.shape[1]
    half = width // 2
    part = o0.shape[0]
    mine = pl.ds(pl.multiple_of(core[0] * half, 128), half)
    other = pl.ds(pl.multiple_of((1 - core[0]) * half, 128), half)
    total = hidden[...]
    for at, weight in enumerate((wq, wk, wv)):
        total += dot(keep[at], weight[:, mine], 1, 1) + dot(send[at], weight[:, other], 1, 1)
    total = total.astype(bf16)
    for at, out in enumerate((o0, o1, o2.at[0], o2.at[1])):
        out[...] = total[at * part : (at + 1) * part]


def down_weight_kernel(own, other, keep, out, *, flush):
    size = out.shape[0] // 4
    for at in range(4):
        rows = slice(at * size, (at + 1) * size)
        left, right = own[:, rows], other[:, rows]
        out[rows, :] = (dot(left, keep[...], 0, 0) + dot(right, other[:, 4 * size :], 0, 0)).astype(bf16)


def down_weight(own, other, keep):
    half = keep.shape[1]
    outs = [shape((own.shape[1] - half, half))]
    return in_vmem(down_weight_kernel, "down_weight", 14, outs, (own, other, keep), 4e9 * LATE, free=(0,))[0]


def weights_kernel(
    core, low, low_other, mixed, mixed_other, row, row_other, keep_u, got_u, keep_h, send_h, got_h, hidden, wq, wk, wv,
    b_up, sums_head, sums_one, sums_two,
    out_u, out_o, out_h, vec, g0, g1, g2,
    *, flush,
):
    half = out_o.shape[1]
    tiles = out_u.shape[0]
    for at in range(tiles):
        cols = slice(at * half, (at + 1) * half)
        out_u[at] = (dot(low[...], keep_u[:, cols], 0, 0) + dot(low_other[...], got_u[:, cols], 0, 0)).astype(bf16)
    cols = slice(tiles * half, (tiles + 1) * half)
    out_o[...] = (dot(mixed[...], keep_u[:, cols], 0, 0) + dot(mixed_other[...], got_u[:, cols], 0, 0)).astype(bf16)
    for at in range(3):
        out_h[at] = (dot(row[...], keep_h[at], 0, 0) + dot(row_other[...], got_h[at], 0, 0)).astype(bf16)
    add_input_grad(core, hidden, keep_h, send_h, wq, wk, wv, g0, g1, g2)
    shards = vec.shape[0]
    lines = jnp.concatenate([sums_head[0:2], sums_one[0:3], sums_two[0:3]], axis=0)
    line = lines.shape[1] // shards
    up = b_up.shape[1] // shards
    first = lax.broadcasted_iota(jnp.int32, (8, up), 0) == 0
    for at in range(shards):
        piece = lines[:, at * line : (at + 1) * line]
        if line < half:
            piece = jnp.concatenate([piece, jnp.zeros((8, half - line), f32)], axis=1)
        vec[at, 0] = jnp.concatenate([piece, jnp.zeros((8, half), f32)], axis=0).astype(bf16)
        piece = jnp.where(first, b_up[:, at * up : (at + 1) * up], 0.0)
        if up < half:
            piece = jnp.concatenate([piece, jnp.zeros((8, half - up), f32)], axis=1)
        vec[at, 1] = jnp.concatenate([piece, jnp.zeros((8, half), f32)], axis=0).astype(bf16)


def weights(shards, *args):
    low, keep_u = args[1], args[7]
    length, width = low.shape
    half = width // 2
    part = length // 4
    outs = [
        shape((keep_u.shape[1] // half - 1, width, half)), shape((width, half)), shape((3, width, half)),
        shape((shards, 2, 16, half)), shape((part, width)), shape((part, width)), shape((2, part, width)),
    ]
    every = range(len(outs))
    return in_vmem(weights_kernel, "other_weights", 14, outs, args, 11e9 * LATE, scalars=1, free=every)


def pack_kernel(seq_at, tokens, *rest, flush):
    ids, outs, sems = (rest[0], rest[1:5], rest[5]) if len(rest) == 6 else (None, rest[:4], rest[4])
    part, width = tokens.shape[1:]
    copies = []
    for at in (2, 3, 1, 0):
        copies.append(pltpu.make_async_copy(tokens.at[seq_at[0] ^ at], outs[at].at[:part, :], sems.at[at]))
        copies[-1].start()
    if ids is not None:
        for at, out in enumerate(outs):
            line = ids[pl.ds(seq_at[0] ^ at, 1), :].astype(f32)
            line = jnp.concatenate([line, jnp.zeros((1, width - part), f32)], axis=1)
            out[part : part + 16, :] = jnp.broadcast_to(line, (16, width)).astype(bf16)
    for copy in copies:
        copy.wait()


def pack(seq_at, tokens, ids=None):
    _, part, width = tokens.shape
    extra = 0 if ids is None else 16
    args = (seq_at, tokens) if ids is None else (seq_at, tokens, ids)
    outs = [shape((part + extra, width))] * 4
    fetch = {} if ids is None else {2: (0, 1)}
    scratch = [pltpu.SemaphoreType.DMA((4,))]
    return in_vmem(
        pack_kernel, "pack_rows", 6, outs, args, 1e8, scratch, 1, fetch=fetch, far_in=(1,), near=(0, 1, 2, 3)
    )


def place_kernel(seq_at, b0, b1, b2, b3, out, *pooled, flush):
    part, width = out.shape[1:]
    for at, block in enumerate((b0, b1, b2, b3)):
        to = seq_at[0] ^ at
        rows = block.piece()[0] if at == 2 else block[...]
        out[to] = rows[:part, :]
        if pooled:
            first = 0
            rows = rows[part : part + 32, :].astype(f32)
            for window, (row, lane) in zip(pool_windows(width), pool_places(width)):
                pooled[0][to, :, first : first + window] = rows[row : row + 8, lane : lane + window]
                first += window


def place(seq_at, blocks, part, pooled):
    width = blocks[0].shape[1]
    outs = [shape((4, part, width))]
    if pooled:
        outs.append(shape((4, SEGS, sum(pool_windows(width))), f32))
    fetch = {at: (0, 1) for at in range(1, 5)}
    return in_vmem(place_kernel, "place_rows", 6, outs, (seq_at, *blocks), 1e8, scalars=1, fetch=fetch)


def swap_seq(value, mask):
    return lax.ppermute(value, "seq", [(at, at ^ mask) for at in range(4)])


def exchange(own, core_block, chip_blocks):
    got_core = swap_seq(core_block, 1)
    got_chip = swap_seq(chip_blocks, 2)
    return [own, got_core, got_chip]


def forward(blocks):
    return [*blocks, swap_seq(blocks[2][1], 1)]


class Part:
    def __init__(self, blocks, names, first, rows):
        self.blocks, self.names, self.first, self.rows, self.got = blocks, names, first, rows, None


class Exchanges:
    def __init__(self, row_at, seq_at, row_count):
        self.row_count = row_count
        self.axes = ["x"] + [1 << at for at in range(row_count.bit_length() - 1)]
        self.bits = jnp.stack([(seq_at >> 1) & 1] + [(row_at // axis) & 1 for axis in self.axes[1:]])

    def part(self, blocks, first=0, rows=None):
        names = [("tile", blocks.shape[0])] + [(axis, 2) for axis in reversed(self.axes[1:])] + [("x", 2)]
        rows = blocks.shape[3] if rows is None else rows
        return Part(blocks.reshape(-1, *blocks.shape[3:]), names, first, rows)

    def swap(self, value, axis):
        if axis == "x":
            return swap_seq(value, 2)
        return lax.ppermute(value, "rows", [(at, at ^ axis) for at in range(self.row_count)])

    def tick(self, moves, settle=(), far=False):
        parts = [part for part, _ in moves] + list(settle)
        ins = []
        for part in parts:
            for value in (part.blocks, part.got and part.got[0]):
                if value is not None and not any(value is other for other in ins):
                    ins.append(value)
        find = lambda value: [value is other for other in ins].index(True)
        lanes = parts[0].blocks.shape[2]
        used = list(dict.fromkeys(axis for _, axis in moves))
        outs, plan, rows_of, kept = [], [], dict.fromkeys([*used, None], 0), []
        for part, axis in [*moves, *[(part, None) for part in settle]]:
            count = part.blocks.shape[0]
            source = (find(part.blocks), part.first, part.rows, part.got and (find(part.got[0]), part.got[1]))
            if axis is None:
                plan.append((source, axis, [(at, None) for at in range(count)], rows_of[axis], None))
                rows_of[axis] += count * part.rows
                continue
            names = [name for name, _ in part.names]
            low = 1
            for _, size in part.names[names.index(axis) + 1 :]:
                low *= size
            pairs = [(at, at + low) for at in range(count) if (at // low) % 2 == 0]
            plan.append((source, axis, pairs, rows_of[axis], len(kept)))
            kept.append(shape((count // 2, part.rows, lanes)))
            part.got = (axis, rows_of[axis])
            rows_of[axis] += len(pairs) * part.rows
            part.names = [entry for entry in part.names if entry[0] != axis]
        flat = [*used, *([None] if settle else [])]
        outs = [shape((rows_of[axis], lanes)) for axis in flat] + kept

        def kernel(bits, *refs, flush):
            given, sends, keeps = refs[: len(ins)], refs[len(ins) : len(ins) + len(flat)], refs[len(ins) + len(flat) :]
            for (blocks, first, rows, got), axis, pairs, row, keep in plan:
                send = sends[flat.index(axis)]

                def value(at):
                    block = given[blocks][at, first : first + rows, :]
                    if got is None:
                        return block
                    other = given[got[0]][got[1] + at * rows : got[1] + (at + 1) * rows, :]
                    return (block.astype(f32) + other.astype(f32)).astype(bf16)

                for number, (zero, one) in enumerate(pairs):
                    where = slice(row + number * rows, row + (number + 1) * rows)
                    if axis is None:
                        send[where, :] = value(zero)
                        continue
                    bit = bits[self.axes.index(axis)] == 0
                    left, right = value(zero), value(one)
                    send[where, :] = jnp.where(bit, right, left)
                    keeps[keep][number] = jnp.where(bit, left, right)

        every = range(len(flat) if far else 0, len(outs))
        results = in_vmem(kernel, "halves", 10, outs, (self.bits, *ins), 1e8, scalars=1, free=every)
        arrived = {axis: self.swap(results[flat.index(axis)], axis) for axis in used}
        for (part, axis), blocks in zip(moves, results[len(flat) :]):
            part.blocks, part.first = blocks, 0
            part.got = (arrived[axis], part.got[1])
        return results[len(used)] if settle else None

    def before(self, parts, value):
        blocks = [part.blocks for part in parts]
        value, blocks = lax.optimization_barrier((value, blocks))
        for part, new in zip(parts, blocks):
            part.blocks = new
        return value

    def after(self, parts, value):
        found = []
        for part in parts:
            if not any(part.got[0] is other for other in found):
                found.append(part.got[0])
        value, new = lax.optimization_barrier((value, found))
        for part in parts:
            at = [part.got[0] is other for other in found].index(True)
            part.got = (new[at], part.got[1])
        return value


def sides(bits, piece, got_x, got_c, got_xc):
    mine = [jnp.where(bits[0] == 0, piece, got_x), jnp.where(bits[0] == 0, got_x, piece)]
    other = [jnp.where(bits[0] == 0, got_c, got_xc), jnp.where(bits[0] == 0, got_xc, got_c)]
    left = [jnp.where(bits[1] == 0, a, b) for a, b in zip(mine, other)]
    right = [jnp.where(bits[1] == 0, b, a) for a, b in zip(mine, other)]
    return left, right


def final_kernel(kinds, bits, *refs, flush):
    own, outs = refs[:4], refs[4:]
    half = own[0].shape[1]
    for number, (pieces, out) in enumerate(zip(kinds, outs)):
        for at, rows, to_row, to_lane in pieces:
            left, right = sides(bits, *[ref[at : at + rows, :].astype(f32) for ref in own])
            if to_lane is None:
                line = (left[to_row // 16] + right[to_row // 16])[to_row % 16, : out.shape[0]]
                out[...] = line
                continue
            for x in range(2):
                first = x * (out.shape[0] // 2) + to_row
                out[first : first + rows, to_lane : to_lane + half] = left[x]
                right_lane = out.shape[1] // 2 + to_lane
                out[first : first + rows, right_lane : right_lane + half] = right[x]
        flush(number)


def gather(piece, meanwhile=None):
    got_x = swap_seq(piece, 2)
    if meanwhile is not None:
        got_x, meanwhile = lax.optimization_barrier((got_x, meanwhile))
    return (piece, got_x, swap_seq(piece, 1), swap_seq(got_x, 1)), meanwhile


def final(bits, pieces, kinds, outs):
    kernel = functools.partial(final_kernel, kinds)
    return in_vmem(kernel, "final_rows", 12, outs, (bits, *pieces), 1e8, scalars=1)


def together(*values):
    return lax.optimization_barrier(values)


def local(
    row_count,
    tokens, segment_ids, w_query, w_key, w_value, b_query, b_value, w_out, b_out, gain_attn, shift_attn,
    w_up, b_up, w_down, b_down, gain_out, shift_out, token_cot, pool_cot,
):
    part, width = tokens.shape[1:]
    feed_width = w_up.shape[1]
    half = width // 2
    seq_at = lax.axis_index("seq")
    row_at = lax.axis_index("rows")
    core = (seq_at & 1).reshape(1)
    where_at = seq_at.reshape(1)
    ex = Exchanges(row_at, seq_at, row_count)
    last_bits = jnp.stack([(seq_at >> 1) & 1, seq_at & 1])
    y, zs = ex.axes[1], ex.axes[2:]
    z1, z2 = zs[0], zs[1]

    def vec(v):
        return v.reshape(1, -1)

    own = pack(where_at, tokens, segment_ids)
    token_cot, own, near = together(token_cot, own, (w_query, w_key, w_value))
    swapped = {mask: swap_seq(own[mask], mask) for mask in (2, 3, 1)}
    blocks = [own[0]] + [swapped[mask] for mask in (1, 2, 3)]
    near_query, near_key, near_value = load(*near)
    own = pack(where_at, token_cot)
    own, blocks[1], near_query, near_key, near_value = together(own, blocks[1], near_query, near_key, near_value)
    swapped = {mask: swap_seq(own[mask], mask) for mask in (2, 3, 1)}
    cots = [own[0]] + [swapped[mask] for mask in (1, 2, 3)]
    row_pool_cot = lax.dynamic_index_in_dim(pool_cot, seq_at, 0, keepdims=False)

    expo, total, row, q, k, v, mix_t, mixed_near, mixed, row_near, ids_row = attend(
        blocks, near_query, near_key, near_value, vec(b_query), vec(b_value)
    )
    low_far, act, l0, l1, l2, keep_d, sums_two, keep_u, send_u, b_up_sum, hidden_one, grad_mixed, sums_one = feed(
        core, mixed_near, w_up, vec(b_up), w_down, row_near, vec(gain_attn), vec(shift_attn), vec(b_down),
        vec(gain_out), vec(shift_out), cots, ids_row, row_pool_cot, vec(b_out), w_out,
    )
    row_other, mixed_other, low_other = swap_seq(row, 1), swap_seq(mixed, 1), swap_seq(low_far, 1)
    act_other, got_u = swap_seq(act, 1), swap_seq(send_u, 1)
    layer_blocks = exchange(l0, l1, l2)

    def cut(value):
        return value.reshape(-1, row_count, 2, value.shape[-2] // row_count // 2, half)

    row_other, mixed_other, grad_mixed = together(row_other, mixed_other, grad_mixed)
    keep_h, send_h, sums_head = attend_back(core, expo, total, q, k, v, mix_t, grad_mixed)
    act_other, got_u, layer_blocks[1], keep_d, send_h = together(act_other, got_u, layer_blocks[1], keep_d, send_h)
    got_h = swap_seq(send_h, 1)
    grad_w_down = cut(down_weight(act, act_other, keep_d))
    layer_blocks, got_h, low_other, grad_w_down = together(layer_blocks, got_h, low_other, grad_w_down)
    down = grad_w_down.shape[3]
    sizes = [down * at // 12 for at in D_SPLIT]
    d_a, d_b, d_c = (ex.part(grad_w_down, sum(sizes[:at]), sizes[at]) for at in range(3))
    d_parts = [d_a, d_b, d_c]
    ex.tick([(d_c, z1), (d_b, y), (d_a, "x")])
    keep_u = ex.before(d_parts, keep_u)
    grad_w_up, grad_w_out, head, lines, *grads = weights(
        row_count, core, low_far, low_other, mixed, mixed_other, row, row_other, keep_u, got_u, keep_h, send_h, got_h,
        hidden_one, w_query, w_key, w_value, b_up_sum, sums_head, sums_one, sums_two,
    )
    grad_w_up, grad_w_out, head = cut(grad_w_up), cut(grad_w_out), cut(head)
    rows = grad_w_up.shape[3]
    u_a, u_b, u_c, o = ex.part(grad_w_up[:1]), ex.part(grad_w_up[1:2]), ex.part(grad_w_up[2:]), ex.part(grad_w_out)
    u_parts = [u_a, u_b, u_c, o]
    third = rows // 3
    q_part, k_first, k_rest = ex.part(head[0:1]), ex.part(head[1:2], 0, third), ex.part(head[1:2], third, rows - third)
    v_part, line_part = ex.part(head[2:3]), ex.part(lines[None])
    a_parts, b_parts = [q_part, k_first, line_part], [k_rest, v_part]
    head_parts = a_parts + b_parts

    def moves(parts, axis):
        return [(part, axis) for part in parts]

    ex.tick(
        moves([d_b, u_a, *a_parts], "x") + moves([d_a, u_b, *b_parts], y) + moves([u_c, o], z1) + moves([d_c], z2)
    )
    every_part = d_parts + u_parts + head_parts
    layer_blocks = forward(ex.before(head_parts, layer_blocks))
    layer_out, pooled = place(where_at, layer_blocks, part, True)
    layer_out, grads = ex.after(every_part, (layer_out, grads))
    ex.tick(
        moves([u_c], z2) + moves([u_a, *a_parts], y) + moves([d_c, u_b, o, *b_parts], "x") + moves([d_a, d_b], z1)
    )
    grads, grad_core = ex.after(every_part, (grads, swap_seq(grads[1], 1)))
    ex.tick(moves([u_a, u_b, *head_parts], z1) + moves([d_c, u_c, o], y) + moves([d_a, d_b], z2))
    grads = ex.before(head_parts, grads)
    grad_blocks = ex.after(d_parts + u_parts + head_parts, [grads[0], grad_core, swap_seq(grads[2], 2)])
    late = u_parts + head_parts
    if zs[2:]:
        ex.tick(moves([u_a, u_b, o, *head_parts], z2) + moves([u_c], "x"))
        for z in zs[2:]:
            ex.tick(moves(d_parts + late, z))
        down_piece = ex.tick([], d_parts)
    else:
        down_piece = ex.tick(moves([u_a, u_b, o, *head_parts], z2) + moves([u_c], "x"), d_parts)
    d_kinds = (tuple((sum(sizes[:at]), sizes[at], sum(sizes[:at]), 0) for at in range(3) if sizes[at]),)
    grad_tokens = place(where_at, forward(grad_blocks), part, False)[0]
    grad_tokens, down_pieces = ex.after(late, (grad_tokens, gather(down_piece)[0]))
    late_piece = ex.tick([], late)
    down_pieces, late_piece = together(down_pieces, late_piece)
    out_w_down = final(last_bits, down_pieces, d_kinds, [shape((2 * down, width), f32)])[0]
    late_pieces, out_w_down = gather(late_piece, out_w_down)
    wide = [shape((2 * rows, feed_width), f32)] + [shape((2 * rows, width), f32)] * 4 + [shape((width // row_count,), f32)] * 8
    wide += [shape((feed_width // row_count,), f32)]
    at_q = 5 * rows
    at_k = at_q + rows
    at_lines = at_k + third
    at_rest = at_lines + 16
    kinds = (
        tuple((at * rows, rows, 0, at * half) for at in range(4)),
        ((4 * rows, rows, 0, 0),),
        ((at_q, rows, 0, 0),),
        ((at_k, third, 0, 0), (at_rest, rows - third, third, 0)),
        ((at_rest + rows - third, rows, 0, 0),),
        *[((at_lines, 16, at, None),) for at in (*range(8), 16)],
    )
    out_w_up, out_w_out, out_w_query, out_w_key, out_w_value, *rest = final(last_bits, late_pieces, kinds, wide)
    return (
        layer_out, pooled, grad_tokens,
        out_w_query, out_w_key, out_w_value, rest[0], rest[1], out_w_out, rest[4], rest[2], rest[3],
        out_w_up, rest[8], out_w_down, rest[7], rest[5], rest[6],
    )


def solution(mesh):
    split = P("rows", "seq", None)
    in_specs = (split, P("rows", "seq"), *[P()] * 15, split, P("rows", None, None))
    mat, line = P("rows", None), P("rows")
    out_specs = (
        split, P("rows", None, None), split,
        mat, mat, mat, line, line, mat, line, line, line, mat, line, mat, line, line, line,
    )
    body = functools.partial(local, mesh.shape["rows"])
    return jax.shard_map(body, mesh=mesh, in_specs=in_specs, out_specs=out_specs, check_vma=False)
```

```python
import functools

import jax
import jax.numpy as jnp
from jax import lax
from jax.experimental import pallas as pl
from jax.experimental.pallas import tpu as pltpu
from jax.sharding import PartitionSpec as P

HEADS = 12
SEGS = 8
FEED_TILE = 1024
PIECES = 3
COST = 0.001
LATE = 8000.0
D_SPLIT = (4, 4, 4)
BYTES = 1.0
norm_eps = 1e-12
pool_eps = 1e-06
bf16 = jnp.bfloat16
f32 = jnp.float32
MIB = 2**20


def shape(dims, dtype=bf16):
    return jax.ShapeDtypeStruct(dims, dtype)


def dot(left, right, left_dim=1, right_dim=0):
    return lax.dot_general(
        left, right, (((left_dim,), (right_dim,)), ((), ())), preferred_element_type=f32
    )


def in_vmem(kernel, name, mib, outs, args, work, scratch=(), scalars=0, fetch=(), far_in=(), near=(), free=(), far_own=()):
    args, outs, fetch = list(args), list(outs), dict(fetch)
    in_specs = [pl.BlockSpec(memory_space=pltpu.VMEM)] * len(args)
    for at in range(scalars):
        in_specs[at] = pl.BlockSpec(memory_space=pltpu.SMEM)
    for at in [*fetch, *far_in]:
        in_specs[at] = pl.BlockSpec(memory_space=pltpu.HBM)
        args[at] = pltpu.with_memory_space_constraint(args[at], pltpu.HBM)
    out_specs = [pl.BlockSpec(memory_space=pltpu.VMEM)] * len(outs)
    far_out = [at for at in range(len(outs)) if at not in near and at not in free and at not in far_own]
    held_in = [pltpu.VMEM(args[at].shape, args[at].dtype) for at in fetch]
    held_out = [pltpu.VMEM(outs[at].shape, outs[at].dtype) for at in far_out]
    size = sum(v.size * v.dtype.itemsize for v in (*args, *outs))
    for at in [*far_out, *far_own]:
        out_specs[at] = pl.BlockSpec(memory_space=pltpu.HBM)
        outs[at] = pltpu.HBM(outs[at].shape, outs[at].dtype)
    pieces = [(at, dim, count, piece) for at, (dim, count) in fetch.items() for piece in range(count)]
    pieces.sort(key=lambda piece: piece[3])
    count_in, count_out = len(args), len(outs)

    def body(*refs):
        ins, results = list(refs[:count_in]), list(refs[count_in : count_in + count_out])
        rest = list(refs[count_in + count_out :])
        own = [rest.pop(0) for _ in scratch]
        buffers = dict(zip(fetch, [rest.pop(0) for _ in held_in]))
        staged = dict(zip(far_out, [rest.pop(0) for _ in held_out]))
        sems_in = rest.pop(0) if pieces else None
        sems_out = rest.pop(0) if far_out else None
        copies = {at: [] for at in fetch}
        for number, (at, dim, count, piece) in enumerate(pieces):
            length = args[at].shape[dim] // count
            where = [slice(None)] * args[at].ndim
            where[dim] = pl.ds(piece * length, length)
            where = tuple(where)
            copy = pltpu.make_async_copy(ins[at].at[where], buffers[at].at[where], sems_in.at[number])
            copy.start()
            copies[at].append(copy)
        for at in fetch:
            ins[at] = Fetched(buffers[at], copies[at])
        sent = {}

        def flush(*numbers):
            for at in numbers:
                sent[at] = pltpu.make_async_copy(staged[at], results[at], sems_out.at[far_out.index(at)])
                sent[at].start()

        kernel(*ins, *[staged.get(at, results[at]) for at in range(count_out)], *own, flush=flush)
        flush(*[at for at in far_out if at not in sent])
        for copy in sent.values():
            copy.wait()
        for one in ins:
            if isinstance(one, Fetched):
                one.finish()

    sems = [pltpu.SemaphoreType.DMA((count,)) for count in (len(pieces), len(far_out)) if count]
    return pl.pallas_call(
        body,
        in_specs=in_specs,
        out_specs=out_specs,
        out_shape=outs,
        scratch_shapes=[*scratch, *held_in, *held_out, *sems],
        compiler_params=pltpu.CompilerParams(vmem_limit_bytes=mib * MIB),
        cost_estimate=pl.CostEstimate(flops=int(work * COST), bytes_accessed=int(size * BYTES), transcendentals=0),
        name=name,
    )(*args)


class Fetched:
    def __init__(self, ref, copies):
        self.ref, self.copies, self.waited = ref, copies, set()

    def piece(self, at=0):
        if at not in self.waited:
            self.waited.add(at)
            self.copies[at].wait()
        return self.ref

    def finish(self):
        for at in range(len(self.copies)):
            self.piece(at)

    def __getitem__(self, where):
        self.finish()
        return self.ref[where]

    @property
    def shape(self):
        return self.ref.shape


def load_kernel(*refs, flush):
    count = (len(refs) - 1) // 2
    copies = [pltpu.make_async_copy(refs[at], refs[count + at], refs[-1].at[at]) for at in range(count)]
    for copy in copies:
        copy.start()
    for copy in copies:
        copy.wait()


def load(*arrays):
    outs = [shape(v.shape, v.dtype) for v in arrays]
    every = range(len(arrays))
    scratch = [pltpu.SemaphoreType.DMA((len(arrays),))]
    return in_vmem(load_kernel, "load_weights", 4, outs, arrays, 1e9, scratch, far_in=every, near=every)


def split_two(value):
    high = value.astype(bf16)
    return high, (value - high.astype(f32)).astype(bf16)


def attend_kernel(
    t0, t1, t2, t3, wq, wk, wv, bq, bv,
    exp_out, total_out, row_out, q_out, k_out, v_out, mix_t, mixed_out, mixed_far, row_near, ids_out,
    mask, stage, sems,
    *, flush,
):
    blocks = (t0, t1, t2, t3)
    part = t0.shape[0] - 16
    length, width = row_out.shape
    for at, block in enumerate(blocks):
        row_out[at * part : (at + 1) * part, :] = block[:part, :]
    rows = row_out[...]
    row_near[...] = rows
    q_out[...] = (dot(rows, wq[...]) + bq[...]).astype(bf16) * bf16(0.125)
    k_out[...] = dot(rows, wk[...]).astype(bf16)
    v_out[...] = (dot(rows, wv[...]) + bv[...]).astype(bf16)
    flush(2, 3, 4, 5)
    ids = jnp.concatenate([block[part : part + 16, :part].astype(f32)[0:1] for block in blocks], axis=1)
    ids_out[...] = jnp.broadcast_to(ids, ids_out.shape)
    column = jnp.broadcast_to(ids, (128, length)).T[:, 0:1]
    mask[...] = jnp.where(column == ids, 0.0, -1e30)

    sent = []
    for pair in range(width // 128):
        lanes = slice(pair * 128, pair * 128 + 128)
        keys = k_out[:, lanes]
        query_t = q_out[:, lanes].T
        value_t = v_out[:, lanes].T
        for half in range(2):
            at = slice(half * 64, half * 64 + 64)
            head = 2 * pair + half
            scores = dot(keys[:, at], query_t[at, :]) + mask[...]
            expo = jnp.exp(scores - jnp.max(scores, axis=0, keepdims=True))
            inverse = 1.0 / jnp.sum(expo, axis=0, keepdims=True)
            low = expo.astype(bf16)
            stage[head] = low
            sent.append(pltpu.make_async_copy(stage.at[head], exp_out.at[head], sems.at[head]))
            sent[-1].start()
            total_out[head : head + 1, :] = inverse
            mix_t[head * 64 : head * 64 + 64, :] = dot(value_t[at, :], low) * inverse

    flush(1, 6)
    mixed = mix_t[...].astype(bf16).T
    mixed_out[...] = mixed
    mixed_far[...] = mixed
    for copy in sent:
        copy.wait()


def attend(blocks, wq, wk, wv, bq, bv):
    part, width = blocks[0].shape
    length = (part - 16) * 4
    heads = width // 64
    flat = shape((length, width))
    outs = [
        shape((heads, length, length)), shape((16, length), f32), flat, flat, flat, flat, shape((width, length), f32),
        flat, flat, flat, shape((8, length), f32),
    ]
    args = (*blocks, wq, wk, wv, bq, bv)
    scratch = [
        pltpu.VMEM((length, length), f32),
        pltpu.VMEM((heads, length, length), bf16),
        pltpu.SemaphoreType.DMA((heads,)),
    ]
    fetch = {at: (0, 1) for at in range(1, 4)}
    return in_vmem(
        attend_kernel, "attend_forward", 20, outs, args, 10e9 * LATE, scratch, fetch=fetch, near=(7, 9, 10), far_own=(0,)
    )


def gelu_both(v):
    phi = 0.5 + 0.5 * lax.erf(v * 0.7071067811865476)
    bell = jnp.exp2(v * (v * (-0.5 * 1.4426950408889634)))
    return v * phi, phi + (v * 0.3989422804014327) * bell


def pool_windows(width):
    return (width, width * 2 // 3, width // 3, width // 6, width // 12)


def pool_places(width):
    w = pool_windows(width)
    return ((0, 0), (8, 0), (8, w[1]), (16, 0), (16, w[3]))


def feed_kernel(
    core, mixed, w_up, b_up, w_down, row, gain_a, shift_a, b_down, gain, shift, c0, c1, c2, c3, ids, pool_cot, bo, wo,
    low_far, act_out, l0, l1, l2, keep_out, sums_out,
    keep_u, send_u, b_up_out, hidden_one, mixed_out, sums_one,
    acc, unit_s, rstd_s, slope_out, low_out, up_s, down_s, cot_s, out_s, normal, rstd_a, sems,
    *, flush,
):
    length, width = mixed.shape
    part = length // 4
    hidden_width = w_up.shape[1]
    tile = FEED_TILE
    early, ups, downs = [], [], []
    numbers = iter(range(3 * PIECES + 4))
    for piece in range(PIECES):
        rows = slice(piece * (width // PIECES), (piece + 1) * (width // PIECES))
        early.append(pltpu.make_async_copy(wo.at[rows, :], out_s.at[rows, :], sems.at[next(numbers)]))
        ups.append(pltpu.make_async_copy(w_up.at[rows, :], up_s.at[rows, :], sems.at[next(numbers)]))
        rows = slice(piece * (hidden_width // PIECES), (piece + 1) * (hidden_width // PIECES))
        downs.append(pltpu.make_async_copy(w_down.at[rows, :], down_s.at[rows, :], sems.at[next(numbers)]))
    late = [
        pltpu.make_async_copy(source, cot_s.at[number], sems.at[next(numbers)])
        for number, source in enumerate((c0, c1, c2, c3))
    ]
    for copy in early + ups:
        copy.start()
    for copy in early:
        copy.wait()
    for copy in downs + late:
        copy.start()
    acc[...] = dot(mixed[...], out_s[...])
    for at in range(0, length, 32):
        rows = slice(at, at + 32)
        hidden = row[rows, :].astype(f32) + (acc[rows, :] + bo[...])
        centered = hidden - jnp.mean(hidden, axis=-1, keepdims=True)
        rstd = lax.rsqrt(jnp.mean(centered * centered, axis=-1, keepdims=True) + norm_eps)
        unit = centered * rstd
        normal[rows, :] = unit
        rstd_a[rows, :] = jnp.broadcast_to(rstd, (32, 128))
        low_far[rows, :] = (unit * gain_a[...] + shift_a[...]).astype(bf16)
    flush(0)
    for copy in ups:
        copy.wait()
    for at in range(0, hidden_width, tile):
        cols = slice(at, at + tile)
        up = dot(low_far[...], up_s[:, cols]) + b_up[:, cols]
        active, slope = gelu_both(up)
        active_low = active.astype(bf16)
        act_out[:, cols] = active_low
        slope_out[:, cols] = slope.astype(bf16)
        if at == 0:
            for copy in downs:
                copy.wait()
        down = dot(active_low, down_s[cols, :])
        if at == 0:
            acc[...] = down
        else:
            acc[...] += down

    groups = lax.broadcasted_iota(jnp.int32, (16, length), 0).astype(f32)
    member = jnp.where((groups == ids[0:1, :]) & (groups < SEGS), 1.0, 0.0).astype(bf16)
    outs = (l0, l1, l2.at[0], l2.at[1])
    seg_sums = jnp.zeros((16, width), f32)
    for at in range(4):
        rows = slice(at * part, (at + 1) * part)
        hidden = normal[rows, :] * gain_a[...] + shift_a[...] + (acc[rows, :] + b_down[...])
        centered = hidden - jnp.mean(hidden, axis=-1, keepdims=True)
        rstd = lax.rsqrt(jnp.mean(centered * centered, axis=-1, keepdims=True) + norm_eps)
        unit = centered * rstd
        unit_s[rows, :] = unit
        rstd_s[rows, :] = jnp.broadcast_to(rstd, (part, 128))
        result = unit * gain[...] + shift[...]
        outs[at][0:part, :] = result.astype(bf16)
        for piece in split_two(result):
            seg_sums += dot(member[:, rows], piece)
    seg_sums = seg_sums[:SEGS]
    first_lane = 0
    total = jnp.zeros((SEGS, width), f32)
    pooled = []
    for window in pool_windows(width):
        sums = seg_sums[:, :window]
        cot = pool_cot[:, first_lane : first_lane + window]
        factor = lax.rsqrt(jnp.mean(sums * sums, axis=-1, keepdims=True) + pool_eps)
        pooled.append(sums * factor)
        inner = jnp.sum(cot * sums, axis=-1, keepdims=True) * (factor * factor * factor / window)
        piece = cot * factor - sums * inner
        if window < width:
            piece = jnp.concatenate([piece, jnp.zeros((SEGS, width - window), f32)], axis=1)
        total += piece
        first_lane += window
    zeros = jnp.zeros((8, width), f32)
    rest = jnp.zeros((8, width - pooled[3].shape[1] - pooled[4].shape[1]), f32)
    upper = jnp.concatenate([pooled[0], jnp.concatenate(pooled[1:3], axis=1)], axis=0).astype(bf16)
    lower = jnp.concatenate([jnp.concatenate([pooled[3], pooled[4], rest], axis=1), zeros], axis=0).astype(bf16)
    for out in outs:
        out[part : part + 16, :] = upper
        out[part + 16 : part + 32, :] = lower
    flush(2, 3, 4)
    total = split_two(jnp.concatenate([total, zeros], axis=0))
    half = width // 2
    first = core[0] == 0
    sums = [jnp.zeros((1, width), f32)] * 3
    for copy in late:
        copy.wait()
    for at in range(4):
        rows = slice(at * part, (at + 1) * part)
        grad = cot_s[at].astype(f32) + sum(dot(member[:, rows], piece, 0, 0) for piece in total)
        unit = unit_s[rows, :]
        scaled = grad * gain[...]
        hidden_grad = rstd_s[rows, 0:1] * (
            scaled
            - jnp.mean(scaled, axis=-1, keepdims=True)
            - unit * jnp.mean(scaled * unit, axis=-1, keepdims=True)
        )
        acc[rows, :] = hidden_grad
        rounded = hidden_grad.astype(bf16)
        low_out[rows, :] = rounded
        keep_out[rows, :] = jnp.where(first, rounded[:, :half], rounded[:, half:])
        act_out[rows, hidden_width:] = jnp.where(first, rounded[:, half:], rounded[:, :half])
        for to, value in enumerate((grad * unit, grad, rounded.astype(f32))):
            sums[to] += jnp.sum(value, axis=0, keepdims=True)
    sums_out[...] = jnp.concatenate([*sums, jnp.zeros((5, width), f32)], axis=0)

    half_feed = hidden_width // 2
    for at, out in enumerate((send_u, keep_u)):
        which = core[0] if at == 1 else 1 - core[0]
        cols = pl.ds(pl.multiple_of(which * half_feed, 128), half_feed)
        grad_up = (dot(low_out[...], down_s[cols, :], 1, 1) * slope_out[:, cols].astype(f32)).astype(bf16)
        out[:, :half_feed] = grad_up
        b_up_out[:, cols] = jnp.broadcast_to(jnp.sum(grad_up.astype(f32), axis=0, keepdims=True), (8, half_feed))
        if at == 0:
            flush(1, 5, 6)
        back = dot(grad_up, up_s[:, cols], 1, 1)
        acc[...] += back

    sums = [jnp.zeros((1, width), f32)] * 3
    for at in range(0, length, 64):
        rows = slice(at, at + 64)
        grad = acc[rows, :]
        unit = normal[rows, :]
        scaled = grad * gain_a[...]
        hidden_grad = rstd_a[rows, 0:1] * (
            scaled
            - jnp.mean(scaled, axis=-1, keepdims=True)
            - unit * jnp.mean(scaled * unit, axis=-1, keepdims=True)
        )
        hidden_one[rows, :] = hidden_grad
        rounded = hidden_grad.astype(bf16)
        low_out[rows, :] = rounded
        keep_u[rows, half_feed:] = jnp.where(first, rounded[:, :half], rounded[:, half:])
        send_u[rows, half_feed:] = jnp.where(first, rounded[:, half:], rounded[:, :half])
        for to, value in enumerate((grad * unit, grad, rounded.astype(f32))):
            sums[to] += jnp.sum(value, axis=0, keepdims=True)
    flush(8, 7, 9, 10)
    mixed_out[...] = dot(low_out[...], out_s[...], 1, 1).astype(bf16)
    sums_one[...] = jnp.concatenate([*sums, jnp.zeros((5, width), f32)], axis=0)


def feed(core, mixed, w_up, b_up, w_down, row, gain_a, shift_a, b_down, gain, shift, cots, ids, pool_cot, bo, wo):
    length, width = mixed.shape
    hidden = w_up.shape[1]
    half = shape((length, width // 2))
    wide = shape((length, width), f32)
    part = length // 4 + 32
    outs = [
        shape((length, width)), shape((length, hidden + width // 2)), shape((part, width)), shape((part, width)), shape((2, part, width)),
        half, shape((8, width), f32), shape((length, hidden // 2 + width // 2)), shape((length, hidden // 2 + width // 2)),
        shape((8, hidden), f32), wide, shape((length, width)), shape((8, width), f32),
    ]
    scratch = [
        pltpu.VMEM((length, width), f32),
        pltpu.VMEM((length, width), f32),
        pltpu.VMEM((length, 128), f32),
        pltpu.VMEM((length, hidden), bf16),
        pltpu.VMEM((length, width), bf16),
        pltpu.VMEM(w_up.shape, bf16),
        pltpu.VMEM(w_down.shape, bf16),
        pltpu.VMEM((4, length // 4, width), bf16),
        pltpu.VMEM((width, width), bf16),
        pltpu.VMEM((length, width), f32),
        pltpu.VMEM((length, 128), f32),
        pltpu.SemaphoreType.DMA((3 * PIECES + 4,)),
    ]
    args = (core, mixed, w_up, b_up, w_down, row, gain_a, shift_a, b_down, gain, shift, *cots, ids, pool_cot, bo, wo)
    return in_vmem(
        feed_kernel, "feed_both", 37, outs, args, 18e9 * LATE, scratch, 1, far_in=(2, 4, 11, 12, 13, 14, 18)
    )


def attend_back_kernel(
    core, expo, total, q, k, v, mix_t, grad_mixed, keep_out, send_out, sums_out,
    held, q_s, k_s, v_s, mix_s, grad_s, sems,
    *, flush,
):
    length = expo.shape[1]
    pairs = q.shape[1] // 128
    per = pairs // 2
    slots = held.shape[0]

    def copies(at):
        which = core[0] if at >= per else 1 - core[0]
        pair = which * per + at % per
        lanes = pl.ds(pl.multiple_of(pair * 128, 128), 128)
        slot = at % slots
        sources = [
            (q.at[:, lanes], q_s), (k.at[:, lanes], k_s), (v.at[:, lanes], v_s),
            (mix_t.at[lanes, :], mix_s), (grad_mixed.at[:, lanes], grad_s),
            (expo.at[pl.ds(2 * pair, 2)], held),
        ]
        return [
            pltpu.make_async_copy(source, to.at[slot], sems.at[slot, number])
            for number, (source, to) in enumerate(sources)
        ]

    def start(group):
        for at in group:
            for copy in copies(at):
                copy.start()

    groups = [range(0, 1), range(1, per), range(per, pairs)]
    start(groups[0])
    start(groups[1])
    for at in range(pairs):
        for number, group in enumerate(groups):
            if at == group[0]:
                for member in group:
                    for copy in copies(member):
                        copy.wait()
                if number == 0:
                    start(groups[2])
        which = core[0] if at >= per else 1 - core[0]
        out = keep_out if at >= per else send_out
        pair, slot = at % per, at % slots
        lanes = pl.ds(pl.multiple_of(which * (per * 128) + pair * 128, 128), 128)
        grad_t = grad_s[slot].T.astype(f32)
        query, value, mix = q_s[slot], v_s[slot], mix_s[slot]
        key_t = k_s[slot].T
        halves = []
        inner = []
        for half in range(2):
            rows = slice(half * 64, half * 64 + 64)
            inverse = total[pl.ds(which * pairs + 2 * pair + half, 1), :]
            scaled = (grad_t[rows] * inverse).astype(bf16)
            halves.append(scaled)
            inner.append(jnp.sum(scaled.astype(f32) * mix[rows], axis=0, keepdims=True))
        scaled_rows = jnp.concatenate(halves, axis=0).T
        grads_q, grads_k, grads_v = [], [], []
        for half in range(2):
            rows = slice(half * 64, half * 64 + 64)
            probs = held[slot, half]
            grad_probs = dot(value[:, rows], halves[half])
            grad_scores = (probs.astype(f32) * (grad_probs - inner[half])).astype(bf16)
            grads_v.append(dot(probs, scaled_rows[:, rows]))
            grads_k.append(dot(grad_scores, query[:, rows]))
            grads_q.append(dot(key_t[rows, :], grad_scores))
        here = slice(pair * 128, pair * 128 + 128)
        grad_query = (jnp.concatenate(grads_q, axis=0).T * 0.125).astype(bf16)
        grad_value = jnp.concatenate(grads_v, axis=1).astype(bf16)
        out[0, :, here] = grad_query
        out[1, :, here] = jnp.concatenate(grads_k, axis=1).astype(bf16)
        out[2, :, here] = grad_value
        sums_out[:, lanes] = jnp.concatenate(
            [
                jnp.sum(grad_query.astype(f32), axis=0, keepdims=True),
                jnp.sum(grad_value.astype(f32), axis=0, keepdims=True),
                jnp.zeros((6, 128), f32),
            ],
            axis=0,
        )


def attend_back(core, expo, total, q, k, v, mix_t, grad_mixed):
    length, width = q.shape
    outs = [shape((3, length, width // 2)), shape((3, length, width // 2)), shape((8, width), f32)]
    args = (core, expo, total, q, k, v, mix_t, grad_mixed)
    slots = width // 128
    scratch = [
        pltpu.VMEM((slots, 2, length, length), bf16),
        *[pltpu.VMEM((slots, length, 128), bf16)] * 3,
        pltpu.VMEM((slots, 128, length), f32),
        pltpu.VMEM((slots, length, 128), bf16),
        pltpu.SemaphoreType.DMA((slots, 6)),
    ]
    return in_vmem(
        attend_back_kernel, "attend_backward", 20, outs, args, 9e9 * LATE, scratch, 1,
        fetch={2: (0, 1)}, far_in=(1, 3, 4, 5, 6, 7), free=(0, 1, 2),
    )


def add_input_grad(core, hidden, keep, send, wq, wk, wv, o0, o1, o2):
    width = hidden.shape[1]
    half = width // 2
    part = o0.shape[0]
    mine = pl.ds(pl.multiple_of(core[0] * half, 128), half)
    other = pl.ds(pl.multiple_of((1 - core[0]) * half, 128), half)
    total = hidden[...]
    for at, weight in enumerate((wq, wk, wv)):
        total += dot(keep[at], weight[:, mine], 1, 1) + dot(send[at], weight[:, other], 1, 1)
    total = total.astype(bf16)
    for at, out in enumerate((o0, o1, o2.at[0], o2.at[1])):
        out[...] = total[at * part : (at + 1) * part]


def down_weight_kernel(own, other, keep, out, *, flush):
    size = out.shape[0] // 4
    for at in range(4):
        rows = slice(at * size, (at + 1) * size)
        left, right = own[:, rows], other[:, rows]
        out[rows, :] = (dot(left, keep[...], 0, 0) + dot(right, other[:, 4 * size :], 0, 0)).astype(bf16)


def down_weight(own, other, keep):
    half = keep.shape[1]
    outs = [shape((own.shape[1] - half, half))]
    return in_vmem(down_weight_kernel, "down_weight", 14, outs, (own, other, keep), 4e9 * LATE, free=(0,))[0]


def weights_kernel(
    core, low, low_other, mixed, mixed_other, row, row_other, keep_u, got_u, keep_h, send_h, got_h, hidden, wq, wk, wv,
    b_up, sums_head, sums_one, sums_two,
    out_u, out_o, out_h, vec, g0, g1, g2,
    *, flush,
):
    half = out_o.shape[1]
    tiles = out_u.shape[0]
    for at in range(tiles):
        cols = slice(at * half, (at + 1) * half)
        out_u[at] = (dot(low[...], keep_u[:, cols], 0, 0) + dot(low_other[...], got_u[:, cols], 0, 0)).astype(bf16)
    cols = slice(tiles * half, (tiles + 1) * half)
    out_o[...] = (dot(mixed[...], keep_u[:, cols], 0, 0) + dot(mixed_other[...], got_u[:, cols], 0, 0)).astype(bf16)
    for at in range(3):
        out_h[at] = (dot(row[...], keep_h[at], 0, 0) + dot(row_other[...], got_h[at], 0, 0)).astype(bf16)
    add_input_grad(core, hidden, keep_h, send_h, wq, wk, wv, g0, g1, g2)
    shards = vec.shape[0]
    lines = jnp.concatenate([sums_head[0:2], sums_one[0:3], sums_two[0:3]], axis=0)
    line = lines.shape[1] // shards
    up = b_up.shape[1] // shards
    first = lax.broadcasted_iota(jnp.int32, (8, up), 0) == 0
    for at in range(shards):
        piece = lines[:, at * line : (at + 1) * line]
        if line < half:
            piece = jnp.concatenate([piece, jnp.zeros((8, half - line), f32)], axis=1)
        vec[at, 0] = jnp.concatenate([piece, jnp.zeros((8, half), f32)], axis=0).astype(bf16)
        piece = jnp.where(first, b_up[:, at * up : (at + 1) * up], 0.0)
        if up < half:
            piece = jnp.concatenate([piece, jnp.zeros((8, half - up), f32)], axis=1)
        vec[at, 1] = jnp.concatenate([piece, jnp.zeros((8, half), f32)], axis=0).astype(bf16)


def weights(shards, *args):
    low, keep_u = args[1], args[7]
    length, width = low.shape
    half = width // 2
    part = length // 4
    outs = [
        shape((keep_u.shape[1] // half - 1, width, half)), shape((width, half)), shape((3, width, half)),
        shape((shards, 2, 16, half)), shape((part, width)), shape((part, width)), shape((2, part, width)),
    ]
    every = range(len(outs))
    return in_vmem(weights_kernel, "other_weights", 14, outs, args, 11e9 * LATE, scalars=1, free=every)


def pack_kernel(seq_at, tokens, *rest, flush):
    ids, outs, sems = (rest[0], rest[1:5], rest[5]) if len(rest) == 6 else (None, rest[:4], rest[4])
    part, width = tokens.shape[1:]
    copies = []
    for at in (2, 3, 1, 0):
        copies.append(pltpu.make_async_copy(tokens.at[seq_at[0] ^ at], outs[at].at[:part, :], sems.at[at]))
        copies[-1].start()
    if ids is not None:
        for at, out in enumerate(outs):
            line = ids[pl.ds(seq_at[0] ^ at, 1), :].astype(f32)
            line = jnp.concatenate([line, jnp.zeros((1, width - part), f32)], axis=1)
            out[part : part + 16, :] = jnp.broadcast_to(line, (16, width)).astype(bf16)
    for copy in copies:
        copy.wait()


def pack(seq_at, tokens, ids=None):
    _, part, width = tokens.shape
    extra = 0 if ids is None else 16
    args = (seq_at, tokens) if ids is None else (seq_at, tokens, ids)
    outs = [shape((part + extra, width))] * 4
    fetch = {} if ids is None else {2: (0, 1)}
    scratch = [pltpu.SemaphoreType.DMA((4,))]
    return in_vmem(
        pack_kernel, "pack_rows", 6, outs, args, 1e8, scratch, 1, fetch=fetch, far_in=(1,), near=(0, 1, 2, 3)
    )


def place_kernel(seq_at, b0, b1, b2, b3, out, *pooled, flush):
    part, width = out.shape[1:]
    for at, block in enumerate((b0, b1, b2, b3)):
        to = seq_at[0] ^ at
        rows = block.piece()[0] if at == 2 else block[...]
        out[to] = rows[:part, :]
        if pooled:
            first = 0
            rows = rows[part : part + 32, :].astype(f32)
            for window, (row, lane) in zip(pool_windows(width), pool_places(width)):
                pooled[0][to, :, first : first + window] = rows[row : row + 8, lane : lane + window]
                first += window


def place(seq_at, blocks, part, pooled):
    width = blocks[0].shape[1]
    outs = [shape((4, part, width))]
    if pooled:
        outs.append(shape((4, SEGS, sum(pool_windows(width))), f32))
    fetch = {at: (0, 1) for at in range(1, 5)}
    return in_vmem(place_kernel, "place_rows", 6, outs, (seq_at, *blocks), 1e8, scalars=1, fetch=fetch)


def swap_seq(value, mask):
    return lax.ppermute(value, "seq", [(at, at ^ mask) for at in range(4)])


def exchange(own, core_block, chip_blocks):
    got_core = swap_seq(core_block, 1)
    got_chip = swap_seq(chip_blocks, 2)
    return [own, got_core, got_chip]


def forward(blocks):
    return [*blocks, swap_seq(blocks[2][1], 1)]


class Part:
    def __init__(self, blocks, names, first, rows):
        self.blocks, self.names, self.first, self.rows, self.got = blocks, names, first, rows, None


class Exchanges:
    def __init__(self, row_at, seq_at, row_count):
        self.row_count = row_count
        self.axes = ["x"] + [1 << at for at in range(row_count.bit_length() - 1)]
        self.bits = jnp.stack([(seq_at >> 1) & 1] + [(row_at // axis) & 1 for axis in self.axes[1:]])

    def part(self, blocks, first=0, rows=None):
        names = [("tile", blocks.shape[0])] + [(axis, 2) for axis in reversed(self.axes[1:])] + [("x", 2)]
        rows = blocks.shape[3] if rows is None else rows
        return Part(blocks.reshape(-1, *blocks.shape[3:]), names, first, rows)

    def swap(self, value, axis):
        if axis == "x":
            return swap_seq(value, 2)
        return lax.ppermute(value, "rows", [(at, at ^ axis) for at in range(self.row_count)])

    def tick(self, moves, settle=(), far=False):
        parts = [part for part, _ in moves] + list(settle)
        ins = []
        for part in parts:
            for value in (part.blocks, part.got and part.got[0]):
                if value is not None and not any(value is other for other in ins):
                    ins.append(value)
        find = lambda value: [value is other for other in ins].index(True)
        lanes = parts[0].blocks.shape[2]
        used = list(dict.fromkeys(axis for _, axis in moves))
        outs, plan, rows_of, kept = [], [], dict.fromkeys([*used, None], 0), []
        for part, axis in [*moves, *[(part, None) for part in settle]]:
            count = part.blocks.shape[0]
            source = (find(part.blocks), part.first, part.rows, part.got and (find(part.got[0]), part.got[1]))
            if axis is None:
                plan.append((source, axis, [(at, None) for at in range(count)], rows_of[axis], None))
                rows_of[axis] += count * part.rows
                continue
            names = [name for name, _ in part.names]
            low = 1
            for _, size in part.names[names.index(axis) + 1 :]:
                low *= size
            pairs = [(at, at + low) for at in range(count) if (at // low) % 2 == 0]
            plan.append((source, axis, pairs, rows_of[axis], len(kept)))
            kept.append(shape((count // 2, part.rows, lanes)))
            part.got = (axis, rows_of[axis])
            rows_of[axis] += len(pairs) * part.rows
            part.names = [entry for entry in part.names if entry[0] != axis]
        flat = [*used, *([None] if settle else [])]
        outs = [shape((rows_of[axis], lanes)) for axis in flat] + kept

        def kernel(bits, *refs, flush):
            given, sends, keeps = refs[: len(ins)], refs[len(ins) : len(ins) + len(flat)], refs[len(ins) + len(flat) :]
            for (blocks, first, rows, got), axis, pairs, row, keep in plan:
                send = sends[flat.index(axis)]

                def value(at):
                    block = given[blocks][at, first : first + rows, :]
                    if got is None:
                        return block
                    other = given[got[0]][got[1] + at * rows : got[1] + (at + 1) * rows, :]
                    return (block.astype(f32) + other.astype(f32)).astype(bf16)

                for number, (zero, one) in enumerate(pairs):
                    where = slice(row + number * rows, row + (number + 1) * rows)
                    if axis is None:
                        send[where, :] = value(zero)
                        continue
                    bit = bits[self.axes.index(axis)] == 0
                    left, right = value(zero), value(one)
                    send[where, :] = jnp.where(bit, right, left)
                    keeps[keep][number] = jnp.where(bit, left, right)

        every = range(len(flat) if far else 0, len(outs))
        results = in_vmem(kernel, "halves", 10, outs, (self.bits, *ins), 1e8, scalars=1, free=every)
        arrived = {axis: self.swap(results[flat.index(axis)], axis) for axis in used}
        for (part, axis), blocks in zip(moves, results[len(flat) :]):
            part.blocks, part.first = blocks, 0
            part.got = (arrived[axis], part.got[1])
        return results[len(used)] if settle else None

    def before(self, parts, value):
        blocks = [part.blocks for part in parts]
        value, blocks = lax.optimization_barrier((value, blocks))
        for part, new in zip(parts, blocks):
            part.blocks = new
        return value

    def after(self, parts, value):
        found = []
        for part in parts:
            if not any(part.got[0] is other for other in found):
                found.append(part.got[0])
        value, new = lax.optimization_barrier((value, found))
        for part in parts:
            at = [part.got[0] is other for other in found].index(True)
            part.got = (new[at], part.got[1])
        return value


def sides(bits, piece, got_x, got_c, got_xc):
    mine = [jnp.where(bits[0] == 0, piece, got_x), jnp.where(bits[0] == 0, got_x, piece)]
    other = [jnp.where(bits[0] == 0, got_c, got_xc), jnp.where(bits[0] == 0, got_xc, got_c)]
    left = [jnp.where(bits[1] == 0, a, b) for a, b in zip(mine, other)]
    right = [jnp.where(bits[1] == 0, b, a) for a, b in zip(mine, other)]
    return left, right


def final_kernel(kinds, bits, *refs, flush):
    own, outs = refs[:4], refs[4:]
    half = own[0].shape[1]
    for number, (pieces, out) in enumerate(zip(kinds, outs)):
        for at, rows, to_row, to_lane in pieces:
            left, right = sides(bits, *[ref[at : at + rows, :].astype(f32) for ref in own])
            if to_lane is None:
                line = (left[to_row // 16] + right[to_row // 16])[to_row % 16, : out.shape[0]]
                out[...] = line
                continue
            for x in range(2):
                first = x * (out.shape[0] // 2) + to_row
                out[first : first + rows, to_lane : to_lane + half] = left[x]
                right_lane = out.shape[1] // 2 + to_lane
                out[first : first + rows, right_lane : right_lane + half] = right[x]
        flush(number)


def gather(piece, meanwhile=None):
    got_x = swap_seq(piece, 2)
    if meanwhile is not None:
        got_x, meanwhile = lax.optimization_barrier((got_x, meanwhile))
    return (piece, got_x, swap_seq(piece, 1), swap_seq(got_x, 1)), meanwhile


def final(bits, pieces, kinds, outs):
    kernel = functools.partial(final_kernel, kinds)
    return in_vmem(kernel, "final_rows", 12, outs, (bits, *pieces), 1e8, scalars=1)


def together(*values):
    return lax.optimization_barrier(values)


def local(
    row_count,
    tokens, segment_ids, w_query, w_key, w_value, b_query, b_value, w_out, b_out, gain_attn, shift_attn,
    w_up, b_up, w_down, b_down, gain_out, shift_out, token_cot, pool_cot,
):
    part, width = tokens.shape[1:]
    feed_width = w_up.shape[1]
    half = width // 2
    seq_at = lax.axis_index("seq")
    row_at = lax.axis_index("rows")
    core = (seq_at & 1).reshape(1)
    where_at = seq_at.reshape(1)
    ex = Exchanges(row_at, seq_at, row_count)
    last_bits = jnp.stack([(seq_at >> 1) & 1, seq_at & 1])
    y, zs = ex.axes[1], ex.axes[2:]
    z1, z2 = zs[0], zs[1]

    def vec(v):
        return v.reshape(1, -1)

    own = pack(where_at, tokens, segment_ids)
    token_cot, own, near = together(token_cot, own, (w_query, w_key, w_value))
    swapped = {mask: swap_seq(own[mask], mask) for mask in (2, 3, 1)}
    blocks = [own[0]] + [swapped[mask] for mask in (1, 2, 3)]
    near_query, near_key, near_value = load(*near)
    own = pack(where_at, token_cot)
    own, blocks[1], near_query, near_key, near_value = together(own, blocks[1], near_query, near_key, near_value)
    swapped = {mask: swap_seq(own[mask], mask) for mask in (2, 3, 1)}
    cots = [own[0]] + [swapped[mask] for mask in (1, 2, 3)]
    row_pool_cot = lax.dynamic_index_in_dim(pool_cot, seq_at, 0, keepdims=False)

    expo, total, row, q, k, v, mix_t, mixed_near, mixed, row_near, ids_row = attend(
        blocks, near_query, near_key, near_value, vec(b_query), vec(b_value)
    )
    low_far, act, l0, l1, l2, keep_d, sums_two, keep_u, send_u, b_up_sum, hidden_one, grad_mixed, sums_one = feed(
        core, mixed_near, w_up, vec(b_up), w_down, row_near, vec(gain_attn), vec(shift_attn), vec(b_down),
        vec(gain_out), vec(shift_out), cots, ids_row, row_pool_cot, vec(b_out), w_out,
    )
    row_other, mixed_other, low_other = swap_seq(row, 1), swap_seq(mixed, 1), swap_seq(low_far, 1)
    act_other, got_u = swap_seq(act, 1), swap_seq(send_u, 1)
    layer_blocks = exchange(l0, l1, l2)

    def cut(value):
        return value.reshape(-1, row_count, 2, value.shape[-2] // row_count // 2, half)

    row_other, mixed_other, grad_mixed = together(row_other, mixed_other, grad_mixed)
    keep_h, send_h, sums_head = attend_back(core, expo, total, q, k, v, mix_t, grad_mixed)
    act_other, got_u, layer_blocks[1], keep_d, send_h = together(act_other, got_u, layer_blocks[1], keep_d, send_h)
    got_h = swap_seq(send_h, 1)
    grad_w_down = cut(down_weight(act, act_other, keep_d))
    layer_blocks, got_h, low_other, grad_w_down = together(layer_blocks, got_h, low_other, grad_w_down)
    down = grad_w_down.shape[3]
    sizes = [down * at // 12 for at in D_SPLIT]
    d_a, d_b, d_c = (ex.part(grad_w_down, sum(sizes[:at]), sizes[at]) for at in range(3))
    d_parts = [d_a, d_b, d_c]
    ex.tick([(d_c, z1), (d_b, y), (d_a, "x")])
    keep_u = ex.before(d_parts, keep_u)
    grad_w_up, grad_w_out, head, lines, *grads = weights(
        row_count, core, low_far, low_other, mixed, mixed_other, row, row_other, keep_u, got_u, keep_h, send_h, got_h,
        hidden_one, w_query, w_key, w_value, b_up_sum, sums_head, sums_one, sums_two,
    )
    grad_w_up, grad_w_out, head = cut(grad_w_up), cut(grad_w_out), cut(head)
    rows = grad_w_up.shape[3]
    u_a, u_b, u_c, o = ex.part(grad_w_up[:1]), ex.part(grad_w_up[1:2]), ex.part(grad_w_up[2:]), ex.part(grad_w_out)
    u_parts = [u_a, u_b, u_c, o]
    third = rows // 3
    q_part, k_first, k_rest = ex.part(head[0:1]), ex.part(head[1:2], 0, third), ex.part(head[1:2], third, rows - third)
    v_part, line_part = ex.part(head[2:3]), ex.part(lines[None])
    a_parts, b_parts = [q_part, k_first, line_part], [k_rest, v_part]
    head_parts = a_parts + b_parts

    def moves(parts, axis):
        return [(part, axis) for part in parts]

    ex.tick(
        moves([d_b, u_a, *a_parts], "x") + moves([d_a, u_b, *b_parts], y) + moves([u_c, o], z1) + moves([d_c], z2)
    )
    every_part = d_parts + u_parts + head_parts
    layer_blocks = forward(ex.before(head_parts, layer_blocks))
    layer_out, pooled = place(where_at, layer_blocks, part, True)
    layer_out, grads = ex.after(every_part, (layer_out, grads))
    ex.tick(
        moves([u_c], z2) + moves([u_a, *a_parts], y) + moves([d_c, u_b, o, *b_parts], "x") + moves([d_a, d_b], z1)
    )
    grads, grad_core = ex.after(every_part, (grads, swap_seq(grads[1], 1)))
    ex.tick(moves([u_a, u_b, *head_parts], z1) + moves([d_c, u_c, o], y) + moves([d_a, d_b], z2))
    grads = ex.before(head_parts, grads)
    grad_blocks = ex.after(d_parts + u_parts + head_parts, [grads[0], grad_core, swap_seq(grads[2], 2)])
    late = u_parts + head_parts
    if zs[2:]:
        ex.tick(moves([u_a, u_b, o, *head_parts], z2) + moves([u_c], "x"))
        for z in zs[2:]:
            ex.tick(moves(d_parts + late, z))
        down_piece = ex.tick([], d_parts)
    else:
        down_piece = ex.tick(moves([u_a, u_b, o, *head_parts], z2) + moves([u_c], "x"), d_parts)
    d_kinds = (tuple((sum(sizes[:at]), sizes[at], sum(sizes[:at]), 0) for at in range(3) if sizes[at]),)
    grad_tokens = place(where_at, forward(grad_blocks), part, False)[0]
    grad_tokens, down_pieces = ex.after(late, (grad_tokens, gather(down_piece)[0]))
    late_piece = ex.tick([], late)
    down_pieces, late_piece = together(down_pieces, late_piece)
    out_w_down = final(last_bits, down_pieces, d_kinds, [shape((2 * down, width), f32)])[0]
    late_pieces, out_w_down = gather(late_piece, out_w_down)
    wide = [shape((2 * rows, feed_width), f32)] + [shape((2 * rows, width), f32)] * 4 + [shape((width // row_count,), f32)] * 8
    wide += [shape((feed_width // row_count,), f32)]
    at_q = 5 * rows
    at_k = at_q + rows
    at_lines = at_k + third
    at_rest = at_lines + 16
    kinds = (
        tuple((at * rows, rows, 0, at * half) for at in range(4)),
        ((4 * rows, rows, 0, 0),),
        ((at_q, rows, 0, 0),),
        ((at_k, third, 0, 0), (at_rest, rows - third, third, 0)),
        ((at_rest + rows - third, rows, 0, 0),),
        *[((at_lines, 16, at, None),) for at in (*range(8), 16)],
    )
    out_w_up, out_w_out, out_w_query, out_w_key, out_w_value, *rest = final(last_bits, late_pieces, kinds, wide)
    return (
        layer_out, pooled, grad_tokens,
        out_w_query, out_w_key, out_w_value, rest[0], rest[1], out_w_out, rest[4], rest[2], rest[3],
        out_w_up, rest[8], out_w_down, rest[7], rest[5], rest[6],
    )


def solution(mesh):
    split = P("rows", "seq", None)
    in_specs = (split, P("rows", "seq"), *[P()] * 15, split, P("rows", None, None))
    mat, line = P("rows", None), P("rows")
    out_specs = (
        split, P("rows", None, None), split,
        mat, mat, mat, line, line, mat, line, line, line, mat, line, mat, line, line, line,
    )
    body = functools.partial(local, mesh.shape["rows"])
    return jax.shard_map(body, mesh=mesh, in_specs=in_specs, out_specs=out_specs, check_vma=False)
```

```python
import functools

import jax
import jax.numpy as jnp
from jax import lax
from jax.experimental import pallas as pl
from jax.experimental.pallas import tpu as pltpu
from jax.sharding import PartitionSpec as P

HEADS = 12
SEGS = 8
FEED_TILE = 1024
PIECES = 3
COST = 0.001
LATE = 8000.0
D_SPLIT = (4, 4, 4)
BYTES = 1.0
norm_eps = 1e-12
pool_eps = 1e-06
bf16 = jnp.bfloat16
f32 = jnp.float32
MIB = 2**20


def shape(dims, dtype=bf16):
    return jax.ShapeDtypeStruct(dims, dtype)


def dot(left, right, left_dim=1, right_dim=0):
    return lax.dot_general(
        left, right, (((left_dim,), (right_dim,)), ((), ())), preferred_element_type=f32
    )


def in_vmem(kernel, name, mib, outs, args, work, scratch=(), scalars=0, fetch=(), far_in=(), near=(), free=(), far_own=()):
    args, outs, fetch = list(args), list(outs), dict(fetch)
    in_specs = [pl.BlockSpec(memory_space=pltpu.VMEM)] * len(args)
    for at in range(scalars):
        in_specs[at] = pl.BlockSpec(memory_space=pltpu.SMEM)
    for at in [*fetch, *far_in]:
        in_specs[at] = pl.BlockSpec(memory_space=pltpu.HBM)
        args[at] = pltpu.with_memory_space_constraint(args[at], pltpu.HBM)
    out_specs = [pl.BlockSpec(memory_space=pltpu.VMEM)] * len(outs)
    far_out = [at for at in range(len(outs)) if at not in near and at not in free and at not in far_own]
    held_in = [pltpu.VMEM(args[at].shape, args[at].dtype) for at in fetch]
    held_out = [pltpu.VMEM(outs[at].shape, outs[at].dtype) for at in far_out]
    size = sum(v.size * v.dtype.itemsize for v in (*args, *outs))
    for at in [*far_out, *far_own]:
        out_specs[at] = pl.BlockSpec(memory_space=pltpu.HBM)
        outs[at] = pltpu.HBM(outs[at].shape, outs[at].dtype)
    pieces = [(at, dim, count, piece) for at, (dim, count) in fetch.items() for piece in range(count)]
    pieces.sort(key=lambda piece: piece[3])
    count_in, count_out = len(args), len(outs)

    def body(*refs):
        ins, results = list(refs[:count_in]), list(refs[count_in : count_in + count_out])
        rest = list(refs[count_in + count_out :])
        own = [rest.pop(0) for _ in scratch]
        buffers = dict(zip(fetch, [rest.pop(0) for _ in held_in]))
        staged = dict(zip(far_out, [rest.pop(0) for _ in held_out]))
        sems_in = rest.pop(0) if pieces else None
        sems_out = rest.pop(0) if far_out else None
        copies = {at: [] for at in fetch}
        for number, (at, dim, count, piece) in enumerate(pieces):
            length = args[at].shape[dim] // count
            where = [slice(None)] * args[at].ndim
            where[dim] = pl.ds(piece * length, length)
            where = tuple(where)
            copy = pltpu.make_async_copy(ins[at].at[where], buffers[at].at[where], sems_in.at[number])
            copy.start()
            copies[at].append(copy)
        for at in fetch:
            ins[at] = Fetched(buffers[at], copies[at])
        sent = {}

        def flush(*numbers):
            for at in numbers:
                sent[at] = pltpu.make_async_copy(staged[at], results[at], sems_out.at[far_out.index(at)])
                sent[at].start()

        kernel(*ins, *[staged.get(at, results[at]) for at in range(count_out)], *own, flush=flush)
        flush(*[at for at in far_out if at not in sent])
        for copy in sent.values():
            copy.wait()
        for one in ins:
            if isinstance(one, Fetched):
                one.finish()

    sems = [pltpu.SemaphoreType.DMA((count,)) for count in (len(pieces), len(far_out)) if count]
    return pl.pallas_call(
        body,
        in_specs=in_specs,
        out_specs=out_specs,
        out_shape=outs,
        scratch_shapes=[*scratch, *held_in, *held_out, *sems],
        compiler_params=pltpu.CompilerParams(vmem_limit_bytes=mib * MIB),
        cost_estimate=pl.CostEstimate(flops=int(work * COST), bytes_accessed=int(size * BYTES), transcendentals=0),
        name=name,
    )(*args)


class Fetched:
    def __init__(self, ref, copies):
        self.ref, self.copies, self.waited = ref, copies, set()

    def piece(self, at=0):
        if at not in self.waited:
            self.waited.add(at)
            self.copies[at].wait()
        return self.ref

    def finish(self):
        for at in range(len(self.copies)):
            self.piece(at)

    def __getitem__(self, where):
        self.finish()
        return self.ref[where]

    @property
    def shape(self):
        return self.ref.shape


def load_kernel(*refs, flush):
    count = (len(refs) - 1) // 2
    copies = [pltpu.make_async_copy(refs[at], refs[count + at], refs[-1].at[at]) for at in range(count)]
    for copy in copies:
        copy.start()
    for copy in copies:
        copy.wait()


def load(*arrays):
    outs = [shape(v.shape, v.dtype) for v in arrays]
    every = range(len(arrays))
    scratch = [pltpu.SemaphoreType.DMA((len(arrays),))]
    return in_vmem(load_kernel, "load_weights", 4, outs, arrays, 1e9, scratch, far_in=every, near=every)


def split_two(value):
    high = value.astype(bf16)
    return high, (value - high.astype(f32)).astype(bf16)


def attend_kernel(
    t0, t1, t2, t3, wq, wk, wv, bq, bv,
    exp_out, total_out, row_out, q_out, k_out, v_out, mix_t, mixed_out, mixed_far, row_near, ids_out,
    mask, stage, sems,
    *, flush,
):
    blocks = (t0, t1, t2, t3)
    part = t0.shape[0] - 16
    length, width = row_out.shape
    for at, block in enumerate(blocks):
        row_out[at * part : (at + 1) * part, :] = block[:part, :]
    rows = row_out[...]
    row_near[...] = rows
    q_out[...] = (dot(rows, wq[...]) + bq[...]).astype(bf16) * bf16(0.125)
    k_out[...] = dot(rows, wk[...]).astype(bf16)
    v_out[...] = (dot(rows, wv[...]) + bv[...]).astype(bf16)
    flush(2, 3, 4, 5)
    ids = jnp.concatenate([block[part : part + 16, :part].astype(f32)[0:1] for block in blocks], axis=1)
    ids_out[...] = jnp.broadcast_to(ids, ids_out.shape)
    column = jnp.broadcast_to(ids, (128, length)).T[:, 0:1]
    mask[...] = jnp.where(column == ids, 0.0, -1e30)

    sent = []
    for pair in range(width // 128):
        lanes = slice(pair * 128, pair * 128 + 128)
        keys = k_out[:, lanes]
        query_t = q_out[:, lanes].T
        value_t = v_out[:, lanes].T
        for half in range(2):
            at = slice(half * 64, half * 64 + 64)
            head = 2 * pair + half
            scores = dot(keys[:, at], query_t[at, :]) + mask[...]
            expo = jnp.exp(scores - jnp.max(scores, axis=0, keepdims=True))
            inverse = 1.0 / jnp.sum(expo, axis=0, keepdims=True)
            low = expo.astype(bf16)
            stage[head] = low
            sent.append(pltpu.make_async_copy(stage.at[head], exp_out.at[head], sems.at[head]))
            sent[-1].start()
            total_out[head : head + 1, :] = inverse
            mix_t[head * 64 : head * 64 + 64, :] = dot(value_t[at, :], low) * inverse

    flush(1, 6)
    mixed = mix_t[...].astype(bf16).T
    mixed_out[...] = mixed
    mixed_far[...] = mixed
    for copy in sent:
        copy.wait()


def attend(blocks, wq, wk, wv, bq, bv):
    part, width = blocks[0].shape
    length = (part - 16) * 4
    heads = width // 64
    flat = shape((length, width))
    outs = [
        shape((heads, length, length)), shape((16, length), f32), flat, flat, flat, flat, shape((width, length), f32),
        flat, flat, flat, shape((8, length), f32),
    ]
    args = (*blocks, wq, wk, wv, bq, bv)
    scratch = [
        pltpu.VMEM((length, length), f32),
        pltpu.VMEM((heads, length, length), bf16),
        pltpu.SemaphoreType.DMA((heads,)),
    ]
    fetch = {at: (0, 1) for at in range(1, 4)}
    return in_vmem(
        attend_kernel, "attend_forward", 20, outs, args, 10e9 * LATE, scratch, fetch=fetch, near=(7, 9, 10), far_own=(0,)
    )


def gelu_both(v):
    phi = 0.5 + 0.5 * lax.erf(v * 0.7071067811865476)
    bell = jnp.exp2(v * (v * (-0.5 * 1.4426950408889634)))
    return v * phi, phi + (v * 0.3989422804014327) * bell


def pool_windows(width):
    return (width, width * 2 // 3, width // 3, width // 6, width // 12)


def pool_places(width):
    w = pool_windows(width)
    return ((0, 0), (8, 0), (8, w[1]), (16, 0), (16, w[3]))


def feed_kernel(
    core, mixed, w_up, b_up, w_down, row, gain_a, shift_a, b_down, gain, shift, c0, c1, c2, c3, ids, pool_cot, bo, wo,
    low_far, act_out, l0, l1, l2, keep_out, sums_out,
    keep_u, send_u, b_up_out, hidden_one, mixed_out, sums_one,
    acc, unit_s, rstd_s, slope_out, low_out, up_s, down_s, cot_s, out_s, normal, rstd_a, sems,
    *, flush,
):
    length, width = mixed.shape
    part = length // 4
    hidden_width = w_up.shape[1]
    tile = FEED_TILE
    early, ups, downs = [], [], []
    numbers = iter(range(3 * PIECES + 4))
    for piece in range(PIECES):
        rows = slice(piece * (width // PIECES), (piece + 1) * (width // PIECES))
        early.append(pltpu.make_async_copy(wo.at[rows, :], out_s.at[rows, :], sems.at[next(numbers)]))
        ups.append(pltpu.make_async_copy(w_up.at[rows, :], up_s.at[rows, :], sems.at[next(numbers)]))
        rows = slice(piece * (hidden_width // PIECES), (piece + 1) * (hidden_width // PIECES))
        downs.append(pltpu.make_async_copy(w_down.at[rows, :], down_s.at[rows, :], sems.at[next(numbers)]))
    late = [
        pltpu.make_async_copy(source, cot_s.at[number], sems.at[next(numbers)])
        for number, source in enumerate((c0, c1, c2, c3))
    ]
    for copy in early + ups:
        copy.start()
    for copy in early:
        copy.wait()
    for copy in downs + late:
        copy.start()
    acc[...] = dot(mixed[...], out_s[...])
    for at in range(0, length, 32):
        rows = slice(at, at + 32)
        hidden = row[rows, :].astype(f32) + (acc[rows, :] + bo[...])
        centered = hidden - jnp.mean(hidden, axis=-1, keepdims=True)
        rstd = lax.rsqrt(jnp.mean(centered * centered, axis=-1, keepdims=True) + norm_eps)
        unit = centered * rstd
        normal[rows, :] = unit
        rstd_a[rows, :] = jnp.broadcast_to(rstd, (32, 128))
        low_far[rows, :] = (unit * gain_a[...] + shift_a[...]).astype(bf16)
    flush(0)
    for copy in ups:
        copy.wait()
    for at in range(0, hidden_width, tile):
        cols = slice(at, at + tile)
        up = dot(low_far[...], up_s[:, cols]) + b_up[:, cols]
        active, slope = gelu_both(up)
        active_low = active.astype(bf16)
        act_out[:, cols] = active_low
        slope_out[:, cols] = slope.astype(bf16)
        if at == 0:
            for copy in downs:
                copy.wait()
        down = dot(active_low, down_s[cols, :])
        if at == 0:
            acc[...] = down
        else:
            acc[...] += down

    groups = lax.broadcasted_iota(jnp.int32, (16, length), 0).astype(f32)
    member = jnp.where((groups == ids[0:1, :]) & (groups < SEGS), 1.0, 0.0).astype(bf16)
    outs = (l0, l1, l2.at[0], l2.at[1])
    seg_sums = jnp.zeros((16, width), f32)
    for at in range(4):
        rows = slice(at * part, (at + 1) * part)
        hidden = normal[rows, :] * gain_a[...] + shift_a[...] + (acc[rows, :] + b_down[...])
        centered = hidden - jnp.mean(hidden, axis=-1, keepdims=True)
        rstd = lax.rsqrt(jnp.mean(centered * centered, axis=-1, keepdims=True) + norm_eps)
        unit = centered * rstd
        unit_s[rows, :] = unit
        rstd_s[rows, :] = jnp.broadcast_to(rstd, (part, 128))
        result = unit * gain[...] + shift[...]
        outs[at][0:part, :] = result.astype(bf16)
        for piece in split_two(result):
            seg_sums += dot(member[:, rows], piece)
    seg_sums = seg_sums[:SEGS]
    first_lane = 0
    total = jnp.zeros((SEGS, width), f32)
    pooled = []
    for window in pool_windows(width):
        sums = seg_sums[:, :window]
        cot = pool_cot[:, first_lane : first_lane + window]
        factor = lax.rsqrt(jnp.mean(sums * sums, axis=-1, keepdims=True) + pool_eps)
        pooled.append(sums * factor)
        inner = jnp.sum(cot * sums, axis=-1, keepdims=True) * (factor * factor * factor / window)
        piece = cot * factor - sums * inner
        if window < width:
            piece = jnp.concatenate([piece, jnp.zeros((SEGS, width - window), f32)], axis=1)
        total += piece
        first_lane += window
    zeros = jnp.zeros((8, width), f32)
    rest = jnp.zeros((8, width - pooled[3].shape[1] - pooled[4].shape[1]), f32)
    upper = jnp.concatenate([pooled[0], jnp.concatenate(pooled[1:3], axis=1)], axis=0).astype(bf16)
    lower = jnp.concatenate([jnp.concatenate([pooled[3], pooled[4], rest], axis=1), zeros], axis=0).astype(bf16)
    for out in outs:
        out[part : part + 16, :] = upper
        out[part + 16 : part + 32, :] = lower
    flush(2, 3, 4)
    total = split_two(jnp.concatenate([total, zeros], axis=0))
    half = width // 2
    first = core[0] == 0
    sums = [jnp.zeros((1, width), f32)] * 3
    for copy in late:
        copy.wait()
    for at in range(4):
        rows = slice(at * part, (at + 1) * part)
        grad = cot_s[at].astype(f32) + sum(dot(member[:, rows], piece, 0, 0) for piece in total)
        unit = unit_s[rows, :]
        scaled = grad * gain[...]
        hidden_grad = rstd_s[rows, 0:1] * (
            scaled
            - jnp.mean(scaled, axis=-1, keepdims=True)
            - unit * jnp.mean(scaled * unit, axis=-1, keepdims=True)
        )
        acc[rows, :] = hidden_grad
        rounded = hidden_grad.astype(bf16)
        low_out[rows, :] = rounded
        keep_out[rows, :] = jnp.where(first, rounded[:, :half], rounded[:, half:])
        act_out[rows, hidden_width:] = jnp.where(first, rounded[:, half:], rounded[:, :half])
        for to, value in enumerate((grad * unit, grad, rounded.astype(f32))):
            sums[to] += jnp.sum(value, axis=0, keepdims=True)
    sums_out[...] = jnp.concatenate([*sums, jnp.zeros((5, width), f32)], axis=0)

    half_feed = hidden_width // 2
    for at, out in enumerate((send_u, keep_u)):
        which = core[0] if at == 1 else 1 - core[0]
        cols = pl.ds(pl.multiple_of(which * half_feed, 128), half_feed)
        grad_up = (dot(low_out[...], down_s[cols, :], 1, 1) * slope_out[:, cols].astype(f32)).astype(bf16)
        out[:, :half_feed] = grad_up
        b_up_out[:, cols] = jnp.broadcast_to(jnp.sum(grad_up.astype(f32), axis=0, keepdims=True), (8, half_feed))
        if at == 0:
            flush(1, 5, 6)
        back = dot(grad_up, up_s[:, cols], 1, 1)
        acc[...] += back

    sums = [jnp.zeros((1, width), f32)] * 3
    for at in range(0, length, 64):
        rows = slice(at, at + 64)
        grad = acc[rows, :]
        unit = normal[rows, :]
        scaled = grad * gain_a[...]
        hidden_grad = rstd_a[rows, 0:1] * (
            scaled
            - jnp.mean(scaled, axis=-1, keepdims=True)
            - unit * jnp.mean(scaled * unit, axis=-1, keepdims=True)
        )
        hidden_one[rows, :] = hidden_grad
        rounded = hidden_grad.astype(bf16)
        low_out[rows, :] = rounded
        keep_u[rows, half_feed:] = jnp.where(first, rounded[:, :half], rounded[:, half:])
        send_u[rows, half_feed:] = jnp.where(first, rounded[:, half:], rounded[:, :half])
        for to, value in enumerate((grad * unit, grad, rounded.astype(f32))):
            sums[to] += jnp.sum(value, axis=0, keepdims=True)
    flush(8, 7, 9, 10)
    mixed_out[...] = dot(low_out[...], out_s[...], 1, 1).astype(bf16)
    sums_one[...] = jnp.concatenate([*sums, jnp.zeros((5, width), f32)], axis=0)


def feed(core, mixed, w_up, b_up, w_down, row, gain_a, shift_a, b_down, gain, shift, cots, ids, pool_cot, bo, wo):
    length, width = mixed.shape
    hidden = w_up.shape[1]
    half = shape((length, width // 2))
    wide = shape((length, width), f32)
    part = length // 4 + 32
    outs = [
        shape((length, width)), shape((length, hidden + width // 2)), shape((part, width)), shape((part, width)), shape((2, part, width)),
        half, shape((8, width), f32), shape((length, hidden // 2 + width // 2)), shape((length, hidden // 2 + width // 2)),
        shape((8, hidden), f32), wide, shape((length, width)), shape((8, width), f32),
    ]
    scratch = [
        pltpu.VMEM((length, width), f32),
        pltpu.VMEM((length, width), f32),
        pltpu.VMEM((length, 128), f32),
        pltpu.VMEM((length, hidden), bf16),
        pltpu.VMEM((length, width), bf16),
        pltpu.VMEM(w_up.shape, bf16),
        pltpu.VMEM(w_down.shape, bf16),
        pltpu.VMEM((4, length // 4, width), bf16),
        pltpu.VMEM((width, width), bf16),
        pltpu.VMEM((length, width), f32),
        pltpu.VMEM((length, 128), f32),
        pltpu.SemaphoreType.DMA((3 * PIECES + 4,)),
    ]
    args = (core, mixed, w_up, b_up, w_down, row, gain_a, shift_a, b_down, gain, shift, *cots, ids, pool_cot, bo, wo)
    return in_vmem(
        feed_kernel, "feed_both", 37, outs, args, 18e9 * LATE, scratch, 1, far_in=(2, 4, 11, 12, 13, 14, 18)
    )


def attend_back_kernel(
    core, expo, total, q, k, v, mix_t, grad_mixed, keep_out, send_out, sums_out,
    held, q_s, k_s, v_s, mix_s, grad_s, sems,
    *, flush,
):
    length = expo.shape[1]
    pairs = q.shape[1] // 128
    per = pairs // 2
    slots = held.shape[0]

    def copies(at):
        which = core[0] if at >= per else 1 - core[0]
        pair = which * per + at % per
        lanes = pl.ds(pl.multiple_of(pair * 128, 128), 128)
        slot = at % slots
        sources = [
            (q.at[:, lanes], q_s), (k.at[:, lanes], k_s), (v.at[:, lanes], v_s),
            (mix_t.at[lanes, :], mix_s), (grad_mixed.at[:, lanes], grad_s),
            (expo.at[pl.ds(2 * pair, 2)], held),
        ]
        return [
            pltpu.make_async_copy(source, to.at[slot], sems.at[slot, number])
            for number, (source, to) in enumerate(sources)
        ]

    def start(group):
        for at in group:
            for copy in copies(at):
                copy.start()

    groups = [range(0, 1), range(1, per), range(per, pairs)]
    start(groups[0])
    start(groups[1])
    for at in range(pairs):
        for number, group in enumerate(groups):
            if at == group[0]:
                for member in group:
                    for copy in copies(member):
                        copy.wait()
                if number == 0:
                    start(groups[2])
        which = core[0] if at >= per else 1 - core[0]
        out = keep_out if at >= per else send_out
        pair, slot = at % per, at % slots
        lanes = pl.ds(pl.multiple_of(which * (per * 128) + pair * 128, 128), 128)
        grad_t = grad_s[slot].T.astype(f32)
        query, value, mix = q_s[slot], v_s[slot], mix_s[slot]
        key_t = k_s[slot].T
        halves = []
        inner = []
        for half in range(2):
            rows = slice(half * 64, half * 64 + 64)
            inverse = total[pl.ds(which * pairs + 2 * pair + half, 1), :]
            scaled = (grad_t[rows] * inverse).astype(bf16)
            halves.append(scaled)
            inner.append(jnp.sum(scaled.astype(f32) * mix[rows], axis=0, keepdims=True))
        scaled_rows = jnp.concatenate(halves, axis=0).T
        grads_q, grads_k, grads_v = [], [], []
        for half in range(2):
            rows = slice(half * 64, half * 64 + 64)
            probs = held[slot, half]
            grad_probs = dot(value[:, rows], halves[half])
            grad_scores = (probs.astype(f32) * (grad_probs - inner[half])).astype(bf16)
            grads_v.append(dot(probs, scaled_rows[:, rows]))
            grads_k.append(dot(grad_scores, query[:, rows]))
            grads_q.append(dot(key_t[rows, :], grad_scores))
        here = slice(pair * 128, pair * 128 + 128)
        grad_query = (jnp.concatenate(grads_q, axis=0).T * 0.125).astype(bf16)
        grad_value = jnp.concatenate(grads_v, axis=1).astype(bf16)
        out[0, :, here] = grad_query
        out[1, :, here] = jnp.concatenate(grads_k, axis=1).astype(bf16)
        out[2, :, here] = grad_value
        sums_out[:, lanes] = jnp.concatenate(
            [
                jnp.sum(grad_query.astype(f32), axis=0, keepdims=True),
                jnp.sum(grad_value.astype(f32), axis=0, keepdims=True),
                jnp.zeros((6, 128), f32),
            ],
            axis=0,
        )


def attend_back(core, expo, total, q, k, v, mix_t, grad_mixed):
    length, width = q.shape
    outs = [shape((3, length, width // 2)), shape((3, length, width // 2)), shape((8, width), f32)]
    args = (core, expo, total, q, k, v, mix_t, grad_mixed)
    slots = width // 128
    scratch = [
        pltpu.VMEM((slots, 2, length, length), bf16),
        *[pltpu.VMEM((slots, length, 128), bf16)] * 3,
        pltpu.VMEM((slots, 128, length), f32),
        pltpu.VMEM((slots, length, 128), bf16),
        pltpu.SemaphoreType.DMA((slots, 6)),
    ]
    return in_vmem(
        attend_back_kernel, "attend_backward", 20, outs, args, 9e9 * LATE, scratch, 1,
        fetch={2: (0, 1)}, far_in=(1, 3, 4, 5, 6, 7), free=(0, 1, 2),
    )


def add_input_grad(core, hidden, keep, send, wq, wk, wv, o0, o1, o2):
    width = hidden.shape[1]
    half = width // 2
    part = o0.shape[0]
    mine = pl.ds(pl.multiple_of(core[0] * half, 128), half)
    other = pl.ds(pl.multiple_of((1 - core[0]) * half, 128), half)
    total = hidden[...]
    for at, weight in enumerate((wq, wk, wv)):
        total += dot(keep[at], weight[:, mine], 1, 1) + dot(send[at], weight[:, other], 1, 1)
    total = total.astype(bf16)
    for at, out in enumerate((o0, o1, o2.at[0], o2.at[1])):
        out[...] = total[at * part : (at + 1) * part]


def down_weight_kernel(own, other, keep, out, *, flush):
    size = out.shape[0] // 4
    for at in range(4):
        rows = slice(at * size, (at + 1) * size)
        left, right = own[:, rows], other[:, rows]
        out[rows, :] = (dot(left, keep[...], 0, 0) + dot(right, other[:, 4 * size :], 0, 0)).astype(bf16)


def down_weight(own, other, keep):
    half = keep.shape[1]
    outs = [shape((own.shape[1] - half, half))]
    return in_vmem(down_weight_kernel, "down_weight", 14, outs, (own, other, keep), 4e9 * LATE, free=(0,))[0]


def weights_kernel(
    core, low, low_other, mixed, mixed_other, row, row_other, keep_u, got_u, keep_h, send_h, got_h, hidden, wq, wk, wv,
    b_up, sums_head, sums_one, sums_two,
    out_u, out_o, out_h, vec, g0, g1, g2,
    *, flush,
):
    half = out_o.shape[1]
    tiles = out_u.shape[0]
    for at in range(tiles):
        cols = slice(at * half, (at + 1) * half)
        out_u[at] = (dot(low[...], keep_u[:, cols], 0, 0) + dot(low_other[...], got_u[:, cols], 0, 0)).astype(bf16)
    cols = slice(tiles * half, (tiles + 1) * half)
    out_o[...] = (dot(mixed[...], keep_u[:, cols], 0, 0) + dot(mixed_other[...], got_u[:, cols], 0, 0)).astype(bf16)
    for at in range(3):
        out_h[at] = (dot(row[...], keep_h[at], 0, 0) + dot(row_other[...], got_h[at], 0, 0)).astype(bf16)
    add_input_grad(core, hidden, keep_h, send_h, wq, wk, wv, g0, g1, g2)
    shards = vec.shape[0]
    lines = jnp.concatenate([sums_head[0:2], sums_one[0:3], sums_two[0:3]], axis=0)
    line = lines.shape[1] // shards
    up = b_up.shape[1] // shards
    first = lax.broadcasted_iota(jnp.int32, (8, up), 0) == 0
    for at in range(shards):
        piece = lines[:, at * line : (at + 1) * line]
        if line < half:
            piece = jnp.concatenate([piece, jnp.zeros((8, half - line), f32)], axis=1)
        vec[at, 0] = jnp.concatenate([piece, jnp.zeros((8, half), f32)], axis=0).astype(bf16)
        piece = jnp.where(first, b_up[:, at * up : (at + 1) * up], 0.0)
        if up < half:
            piece = jnp.concatenate([piece, jnp.zeros((8, half - up), f32)], axis=1)
        vec[at, 1] = jnp.concatenate([piece, jnp.zeros((8, half), f32)], axis=0).astype(bf16)


def weights(shards, *args):
    low, keep_u = args[1], args[7]
    length, width = low.shape
    half = width // 2
    part = length // 4
    outs = [
        shape((keep_u.shape[1] // half - 1, width, half)), shape((width, half)), shape((3, width, half)),
        shape((shards, 2, 16, half)), shape((part, width)), shape((part, width)), shape((2, part, width)),
    ]
    every = range(len(outs))
    return in_vmem(weights_kernel, "other_weights", 14, outs, args, 11e9 * LATE, scalars=1, free=every)


def pack_kernel(seq_at, tokens, *rest, flush):
    ids, outs, sems = (rest[0], rest[1:5], rest[5]) if len(rest) == 6 else (None, rest[:4], rest[4])
    part, width = tokens.shape[1:]
    copies = []
    for at in (2, 3, 1, 0):
        copies.append(pltpu.make_async_copy(tokens.at[seq_at[0] ^ at], outs[at].at[:part, :], sems.at[at]))
        copies[-1].start()
    if ids is not None:
        for at, out in enumerate(outs):
            line = ids[pl.ds(seq_at[0] ^ at, 1), :].astype(f32)
            line = jnp.concatenate([line, jnp.zeros((1, width - part), f32)], axis=1)
            out[part : part + 16, :] = jnp.broadcast_to(line, (16, width)).astype(bf16)
    for copy in copies:
        copy.wait()


def pack(seq_at, tokens, ids=None):
    _, part, width = tokens.shape
    extra = 0 if ids is None else 16
    args = (seq_at, tokens) if ids is None else (seq_at, tokens, ids)
    outs = [shape((part + extra, width))] * 4
    fetch = {} if ids is None else {2: (0, 1)}
    scratch = [pltpu.SemaphoreType.DMA((4,))]
    return in_vmem(
        pack_kernel, "pack_rows", 6, outs, args, 1e8, scratch, 1, fetch=fetch, far_in=(1,), near=(0, 1, 2, 3)
    )


def place_kernel(seq_at, b0, b1, b2, b3, out, *pooled, flush):
    part, width = out.shape[1:]
    for at, block in enumerate((b0, b1, b2, b3)):
        to = seq_at[0] ^ at
        rows = block.piece()[0] if at == 2 else block[...]
        out[to] = rows[:part, :]
        if pooled:
            first = 0
            rows = rows[part : part + 32, :].astype(f32)
            for window, (row, lane) in zip(pool_windows(width), pool_places(width)):
                pooled[0][to, :, first : first + window] = rows[row : row + 8, lane : lane + window]
                first += window


def place(seq_at, blocks, part, pooled):
    width = blocks[0].shape[1]
    outs = [shape((4, part, width))]
    if pooled:
        outs.append(shape((4, SEGS, sum(pool_windows(width))), f32))
    fetch = {at: (0, 1) for at in range(1, 5)}
    return in_vmem(place_kernel, "place_rows", 6, outs, (seq_at, *blocks), 1e8, scalars=1, fetch=fetch)


def swap_seq(value, mask):
    return lax.ppermute(value, "seq", [(at, at ^ mask) for at in range(4)])


def exchange(own, core_block, chip_blocks):
    got_core = swap_seq(core_block, 1)
    got_chip = swap_seq(chip_blocks, 2)
    return [own, got_core, got_chip]


def forward(blocks):
    return [*blocks, swap_seq(blocks[2][1], 1)]


class Part:
    def __init__(self, blocks, names, first, rows):
        self.blocks, self.names, self.first, self.rows, self.got = blocks, names, first, rows, None


class Exchanges:
    def __init__(self, row_at, seq_at, row_count):
        self.row_count = row_count
        self.axes = ["x"] + [1 << at for at in range(row_count.bit_length() - 1)]
        self.bits = jnp.stack([(seq_at >> 1) & 1] + [(row_at // axis) & 1 for axis in self.axes[1:]])

    def part(self, blocks, first=0, rows=None):
        names = [("tile", blocks.shape[0])] + [(axis, 2) for axis in reversed(self.axes[1:])] + [("x", 2)]
        rows = blocks.shape[3] if rows is None else rows
        return Part(blocks.reshape(-1, *blocks.shape[3:]), names, first, rows)

    def swap(self, value, axis):
        if axis == "x":
            return swap_seq(value, 2)
        return lax.ppermute(value, "rows", [(at, at ^ axis) for at in range(self.row_count)])

    def tick(self, moves, settle=(), far=False):
        parts = [part for part, _ in moves] + list(settle)
        ins = []
        for part in parts:
            for value in (part.blocks, part.got and part.got[0]):
                if value is not None and not any(value is other for other in ins):
                    ins.append(value)
        find = lambda value: [value is other for other in ins].index(True)
        lanes = parts[0].blocks.shape[2]
        used = list(dict.fromkeys(axis for _, axis in moves))
        outs, plan, rows_of, kept = [], [], dict.fromkeys([*used, None], 0), []
        for part, axis in [*moves, *[(part, None) for part in settle]]:
            count = part.blocks.shape[0]
            source = (find(part.blocks), part.first, part.rows, part.got and (find(part.got[0]), part.got[1]))
            if axis is None:
                plan.append((source, axis, [(at, None) for at in range(count)], rows_of[axis], None))
                rows_of[axis] += count * part.rows
                continue
            names = [name for name, _ in part.names]
            low = 1
            for _, size in part.names[names.index(axis) + 1 :]:
                low *= size
            pairs = [(at, at + low) for at in range(count) if (at // low) % 2 == 0]
            plan.append((source, axis, pairs, rows_of[axis], len(kept)))
            kept.append(shape((count // 2, part.rows, lanes)))
            part.got = (axis, rows_of[axis])
            rows_of[axis] += len(pairs) * part.rows
            part.names = [entry for entry in part.names if entry[0] != axis]
        flat = [*used, *([None] if settle else [])]
        outs = [shape((rows_of[axis], lanes)) for axis in flat] + kept

        def kernel(bits, *refs, flush):
            given, sends, keeps = refs[: len(ins)], refs[len(ins) : len(ins) + len(flat)], refs[len(ins) + len(flat) :]
            for (blocks, first, rows, got), axis, pairs, row, keep in plan:
                send = sends[flat.index(axis)]

                def value(at):
                    block = given[blocks][at, first : first + rows, :]
                    if got is None:
                        return block
                    other = given[got[0]][got[1] + at * rows : got[1] + (at + 1) * rows, :]
                    return (block.astype(f32) + other.astype(f32)).astype(bf16)

                for number, (zero, one) in enumerate(pairs):
                    where = slice(row + number * rows, row + (number + 1) * rows)
                    if axis is None:
                        send[where, :] = value(zero)
                        continue
                    bit = bits[self.axes.index(axis)] == 0
                    left, right = value(zero), value(one)
                    send[where, :] = jnp.where(bit, right, left)
                    keeps[keep][number] = jnp.where(bit, left, right)

        every = range(len(flat) if far else 0, len(outs))
        results = in_vmem(kernel, "halves", 10, outs, (self.bits, *ins), 1e8, scalars=1, free=every)
        arrived = {axis: self.swap(results[flat.index(axis)], axis) for axis in used}
        for (part, axis), blocks in zip(moves, results[len(flat) :]):
            part.blocks, part.first = blocks, 0
            part.got = (arrived[axis], part.got[1])
        return results[len(used)] if settle else None

    def before(self, parts, value):
        blocks = [part.blocks for part in parts]
        value, blocks = lax.optimization_barrier((value, blocks))
        for part, new in zip(parts, blocks):
            part.blocks = new
        return value

    def after(self, parts, value):
        found = []
        for part in parts:
            if not any(part.got[0] is other for other in found):
                found.append(part.got[0])
        value, new = lax.optimization_barrier((value, found))
        for part in parts:
            at = [part.got[0] is other for other in found].index(True)
            part.got = (new[at], part.got[1])
        return value


def sides(bits, piece, got_x, got_c, got_xc):
    mine = [jnp.where(bits[0] == 0, piece, got_x), jnp.where(bits[0] == 0, got_x, piece)]
    other = [jnp.where(bits[0] == 0, got_c, got_xc), jnp.where(bits[0] == 0, got_xc, got_c)]
    left = [jnp.where(bits[1] == 0, a, b) for a, b in zip(mine, other)]
    right = [jnp.where(bits[1] == 0, b, a) for a, b in zip(mine, other)]
    return left, right


def final_kernel(kinds, bits, *refs, flush):
    own, outs = refs[:4], refs[4:]
    half = own[0].shape[1]
    for number, (pieces, out) in enumerate(zip(kinds, outs)):
        for at, rows, to_row, to_lane in pieces:
            left, right = sides(bits, *[ref[at : at + rows, :].astype(f32) for ref in own])
            if to_lane is None:
                for x in range(2):
                    out[x, :, :] = left[x] + right[x]
                continue
            for x in range(2):
                first = x * (out.shape[0] // 2) + to_row
                out[first : first + rows, to_lane : to_lane + half] = left[x]
                right_lane = out.shape[1] // 2 + to_lane
                out[first : first + rows, right_lane : right_lane + half] = right[x]
        flush(number)


def gather(piece, meanwhile=None):
    got_x = swap_seq(piece, 2)
    if meanwhile is not None:
        got_x, meanwhile = lax.optimization_barrier((got_x, meanwhile))
    return (piece, got_x, swap_seq(piece, 1), swap_seq(got_x, 1)), meanwhile


def final(bits, pieces, kinds, outs):
    kernel = functools.partial(final_kernel, kinds)
    return in_vmem(kernel, "final_rows", 12, outs, (bits, *pieces), 1e8, scalars=1)


def together(*values):
    return lax.optimization_barrier(values)


def local(
    row_count,
    tokens, segment_ids, w_query, w_key, w_value, b_query, b_value, w_out, b_out, gain_attn, shift_attn,
    w_up, b_up, w_down, b_down, gain_out, shift_out, token_cot, pool_cot,
):
    part, width = tokens.shape[1:]
    feed_width = w_up.shape[1]
    half = width // 2
    seq_at = lax.axis_index("seq")
    row_at = lax.axis_index("rows")
    core = (seq_at & 1).reshape(1)
    where_at = seq_at.reshape(1)
    ex = Exchanges(row_at, seq_at, row_count)
    last_bits = jnp.stack([(seq_at >> 1) & 1, seq_at & 1])
    y, zs = ex.axes[1], ex.axes[2:]
    z1, z2 = zs[0], zs[1]

    def vec(v):
        return v.reshape(1, -1)

    own = pack(where_at, tokens, segment_ids)
    token_cot, own, near = together(token_cot, own, (w_query, w_key, w_value))
    swapped = {mask: swap_seq(own[mask], mask) for mask in (2, 3, 1)}
    blocks = [own[0]] + [swapped[mask] for mask in (1, 2, 3)]
    near_query, near_key, near_value = load(*near)
    own = pack(where_at, token_cot)
    own, blocks[1], near_query, near_key, near_value = together(own, blocks[1], near_query, near_key, near_value)
    swapped = {mask: swap_seq(own[mask], mask) for mask in (2, 3, 1)}
    cots = [own[0]] + [swapped[mask] for mask in (1, 2, 3)]
    row_pool_cot = lax.dynamic_index_in_dim(pool_cot, seq_at, 0, keepdims=False)

    expo, total, row, q, k, v, mix_t, mixed_near, mixed, row_near, ids_row = attend(
        blocks, near_query, near_key, near_value, vec(b_query), vec(b_value)
    )
    low_far, act, l0, l1, l2, keep_d, sums_two, keep_u, send_u, b_up_sum, hidden_one, grad_mixed, sums_one = feed(
        core, mixed_near, w_up, vec(b_up), w_down, row_near, vec(gain_attn), vec(shift_attn), vec(b_down),
        vec(gain_out), vec(shift_out), cots, ids_row, row_pool_cot, vec(b_out), w_out,
    )
    row_other, mixed_other, low_other = swap_seq(row, 1), swap_seq(mixed, 1), swap_seq(low_far, 1)
    act_other, got_u = swap_seq(act, 1), swap_seq(send_u, 1)
    layer_blocks = exchange(l0, l1, l2)

    def cut(value):
        return value.reshape(-1, row_count, 2, value.shape[-2] // row_count // 2, half)

    row_other, mixed_other, grad_mixed = together(row_other, mixed_other, grad_mixed)
    keep_h, send_h, sums_head = attend_back(core, expo, total, q, k, v, mix_t, grad_mixed)
    act_other, got_u, layer_blocks[1], keep_d, send_h = together(act_other, got_u, layer_blocks[1], keep_d, send_h)
    got_h = swap_seq(send_h, 1)
    grad_w_down = cut(down_weight(act, act_other, keep_d))
    layer_blocks, got_h, low_other, grad_w_down = together(layer_blocks, got_h, low_other, grad_w_down)
    down = grad_w_down.shape[3]
    sizes = [down * at // 12 for at in D_SPLIT]
    d_a, d_b, d_c = (ex.part(grad_w_down, sum(sizes[:at]), sizes[at]) for at in range(3))
    d_parts = [d_a, d_b, d_c]
    ex.tick([(d_c, z1), (d_b, y), (d_a, "x")])
    keep_u = ex.before(d_parts, keep_u)
    grad_w_up, grad_w_out, head, lines, *grads = weights(
        row_count, core, low_far, low_other, mixed, mixed_other, row, row_other, keep_u, got_u, keep_h, send_h, got_h,
        hidden_one, w_query, w_key, w_value, b_up_sum, sums_head, sums_one, sums_two,
    )
    grad_w_up, grad_w_out, head = cut(grad_w_up), cut(grad_w_out), cut(head)
    rows = grad_w_up.shape[3]
    u_a, u_b, u_c, o = ex.part(grad_w_up[:1]), ex.part(grad_w_up[1:2]), ex.part(grad_w_up[2:]), ex.part(grad_w_out)
    u_parts = [u_a, u_b, u_c, o]
    third = rows // 3
    q_part, k_first, k_rest = ex.part(head[0:1]), ex.part(head[1:2], 0, third), ex.part(head[1:2], third, rows - third)
    v_part, line_part = ex.part(head[2:3]), ex.part(lines[None])
    a_parts, b_parts = [q_part, k_first, line_part], [k_rest, v_part]
    head_parts = a_parts + b_parts

    def moves(parts, axis):
        return [(part, axis) for part in parts]

    ex.tick(
        moves([d_b, u_a, *a_parts], "x") + moves([d_a, u_b, *b_parts], y) + moves([u_c, o], z1) + moves([d_c], z2)
    )
    every_part = d_parts + u_parts + head_parts
    layer_blocks = forward(ex.before(head_parts, layer_blocks))
    layer_out, pooled = place(where_at, layer_blocks, part, True)
    layer_out, grads = ex.after(every_part, (layer_out, grads))
    ex.tick(
        moves([u_c], z2) + moves([u_a, *a_parts], y) + moves([d_c, u_b, o, *b_parts], "x") + moves([d_a, d_b], z1)
    )
    grads, grad_core = ex.after(every_part, (grads, swap_seq(grads[1], 1)))
    ex.tick(moves([u_a, u_b, *head_parts], z1) + moves([d_c, u_c, o], y) + moves([d_a, d_b], z2))
    grads = ex.before(head_parts, grads)
    grad_blocks = ex.after(d_parts + u_parts + head_parts, [grads[0], grad_core, swap_seq(grads[2], 2)])
    late = u_parts + head_parts
    if zs[2:]:
        ex.tick(moves([u_a, u_b, o, *head_parts], z2) + moves([u_c], "x"))
        for z in zs[2:]:
            ex.tick(moves(d_parts + late, z))
        down_piece = ex.tick([], d_parts)
    else:
        down_piece = ex.tick(moves([u_a, u_b, o, *head_parts], z2) + moves([u_c], "x"), d_parts)
    d_kinds = (tuple((sum(sizes[:at]), sizes[at], sum(sizes[:at]), 0) for at in range(3) if sizes[at]),)
    grad_tokens = place(where_at, forward(grad_blocks), part, False)[0]
    grad_tokens, down_pieces = ex.after(late, (grad_tokens, gather(down_piece)[0]))
    late_piece = ex.tick([], late)
    down_pieces, late_piece = together(down_pieces, late_piece)
    out_w_down = final(last_bits, down_pieces, d_kinds, [shape((2 * down, width), f32)])[0]
    late_pieces, out_w_down = gather(late_piece, out_w_down)
    wide = [shape((2 * rows, feed_width), f32)] + [shape((2 * rows, width), f32)] * 4 + [shape((2, 16, half), f32)]
    at_q = 5 * rows
    at_k = at_q + rows
    at_lines = at_k + third
    at_rest = at_lines + 16
    kinds = (
        tuple((at * rows, rows, 0, at * half) for at in range(4)),
        ((4 * rows, rows, 0, 0),),
        ((at_q, rows, 0, 0),),
        ((at_k, third, 0, 0), (at_rest, rows - third, third, 0)),
        ((at_rest + rows - third, rows, 0, 0),),
        ((at_lines, 16, 0, None),),
    )
    out_w_up, out_w_out, out_w_query, out_w_key, out_w_value, lines = final(last_bits, late_pieces, kinds, wide)
    rest = lines[0, :8, : width // row_count]
    out_b_up = lines[1, 0, : feed_width // row_count]
    return (
        layer_out, pooled, grad_tokens,
        out_w_query, out_w_key, out_w_value, rest[0], rest[1], out_w_out, rest[4], rest[2], rest[3],
        out_w_up, out_b_up, out_w_down, rest[7], rest[5], rest[6],
    )


def solution(mesh):
    split = P("rows", "seq", None)
    in_specs = (split, P("rows", "seq"), *[P()] * 15, split, P("rows", None, None))
    mat, line = P("rows", None), P("rows")
    out_specs = (
        split, P("rows", None, None), split,
        mat, mat, mat, line, line, mat, line, line, line, mat, line, mat, line, line, line,
    )
    body = functools.partial(local, mesh.shape["rows"])
    return jax.shard_map(body, mesh=mesh, in_specs=in_specs, out_specs=out_specs, check_vma=False)
```

```python
import functools

import jax
import jax.numpy as jnp
from jax import lax
from jax.experimental import pallas as pl
from jax.experimental.pallas import tpu as pltpu
from jax.sharding import PartitionSpec as P

HEADS = 12
SEGS = 8
FEED_TILE = 1024
PIECES = 3
COST = 0.001
LATE = 8000.0
D_SPLIT = (4, 4, 4)
BYTES = 1.0
norm_eps = 1e-12
pool_eps = 1e-06
bf16 = jnp.bfloat16
f32 = jnp.float32
MIB = 2**20


def shape(dims, dtype=bf16):
    return jax.ShapeDtypeStruct(dims, dtype)


def dot(left, right, left_dim=1, right_dim=0):
    return lax.dot_general(
        left, right, (((left_dim,), (right_dim,)), ((), ())), preferred_element_type=f32
    )


def in_vmem(kernel, name, mib, outs, args, work, scratch=(), scalars=0, fetch=(), far_in=(), near=(), free=(), far_own=()):
    args, outs, fetch = list(args), list(outs), dict(fetch)
    in_specs = [pl.BlockSpec(memory_space=pltpu.VMEM)] * len(args)
    for at in range(scalars):
        in_specs[at] = pl.BlockSpec(memory_space=pltpu.SMEM)
    for at in [*fetch, *far_in]:
        in_specs[at] = pl.BlockSpec(memory_space=pltpu.HBM)
        args[at] = pltpu.with_memory_space_constraint(args[at], pltpu.HBM)
    out_specs = [pl.BlockSpec(memory_space=pltpu.VMEM)] * len(outs)
    far_out = [at for at in range(len(outs)) if at not in near and at not in free and at not in far_own]
    held_in = [pltpu.VMEM(args[at].shape, args[at].dtype) for at in fetch]
    held_out = [pltpu.VMEM(outs[at].shape, outs[at].dtype) for at in far_out]
    size = sum(v.size * v.dtype.itemsize for v in (*args, *outs))
    for at in [*far_out, *far_own]:
        out_specs[at] = pl.BlockSpec(memory_space=pltpu.HBM)
        outs[at] = pltpu.HBM(outs[at].shape, outs[at].dtype)
    pieces = [(at, dim, count, piece) for at, (dim, count) in fetch.items() for piece in range(count)]
    pieces.sort(key=lambda piece: piece[3])
    count_in, count_out = len(args), len(outs)

    def body(*refs):
        ins, results = list(refs[:count_in]), list(refs[count_in : count_in + count_out])
        rest = list(refs[count_in + count_out :])
        own = [rest.pop(0) for _ in scratch]
        buffers = dict(zip(fetch, [rest.pop(0) for _ in held_in]))
        staged = dict(zip(far_out, [rest.pop(0) for _ in held_out]))
        sems_in = rest.pop(0) if pieces else None
        sems_out = rest.pop(0) if far_out else None
        copies = {at: [] for at in fetch}
        for number, (at, dim, count, piece) in enumerate(pieces):
            length = args[at].shape[dim] // count
            where = [slice(None)] * args[at].ndim
            where[dim] = pl.ds(piece * length, length)
            where = tuple(where)
            copy = pltpu.make_async_copy(ins[at].at[where], buffers[at].at[where], sems_in.at[number])
            copy.start()
            copies[at].append(copy)
        for at in fetch:
            ins[at] = Fetched(buffers[at], copies[at])
        sent = {}

        def flush(*numbers):
            for at in numbers:
                sent[at] = pltpu.make_async_copy(staged[at], results[at], sems_out.at[far_out.index(at)])
                sent[at].start()

        kernel(*ins, *[staged.get(at, results[at]) for at in range(count_out)], *own, flush=flush)
        flush(*[at for at in far_out if at not in sent])
        for copy in sent.values():
            copy.wait()
        for one in ins:
            if isinstance(one, Fetched):
                one.finish()

    sems = [pltpu.SemaphoreType.DMA((count,)) for count in (len(pieces), len(far_out)) if count]
    return pl.pallas_call(
        body,
        in_specs=in_specs,
        out_specs=out_specs,
        out_shape=outs,
        scratch_shapes=[*scratch, *held_in, *held_out, *sems],
        compiler_params=pltpu.CompilerParams(vmem_limit_bytes=mib * MIB),
        cost_estimate=pl.CostEstimate(flops=int(work * COST), bytes_accessed=int(size * BYTES), transcendentals=0),
        name=name,
    )(*args)


class Fetched:
    def __init__(self, ref, copies):
        self.ref, self.copies, self.waited = ref, copies, set()

    def piece(self, at=0):
        if at not in self.waited:
            self.waited.add(at)
            self.copies[at].wait()
        return self.ref

    def finish(self):
        for at in range(len(self.copies)):
            self.piece(at)

    def __getitem__(self, where):
        self.finish()
        return self.ref[where]

    @property
    def shape(self):
        return self.ref.shape


def load_kernel(*refs, flush):
    count = (len(refs) - 1) // 2
    copies = [pltpu.make_async_copy(refs[at], refs[count + at], refs[-1].at[at]) for at in range(count)]
    for copy in copies:
        copy.start()
    for copy in copies:
        copy.wait()


def load(*arrays):
    outs = [shape(v.shape, v.dtype) for v in arrays]
    every = range(len(arrays))
    scratch = [pltpu.SemaphoreType.DMA((len(arrays),))]
    return in_vmem(load_kernel, "load_weights", 4, outs, arrays, 1e9, scratch, far_in=every, near=every)


def split_two(value):
    high = value.astype(bf16)
    return high, (value - high.astype(f32)).astype(bf16)


def attend_kernel(
    t0, t1, t2, t3, wq, wk, wv, bq, bv,
    exp_out, total_out, row_out, q_out, k_out, v_out, mix_t, mixed_out, mixed_far, row_near, ids_out,
    mask, stage, sems,
    *, flush,
):
    blocks = (t0, t1, t2, t3)
    part = t0.shape[0] - 16
    length, width = row_out.shape
    for at, block in enumerate(blocks):
        row_out[at * part : (at + 1) * part, :] = block[:part, :]
    rows = row_out[...]
    row_near[...] = rows
    q_out[...] = (dot(rows, wq[...]) + bq[...]).astype(bf16) * bf16(0.125)
    k_out[...] = dot(rows, wk[...]).astype(bf16)
    v_out[...] = (dot(rows, wv[...]) + bv[...]).astype(bf16)
    flush(2, 3, 4, 5)
    ids = jnp.concatenate([block[part : part + 16, :part].astype(f32)[0:1] for block in blocks], axis=1)
    ids_out[...] = jnp.broadcast_to(ids, ids_out.shape)
    column = jnp.broadcast_to(ids, (128, length)).T[:, 0:1]
    mask[...] = jnp.where(column == ids, 0.0, -1e30)

    sent = []
    for pair in range(width // 128):
        lanes = slice(pair * 128, pair * 128 + 128)
        keys = k_out[:, lanes]
        query_t = q_out[:, lanes].T
        value_t = v_out[:, lanes].T
        for half in range(2):
            at = slice(half * 64, half * 64 + 64)
            head = 2 * pair + half
            scores = dot(keys[:, at], query_t[at, :]) + mask[...]
            expo = jnp.exp(scores - jnp.max(scores, axis=0, keepdims=True))
            inverse = 1.0 / jnp.sum(expo, axis=0, keepdims=True)
            low = expo.astype(bf16)
            stage[head] = low
            sent.append(pltpu.make_async_copy(stage.at[head], exp_out.at[head], sems.at[head]))
            sent[-1].start()
            total_out[head : head + 1, :] = inverse
            mix_t[head * 64 : head * 64 + 64, :] = dot(value_t[at, :], low) * inverse

    flush(1, 6)
    mixed = mix_t[...].astype(bf16).T
    mixed_out[...] = mixed
    mixed_far[...] = mixed
    for copy in sent:
        copy.wait()


def attend(blocks, wq, wk, wv, bq, bv):
    part, width = blocks[0].shape
    length = (part - 16) * 4
    heads = width // 64
    flat = shape((length, width))
    outs = [
        shape((heads, length, length)), shape((16, length), f32), flat, flat, flat, flat, shape((width, length), f32),
        flat, flat, flat, shape((8, length), f32),
    ]
    args = (*blocks, wq, wk, wv, bq, bv)
    scratch = [
        pltpu.VMEM((length, length), f32),
        pltpu.VMEM((heads, length, length), bf16),
        pltpu.SemaphoreType.DMA((heads,)),
    ]
    fetch = {at: (0, 1) for at in range(1, 4)}
    return in_vmem(
        attend_kernel, "attend_forward", 20, outs, args, 10e9 * LATE, scratch, fetch=fetch, near=(7, 9, 10), far_own=(0,)
    )


def gelu_both(v):
    phi = 0.5 + 0.5 * lax.erf(v * 0.7071067811865476)
    bell = jnp.exp2(v * (v * (-0.5 * 1.4426950408889634)))
    return v * phi, phi + (v * 0.3989422804014327) * bell


def pool_windows(width):
    return (width, width * 2 // 3, width // 3, width // 6, width // 12)


def pool_places(width):
    w = pool_windows(width)
    return ((0, 0), (8, 0), (8, w[1]), (16, 0), (16, w[3]))


def feed_kernel(
    core, mixed, w_up, b_up, w_down, row, gain_a, shift_a, b_down, gain, shift, c0, c1, c2, c3, ids, pool_cot, bo, wo,
    low_far, act_out, l0, l1, l2, keep_out, sums_out,
    keep_u, send_u, b_up_out, hidden_one, mixed_out, sums_one,
    acc, unit_s, rstd_s, slope_out, low_out, up_s, down_s, cot_s, out_s, normal, rstd_a, sems,
    *, flush,
):
    length, width = mixed.shape
    part = length // 4
    hidden_width = w_up.shape[1]
    tile = FEED_TILE
    early, ups, downs = [], [], []
    numbers = iter(range(3 * PIECES + 4))
    for piece in range(PIECES):
        rows = slice(piece * (width // PIECES), (piece + 1) * (width // PIECES))
        early.append(pltpu.make_async_copy(wo.at[rows, :], out_s.at[rows, :], sems.at[next(numbers)]))
        ups.append(pltpu.make_async_copy(w_up.at[rows, :], up_s.at[rows, :], sems.at[next(numbers)]))
        rows = slice(piece * (hidden_width // PIECES), (piece + 1) * (hidden_width // PIECES))
        downs.append(pltpu.make_async_copy(w_down.at[rows, :], down_s.at[rows, :], sems.at[next(numbers)]))
    late = [
        pltpu.make_async_copy(source, cot_s.at[number], sems.at[next(numbers)])
        for number, source in enumerate((c0, c1, c2, c3))
    ]
    for copy in early + ups:
        copy.start()
    for copy in early:
        copy.wait()
    for copy in downs + late:
        copy.start()
    acc[...] = dot(mixed[...], out_s[...])
    for at in range(0, length, 32):
        rows = slice(at, at + 32)
        hidden = row[rows, :].astype(f32) + (acc[rows, :] + bo[...])
        centered = hidden - jnp.mean(hidden, axis=-1, keepdims=True)
        rstd = lax.rsqrt(jnp.mean(centered * centered, axis=-1, keepdims=True) + norm_eps)
        unit = centered * rstd
        normal[rows, :] = unit
        rstd_a[rows, :] = jnp.broadcast_to(rstd, (32, 128))
        low_far[rows, :] = (unit * gain_a[...] + shift_a[...]).astype(bf16)
    flush(0)
    for copy in ups:
        copy.wait()
    for at in range(0, hidden_width, tile):
        cols = slice(at, at + tile)
        up = dot(low_far[...], up_s[:, cols]) + b_up[:, cols]
        active, slope = gelu_both(up)
        active_low = active.astype(bf16)
        act_out[:, cols] = active_low
        slope_out[:, cols] = slope.astype(bf16)
        if at == 0:
            for copy in downs:
                copy.wait()
        down = dot(active_low, down_s[cols, :])
        if at == 0:
            acc[...] = down
        else:
            acc[...] += down

    groups = lax.broadcasted_iota(jnp.int32, (16, length), 0).astype(f32)
    member = jnp.where((groups == ids[0:1, :]) & (groups < SEGS), 1.0, 0.0).astype(bf16)
    outs = (l0, l1, l2.at[0], l2.at[1])
    seg_sums = jnp.zeros((16, width), f32)
    for at in range(4):
        rows = slice(at * part, (at + 1) * part)
        hidden = normal[rows, :] * gain_a[...] + shift_a[...] + (acc[rows, :] + b_down[...])
        centered = hidden - jnp.mean(hidden, axis=-1, keepdims=True)
        rstd = lax.rsqrt(jnp.mean(centered * centered, axis=-1, keepdims=True) + norm_eps)
        unit = centered * rstd
        unit_s[rows, :] = unit
        rstd_s[rows, :] = jnp.broadcast_to(rstd, (part, 128))
        result = unit * gain[...] + shift[...]
        outs[at][0:part, :] = result.astype(bf16)
        for piece in split_two(result):
            seg_sums += dot(member[:, rows], piece)
    seg_sums = seg_sums[:SEGS]
    first_lane = 0
    total = jnp.zeros((SEGS, width), f32)
    pooled = []
    for window in pool_windows(width):
        sums = seg_sums[:, :window]
        cot = pool_cot[:, first_lane : first_lane + window]
        factor = lax.rsqrt(jnp.mean(sums * sums, axis=-1, keepdims=True) + pool_eps)
        pooled.append(sums * factor)
        inner = jnp.sum(cot * sums, axis=-1, keepdims=True) * (factor * factor * factor / window)
        piece = cot * factor - sums * inner
        if window < width:
            piece = jnp.concatenate([piece, jnp.zeros((SEGS, width - window), f32)], axis=1)
        total += piece
        first_lane += window
    zeros = jnp.zeros((8, width), f32)
    rest = jnp.zeros((8, width - pooled[3].shape[1] - pooled[4].shape[1]), f32)
    upper = jnp.concatenate([pooled[0], jnp.concatenate(pooled[1:3], axis=1)], axis=0).astype(bf16)
    lower = jnp.concatenate([jnp.concatenate([pooled[3], pooled[4], rest], axis=1), zeros], axis=0).astype(bf16)
    for out in outs:
        out[part : part + 16, :] = upper
        out[part + 16 : part + 32, :] = lower
    flush(2, 3, 4)
    total = split_two(jnp.concatenate([total, zeros], axis=0))
    half = width // 2
    first = core[0] == 0
    sums = [jnp.zeros((1, width), f32)] * 3
    for copy in late:
        copy.wait()
    for at in range(4):
        rows = slice(at * part, (at + 1) * part)
        grad = cot_s[at].astype(f32) + sum(dot(member[:, rows], piece, 0, 0) for piece in total)
        unit = unit_s[rows, :]
        scaled = grad * gain[...]
        hidden_grad = rstd_s[rows, 0:1] * (
            scaled
            - jnp.mean(scaled, axis=-1, keepdims=True)
            - unit * jnp.mean(scaled * unit, axis=-1, keepdims=True)
        )
        acc[rows, :] = hidden_grad
        rounded = hidden_grad.astype(bf16)
        low_out[rows, :] = rounded
        keep_out[rows, :] = jnp.where(first, rounded[:, :half], rounded[:, half:])
        act_out[rows, hidden_width:] = jnp.where(first, rounded[:, half:], rounded[:, :half])
        for to, value in enumerate((grad * unit, grad, rounded.astype(f32))):
            sums[to] += jnp.sum(value, axis=0, keepdims=True)
    sums_out[...] = jnp.concatenate([*sums, jnp.zeros((5, width), f32)], axis=0)

    half_feed = hidden_width // 2
    for at, out in enumerate((send_u, keep_u)):
        which = core[0] if at == 1 else 1 - core[0]
        cols = pl.ds(pl.multiple_of(which * half_feed, 128), half_feed)
        grad_up = (dot(low_out[...], down_s[cols, :], 1, 1) * slope_out[:, cols].astype(f32)).astype(bf16)
        out[:, :half_feed] = grad_up
        b_up_out[:, cols] = jnp.broadcast_to(jnp.sum(grad_up.astype(f32), axis=0, keepdims=True), (8, half_feed))
        if at == 0:
            flush(1, 5, 6)
        back = dot(grad_up, up_s[:, cols], 1, 1)
        acc[...] += back

    sums = [jnp.zeros((1, width), f32)] * 3
    for at in range(0, length, 64):
        rows = slice(at, at + 64)
        grad = acc[rows, :]
        unit = normal[rows, :]
        scaled = grad * gain_a[...]
        hidden_grad = rstd_a[rows, 0:1] * (
            scaled
            - jnp.mean(scaled, axis=-1, keepdims=True)
            - unit * jnp.mean(scaled * unit, axis=-1, keepdims=True)
        )
        hidden_one[rows, :] = hidden_grad
        rounded = hidden_grad.astype(bf16)
        low_out[rows, :] = rounded
        keep_u[rows, half_feed:] = jnp.where(first, rounded[:, :half], rounded[:, half:])
        send_u[rows, half_feed:] = jnp.where(first, rounded[:, half:], rounded[:, :half])
        for to, value in enumerate((grad * unit, grad, rounded.astype(f32))):
            sums[to] += jnp.sum(value, axis=0, keepdims=True)
    flush(8, 7, 9, 10)
    mixed_out[...] = dot(low_out[...], out_s[...], 1, 1).astype(bf16)
    sums_one[...] = jnp.concatenate([*sums, jnp.zeros((5, width), f32)], axis=0)


def feed(core, mixed, w_up, b_up, w_down, row, gain_a, shift_a, b_down, gain, shift, cots, ids, pool_cot, bo, wo):
    length, width = mixed.shape
    hidden = w_up.shape[1]
    half = shape((length, width // 2))
    wide = shape((length, width), f32)
    part = length // 4 + 32
    outs = [
        shape((length, width)), shape((length, hidden + width // 2)), shape((part, width)), shape((part, width)), shape((2, part, width)),
        half, shape((8, width), f32), shape((length, hidden // 2 + width // 2)), shape((length, hidden // 2 + width // 2)),
        shape((8, hidden), f32), wide, shape((length, width)), shape((8, width), f32),
    ]
    scratch = [
        pltpu.VMEM((length, width), f32),
        pltpu.VMEM((length, width), f32),
        pltpu.VMEM((length, 128), f32),
        pltpu.VMEM((length, hidden), bf16),
        pltpu.VMEM((length, width), bf16),
        pltpu.VMEM(w_up.shape, bf16),
        pltpu.VMEM(w_down.shape, bf16),
        pltpu.VMEM((4, length // 4, width), bf16),
        pltpu.VMEM((width, width), bf16),
        pltpu.VMEM((length, width), f32),
        pltpu.VMEM((length, 128), f32),
        pltpu.SemaphoreType.DMA((3 * PIECES + 4,)),
    ]
    args = (core, mixed, w_up, b_up, w_down, row, gain_a, shift_a, b_down, gain, shift, *cots, ids, pool_cot, bo, wo)
    return in_vmem(
        feed_kernel, "feed_both", 37, outs, args, 18e9 * LATE, scratch, 1, far_in=(2, 4, 11, 12, 13, 14, 18)
    )


def attend_back_kernel(
    core, expo, total, q, k, v, mix_t, grad_mixed, keep_out, send_out, sums_out,
    held, q_s, k_s, v_s, mix_s, grad_s, sems,
    *, flush,
):
    length = expo.shape[1]
    pairs = q.shape[1] // 128
    per = pairs // 2
    slots = held.shape[0]

    def copies(at):
        which = core[0] if at >= per else 1 - core[0]
        pair = which * per + at % per
        lanes = pl.ds(pl.multiple_of(pair * 128, 128), 128)
        slot = at % slots
        sources = [
            (q.at[:, lanes], q_s), (k.at[:, lanes], k_s), (v.at[:, lanes], v_s),
            (mix_t.at[lanes, :], mix_s), (grad_mixed.at[:, lanes], grad_s),
            (expo.at[pl.ds(2 * pair, 2)], held),
        ]
        return [
            pltpu.make_async_copy(source, to.at[slot], sems.at[slot, number])
            for number, (source, to) in enumerate(sources)
        ]

    def start(group):
        for at in group:
            for copy in copies(at):
                copy.start()

    groups = [range(0, 1), range(1, per), range(per, pairs)]
    start(groups[0])
    start(groups[1])
    for at in range(pairs):
        for number, group in enumerate(groups):
            if at == group[0]:
                for member in group:
                    for copy in copies(member):
                        copy.wait()
                if number == 0:
                    start(groups[2])
        which = core[0] if at >= per else 1 - core[0]
        out = keep_out if at >= per else send_out
        pair, slot = at % per, at % slots
        lanes = pl.ds(pl.multiple_of(which * (per * 128) + pair * 128, 128), 128)
        grad_t = grad_s[slot].T.astype(f32)
        query, value, mix = q_s[slot], v_s[slot], mix_s[slot]
        key_t = k_s[slot].T
        halves = []
        inner = []
        for half in range(2):
            rows = slice(half * 64, half * 64 + 64)
            inverse = total[pl.ds(which * pairs + 2 * pair + half, 1), :]
            scaled = (grad_t[rows] * inverse).astype(bf16)
            halves.append(scaled)
            inner.append(jnp.sum(scaled.astype(f32) * mix[rows], axis=0, keepdims=True))
        scaled_rows = jnp.concatenate(halves, axis=0).T
        grads_q, grads_k, grads_v = [], [], []
        for half in range(2):
            rows = slice(half * 64, half * 64 + 64)
            probs = held[slot, half]
            grad_probs = dot(value[:, rows], halves[half])
            grad_scores = (probs.astype(f32) * (grad_probs - inner[half])).astype(bf16)
            grads_v.append(dot(probs, scaled_rows[:, rows]))
            grads_k.append(dot(grad_scores, query[:, rows]))
            grads_q.append(dot(key_t[rows, :], grad_scores))
        here = slice(pair * 128, pair * 128 + 128)
        grad_query = (jnp.concatenate(grads_q, axis=0).T * 0.125).astype(bf16)
        grad_value = jnp.concatenate(grads_v, axis=1).astype(bf16)
        out[0, :, here] = grad_query
        out[1, :, here] = jnp.concatenate(grads_k, axis=1).astype(bf16)
        out[2, :, here] = grad_value
        sums_out[:, lanes] = jnp.concatenate(
            [
                jnp.sum(grad_query.astype(f32), axis=0, keepdims=True),
                jnp.sum(grad_value.astype(f32), axis=0, keepdims=True),
                jnp.zeros((6, 128), f32),
            ],
            axis=0,
        )


def attend_back(core, expo, total, q, k, v, mix_t, grad_mixed):
    length, width = q.shape
    outs = [shape((3, length, width // 2)), shape((3, length, width // 2)), shape((8, width), f32)]
    args = (core, expo, total, q, k, v, mix_t, grad_mixed)
    slots = width // 128
    scratch = [
        pltpu.VMEM((slots, 2, length, length), bf16),
        *[pltpu.VMEM((slots, length, 128), bf16)] * 3,
        pltpu.VMEM((slots, 128, length), f32),
        pltpu.VMEM((slots, length, 128), bf16),
        pltpu.SemaphoreType.DMA((slots, 6)),
    ]
    return in_vmem(
        attend_back_kernel, "attend_backward", 20, outs, args, 9e9 * LATE, scratch, 1,
        fetch={2: (0, 1)}, far_in=(1, 3, 4, 5, 6, 7), free=(0, 1, 2),
    )


def add_input_grad(core, hidden, keep, send, wq, wk, wv, o0, o1, o2):
    width = hidden.shape[1]
    half = width // 2
    part = o0.shape[0]
    mine = pl.ds(pl.multiple_of(core[0] * half, 128), half)
    other = pl.ds(pl.multiple_of((1 - core[0]) * half, 128), half)
    total = hidden[...]
    for at, weight in enumerate((wq, wk, wv)):
        total += dot(keep[at], weight[:, mine], 1, 1) + dot(send[at], weight[:, other], 1, 1)
    total = total.astype(bf16)
    for at, out in enumerate((o0, o1, o2.at[0], o2.at[1])):
        out[...] = total[at * part : (at + 1) * part]


def down_weight_kernel(own, other, keep, out, *, flush):
    size = out.shape[0] // 4
    for at in range(4):
        rows = slice(at * size, (at + 1) * size)
        left, right = own[:, rows], other[:, rows]
        out[rows, :] = (dot(left, keep[...], 0, 0) + dot(right, other[:, 4 * size :], 0, 0)).astype(bf16)


def down_weight(own, other, keep):
    half = keep.shape[1]
    outs = [shape((own.shape[1] - half, half))]
    return in_vmem(down_weight_kernel, "down_weight", 14, outs, (own, other, keep), 4e9 * LATE, free=(0,))[0]


def weights_kernel(
    core, low, low_other, mixed, mixed_other, row, row_other, keep_u, got_u, keep_h, send_h, got_h, hidden, wq, wk, wv,
    b_up, sums_head, sums_one, sums_two,
    out_u, out_o, out_h, vec, g0, g1, g2,
    *, flush,
):
    half = out_o.shape[1]
    tiles = out_u.shape[0]
    for at in range(tiles):
        cols = slice(at * half, (at + 1) * half)
        out_u[at] = (dot(low[...], keep_u[:, cols], 0, 0) + dot(low_other[...], got_u[:, cols], 0, 0)).astype(bf16)
    cols = slice(tiles * half, (tiles + 1) * half)
    out_o[...] = (dot(mixed[...], keep_u[:, cols], 0, 0) + dot(mixed_other[...], got_u[:, cols], 0, 0)).astype(bf16)
    for at in range(3):
        out_h[at] = (dot(row[...], keep_h[at], 0, 0) + dot(row_other[...], got_h[at], 0, 0)).astype(bf16)
    add_input_grad(core, hidden, keep_h, send_h, wq, wk, wv, g0, g1, g2)
    shards = vec.shape[0]
    lines = jnp.concatenate([sums_head[0:2], sums_one[0:3], sums_two[0:3]], axis=0)
    line = lines.shape[1] // shards
    up = b_up.shape[1] // shards
    first = lax.broadcasted_iota(jnp.int32, (8, up), 0) == 0
    for at in range(shards):
        piece = lines[:, at * line : (at + 1) * line]
        if line < half:
            piece = jnp.concatenate([piece, jnp.zeros((8, half - line), f32)], axis=1)
        vec[at, 0] = jnp.concatenate([piece, jnp.zeros((8, half), f32)], axis=0).astype(bf16)
        piece = jnp.where(first, b_up[:, at * up : (at + 1) * up], 0.0)
        if up < half:
            piece = jnp.concatenate([piece, jnp.zeros((8, half - up), f32)], axis=1)
        vec[at, 1] = jnp.concatenate([piece, jnp.zeros((8, half), f32)], axis=0).astype(bf16)


def weights(shards, *args):
    low, keep_u = args[1], args[7]
    length, width = low.shape
    half = width // 2
    part = length // 4
    outs = [
        shape((keep_u.shape[1] // half - 1, width, half)), shape((width, half)), shape((3, width, half)),
        shape((shards, 2, 16, half)), shape((part, width)), shape((part, width)), shape((2, part, width)),
    ]
    every = range(len(outs))
    return in_vmem(weights_kernel, "other_weights", 14, outs, args, 11e9 * LATE, scalars=1, free=every)


def pack_kernel(seq_at, tokens, *rest, flush):
    ids, outs, sems = (rest[0], rest[1:5], rest[5]) if len(rest) == 6 else (None, rest[:4], rest[4])
    part, width = tokens.shape[1:]
    copies = []
    for at in (2, 3, 1, 0):
        copies.append(pltpu.make_async_copy(tokens.at[seq_at[0] ^ at], outs[at].at[:part, :], sems.at[at]))
        copies[-1].start()
    if ids is not None:
        for at, out in enumerate(outs):
            line = ids[pl.ds(seq_at[0] ^ at, 1), :].astype(f32)
            line = jnp.concatenate([line, jnp.zeros((1, width - part), f32)], axis=1)
            out[part : part + 16, :] = jnp.broadcast_to(line, (16, width)).astype(bf16)
    for copy in copies:
        copy.wait()


def pack(seq_at, tokens, ids=None):
    _, part, width = tokens.shape
    extra = 0 if ids is None else 16
    args = (seq_at, tokens) if ids is None else (seq_at, tokens, ids)
    outs = [shape((part + extra, width))] * 4
    fetch = {} if ids is None else {2: (0, 1)}
    scratch = [pltpu.SemaphoreType.DMA((4,))]
    return in_vmem(
        pack_kernel, "pack_rows", 6, outs, args, 1e8, scratch, 1, fetch=fetch, far_in=(1,), near=(0, 1, 2, 3)
    )


def place_kernel(seq_at, b0, b1, b2, b3, out, *pooled, flush):
    part, width = out.shape[1:]
    for at, block in enumerate((b0, b1, b2, b3)):
        to = seq_at[0] ^ at
        rows = block.piece()[0] if at == 2 else block[...]
        out[to] = rows[:part, :]
        if pooled:
            first = 0
            rows = rows[part : part + 32, :].astype(f32)
            for window, (row, lane) in zip(pool_windows(width), pool_places(width)):
                pooled[0][to, :, first : first + window] = rows[row : row + 8, lane : lane + window]
                first += window


def place(seq_at, blocks, part, pooled):
    width = blocks[0].shape[1]
    outs = [shape((4, part, width))]
    if pooled:
        outs.append(shape((4, SEGS, sum(pool_windows(width))), f32))
    fetch = {at: (0, 1) for at in range(1, 5)}
    return in_vmem(place_kernel, "place_rows", 6, outs, (seq_at, *blocks), 1e8, scalars=1, fetch=fetch)


def swap_seq(value, mask):
    return lax.ppermute(value, "seq", [(at, at ^ mask) for at in range(4)])


def exchange(own, core_block, chip_blocks):
    got_core = swap_seq(core_block, 1)
    got_chip = swap_seq(chip_blocks, 2)
    return [own, got_core, got_chip]


def forward(blocks):
    return [*blocks, swap_seq(blocks[2][1], 1)]


class Part:
    def __init__(self, blocks, names, first, rows):
        self.blocks, self.names, self.first, self.rows, self.got = blocks, names, first, rows, None


class Exchanges:
    def __init__(self, row_at, seq_at, row_count):
        self.row_count = row_count
        self.axes = ["x"] + [1 << at for at in range(row_count.bit_length() - 1)]
        self.bits = jnp.stack([(seq_at >> 1) & 1] + [(row_at // axis) & 1 for axis in self.axes[1:]])

    def part(self, blocks, first=0, rows=None):
        names = [("tile", blocks.shape[0])] + [(axis, 2) for axis in reversed(self.axes[1:])] + [("x", 2)]
        rows = blocks.shape[3] if rows is None else rows
        return Part(blocks.reshape(-1, *blocks.shape[3:]), names, first, rows)

    def swap(self, value, axis):
        if axis == "x":
            return swap_seq(value, 2)
        return lax.ppermute(value, "rows", [(at, at ^ axis) for at in range(self.row_count)])

    def tick(self, moves, settle=(), far=False):
        parts = [part for part, _ in moves] + list(settle)
        ins = []
        for part in parts:
            for value in (part.blocks, part.got and part.got[0]):
                if value is not None and not any(value is other for other in ins):
                    ins.append(value)
        find = lambda value: [value is other for other in ins].index(True)
        lanes = parts[0].blocks.shape[2]
        used = list(dict.fromkeys(axis for _, axis in moves))
        outs, plan, rows_of, kept = [], [], dict.fromkeys([*used, None], 0), []
        for part, axis in [*moves, *[(part, None) for part in settle]]:
            count = part.blocks.shape[0]
            source = (find(part.blocks), part.first, part.rows, part.got and (find(part.got[0]), part.got[1]))
            if axis is None:
                plan.append((source, axis, [(at, None) for at in range(count)], rows_of[axis], None))
                rows_of[axis] += count * part.rows
                continue
            names = [name for name, _ in part.names]
            low = 1
            for _, size in part.names[names.index(axis) + 1 :]:
                low *= size
            pairs = [(at, at + low) for at in range(count) if (at // low) % 2 == 0]
            plan.append((source, axis, pairs, rows_of[axis], len(kept)))
            kept.append(shape((count // 2, part.rows, lanes)))
            part.got = (axis, rows_of[axis])
            rows_of[axis] += len(pairs) * part.rows
            part.names = [entry for entry in part.names if entry[0] != axis]
        flat = [*used, *([None] if settle else [])]
        outs = [shape((rows_of[axis], lanes)) for axis in flat] + kept

        def kernel(bits, *refs, flush):
            given, sends, keeps = refs[: len(ins)], refs[len(ins) : len(ins) + len(flat)], refs[len(ins) + len(flat) :]
            for (blocks, first, rows, got), axis, pairs, row, keep in plan:
                send = sends[flat.index(axis)]

                def value(at):
                    block = given[blocks][at, first : first + rows, :]
                    if got is None:
                        return block
                    other = given[got[0]][got[1] + at * rows : got[1] + (at + 1) * rows, :]
                    return (block.astype(f32) + other.astype(f32)).astype(bf16)

                for number, (zero, one) in enumerate(pairs):
                    where = slice(row + number * rows, row + (number + 1) * rows)
                    if axis is None:
                        send[where, :] = value(zero)
                        continue
                    bit = bits[self.axes.index(axis)] == 0
                    left, right = value(zero), value(one)
                    send[where, :] = jnp.where(bit, right, left)
                    keeps[keep][number] = jnp.where(bit, left, right)

        every = range(len(flat) if far else 0, len(outs))
        results = in_vmem(kernel, "halves", 10, outs, (self.bits, *ins), 1e8, scalars=1, free=every)
        arrived = {axis: self.swap(results[flat.index(axis)], axis) for axis in used}
        for (part, axis), blocks in zip(moves, results[len(flat) :]):
            part.blocks, part.first = blocks, 0
            part.got = (arrived[axis], part.got[1])
        return results[len(used)] if settle else None

    def before(self, parts, value):
        blocks = [part.blocks for part in parts]
        value, blocks = lax.optimization_barrier((value, blocks))
        for part, new in zip(parts, blocks):
            part.blocks = new
        return value

    def after(self, parts, value):
        found = []
        for part in parts:
            if not any(part.got[0] is other for other in found):
                found.append(part.got[0])
        value, new = lax.optimization_barrier((value, found))
        for part in parts:
            at = [part.got[0] is other for other in found].index(True)
            part.got = (new[at], part.got[1])
        return value


def sides(bits, piece, got_x, got_c, got_xc):
    mine = [jnp.where(bits[0] == 0, piece, got_x), jnp.where(bits[0] == 0, got_x, piece)]
    other = [jnp.where(bits[0] == 0, got_c, got_xc), jnp.where(bits[0] == 0, got_xc, got_c)]
    left = [jnp.where(bits[1] == 0, a, b) for a, b in zip(mine, other)]
    right = [jnp.where(bits[1] == 0, b, a) for a, b in zip(mine, other)]
    return left, right


def final_kernel(kinds, bits, *refs, flush):
    own, outs = refs[:4], refs[4:]
    half = own[0].shape[1]
    for number, (pieces, out) in enumerate(zip(kinds, outs)):
        for at, rows, to_row, to_lane in pieces:
            left, right = sides(bits, *[ref[at : at + rows, :].astype(f32) for ref in own])
            if to_lane is None:
                for x in range(2):
                    out[x, :, :] = left[x] + right[x]
                continue
            for x in range(2):
                first = x * (out.shape[0] // 2) + to_row
                out[first : first + rows, to_lane : to_lane + half] = left[x]
                right_lane = out.shape[1] // 2 + to_lane
                out[first : first + rows, right_lane : right_lane + half] = right[x]
        if len(out.shape) == 2:
            flush(number)


def gather(piece, meanwhile=None):
    got_x = swap_seq(piece, 2)
    if meanwhile is not None:
        got_x, meanwhile = lax.optimization_barrier((got_x, meanwhile))
    return (piece, got_x, swap_seq(piece, 1), swap_seq(got_x, 1)), meanwhile


def final(bits, pieces, kinds, outs, free=()):
    kernel = functools.partial(final_kernel, kinds)
    return in_vmem(kernel, "final_rows", 12, outs, (bits, *pieces), 1e8, scalars=1, free=free)


def together(*values):
    return lax.optimization_barrier(values)


def local(
    row_count,
    tokens, segment_ids, w_query, w_key, w_value, b_query, b_value, w_out, b_out, gain_attn, shift_attn,
    w_up, b_up, w_down, b_down, gain_out, shift_out, token_cot, pool_cot,
):
    part, width = tokens.shape[1:]
    feed_width = w_up.shape[1]
    half = width // 2
    seq_at = lax.axis_index("seq")
    row_at = lax.axis_index("rows")
    core = (seq_at & 1).reshape(1)
    where_at = seq_at.reshape(1)
    ex = Exchanges(row_at, seq_at, row_count)
    last_bits = jnp.stack([(seq_at >> 1) & 1, seq_at & 1])
    y, zs = ex.axes[1], ex.axes[2:]
    z1, z2 = zs[0], zs[1]

    def vec(v):
        return v.reshape(1, -1)

    own = pack(where_at, tokens, segment_ids)
    token_cot, own, near = together(token_cot, own, (w_query, w_key, w_value))
    swapped = {mask: swap_seq(own[mask], mask) for mask in (2, 3, 1)}
    blocks = [own[0]] + [swapped[mask] for mask in (1, 2, 3)]
    near_query, near_key, near_value = load(*near)
    own = pack(where_at, token_cot)
    own, blocks[1], near_query, near_key, near_value = together(own, blocks[1], near_query, near_key, near_value)
    swapped = {mask: swap_seq(own[mask], mask) for mask in (2, 3, 1)}
    cots = [own[0]] + [swapped[mask] for mask in (1, 2, 3)]
    row_pool_cot = lax.dynamic_index_in_dim(pool_cot, seq_at, 0, keepdims=False)

    expo, total, row, q, k, v, mix_t, mixed_near, mixed, row_near, ids_row = attend(
        blocks, near_query, near_key, near_value, vec(b_query), vec(b_value)
    )
    low_far, act, l0, l1, l2, keep_d, sums_two, keep_u, send_u, b_up_sum, hidden_one, grad_mixed, sums_one = feed(
        core, mixed_near, w_up, vec(b_up), w_down, row_near, vec(gain_attn), vec(shift_attn), vec(b_down),
        vec(gain_out), vec(shift_out), cots, ids_row, row_pool_cot, vec(b_out), w_out,
    )
    row_other, mixed_other, low_other = swap_seq(row, 1), swap_seq(mixed, 1), swap_seq(low_far, 1)
    act_other, got_u = swap_seq(act, 1), swap_seq(send_u, 1)
    layer_blocks = exchange(l0, l1, l2)

    def cut(value):
        return value.reshape(-1, row_count, 2, value.shape[-2] // row_count // 2, half)

    row_other, mixed_other, grad_mixed = together(row_other, mixed_other, grad_mixed)
    keep_h, send_h, sums_head = attend_back(core, expo, total, q, k, v, mix_t, grad_mixed)
    act_other, got_u, layer_blocks[1], keep_d, send_h = together(act_other, got_u, layer_blocks[1], keep_d, send_h)
    got_h = swap_seq(send_h, 1)
    grad_w_down = cut(down_weight(act, act_other, keep_d))
    layer_blocks, got_h, low_other, grad_w_down = together(layer_blocks, got_h, low_other, grad_w_down)
    down = grad_w_down.shape[3]
    sizes = [down * at // 12 for at in D_SPLIT]
    d_a, d_b, d_c = (ex.part(grad_w_down, sum(sizes[:at]), sizes[at]) for at in range(3))
    d_parts = [d_a, d_b, d_c]
    ex.tick([(d_c, z1), (d_b, y), (d_a, "x")])
    keep_u = ex.before(d_parts, keep_u)
    grad_w_up, grad_w_out, head, lines, *grads = weights(
        row_count, core, low_far, low_other, mixed, mixed_other, row, row_other, keep_u, got_u, keep_h, send_h, got_h,
        hidden_one, w_query, w_key, w_value, b_up_sum, sums_head, sums_one, sums_two,
    )
    grad_w_up, grad_w_out, head = cut(grad_w_up), cut(grad_w_out), cut(head)
    rows = grad_w_up.shape[3]
    u_a, u_b, u_c, o = ex.part(grad_w_up[:1]), ex.part(grad_w_up[1:2]), ex.part(grad_w_up[2:]), ex.part(grad_w_out)
    u_parts = [u_a, u_b, u_c, o]
    third = rows // 3
    q_part, k_first, k_rest = ex.part(head[0:1]), ex.part(head[1:2], 0, third), ex.part(head[1:2], third, rows - third)
    v_part, line_part = ex.part(head[2:3]), ex.part(lines[None])
    a_parts, b_parts = [q_part, k_first, line_part], [k_rest, v_part]
    head_parts = a_parts + b_parts

    def moves(parts, axis):
        return [(part, axis) for part in parts]

    ex.tick(
        moves([d_b, u_a, *a_parts], "x") + moves([d_a, u_b, *b_parts], y) + moves([u_c, o], z1) + moves([d_c], z2)
    )
    every_part = d_parts + u_parts + head_parts
    layer_blocks = forward(ex.before(head_parts, layer_blocks))
    layer_out, pooled = place(where_at, layer_blocks, part, True)
    layer_out, grads = ex.after(every_part, (layer_out, grads))
    ex.tick(
        moves([u_c], z2) + moves([u_a, *a_parts], y) + moves([d_c, u_b, o, *b_parts], "x") + moves([d_a, d_b], z1)
    )
    grads, grad_core = ex.after(every_part, (grads, swap_seq(grads[1], 1)))
    ex.tick(moves([u_a, u_b, *head_parts], z1) + moves([d_c, u_c, o], y) + moves([d_a, d_b], z2))
    grads = ex.before(head_parts, grads)
    grad_blocks = ex.after(d_parts + u_parts + head_parts, [grads[0], grad_core, swap_seq(grads[2], 2)])
    late = u_parts + head_parts
    if zs[2:]:
        ex.tick(moves([u_a, u_b, o, *head_parts], z2) + moves([u_c], "x"))
        for z in zs[2:]:
            ex.tick(moves(d_parts + late, z))
        down_piece = ex.tick([], d_parts)
    else:
        down_piece = ex.tick(moves([u_a, u_b, o, *head_parts], z2) + moves([u_c], "x"), d_parts)
    d_kinds = (tuple((sum(sizes[:at]), sizes[at], sum(sizes[:at]), 0) for at in range(3) if sizes[at]),)
    grad_tokens = place(where_at, forward(grad_blocks), part, False)[0]
    grad_tokens, down_pieces = ex.after(late, (grad_tokens, gather(down_piece)[0]))
    late_piece = ex.tick([], late)
    down_pieces, late_piece = together(down_pieces, late_piece)
    out_w_down = final(last_bits, down_pieces, d_kinds, [shape((2 * down, width), f32)])[0]
    late_pieces, out_w_down = gather(late_piece, out_w_down)
    wide = [shape((2 * rows, feed_width), f32)] + [shape((2 * rows, width), f32)] * 4 + [shape((2, 16, half), f32)]
    at_q = 5 * rows
    at_k = at_q + rows
    at_lines = at_k + third
    at_rest = at_lines + 16
    kinds = (
        tuple((at * rows, rows, 0, at * half) for at in range(4)),
        ((4 * rows, rows, 0, 0),),
        ((at_q, rows, 0, 0),),
        ((at_k, third, 0, 0), (at_rest, rows - third, third, 0)),
        ((at_rest + rows - third, rows, 0, 0),),
        ((at_lines, 16, 0, None),),
    )
    out_w_up, out_w_out, out_w_query, out_w_key, out_w_value, lines = final(last_bits, late_pieces, kinds, wide, free=(5,))
    rest = lines[0, :8, : width // row_count]
    out_b_up = lines[1, 0, : feed_width // row_count]
    return (
        layer_out, pooled, grad_tokens,
        out_w_query, out_w_key, out_w_value, rest[0], rest[1], out_w_out, rest[4], rest[2], rest[3],
        out_w_up, out_b_up, out_w_down, rest[7], rest[5], rest[6],
    )


def solution(mesh):
    split = P("rows", "seq", None)
    in_specs = (split, P("rows", "seq"), *[P()] * 15, split, P("rows", None, None))
    mat, line = P("rows", None), P("rows")
    out_specs = (
        split, P("rows", None, None), split,
        mat, mat, mat, line, line, mat, line, line, line, mat, line, mat, line, line, line,
    )
    body = functools.partial(local, mesh.shape["rows"])
    return jax.shard_map(body, mesh=mesh, in_specs=in_specs, out_specs=out_specs, check_vma=False)
```
